32 devices in a mesh: rep: 2 (over y), shard: 16 (over z, x, core).
Axes of the slice: x: 2, y: 2, z: 4, core: 2. Of those that a mesh axis runs over, the one named last changes fastest.
Arguments:
- tokens: bfloat16 [12, 2048, 768], P('rep', 'shard'), may hold values from -4 to 4
- query_proj: bfloat16 [768, 768], P('shard')
- key_proj: bfloat16 [768, 768], P('shard')
- value_proj: bfloat16 [768, 768], P('shard')
- pooled_query: bfloat16 [768, 768], P('shard')
- output_proj: bfloat16 [768, 768], P('shard'), may hold values from -1.75 to 1.75
- conv_taps: bfloat16 [5, 2, 768], P(None, None, 'shard'), may hold values from -1.125 to 1.125
- output_bias: bfloat16 [768], P('shard'), may hold values from -2 to 2
- first_gain: bfloat16 [768], P('shard'), may hold values from 0.099609375 to 1.8984375
- first_shift: bfloat16 [768], P('shard'), may hold values from -2 to 2
- inner_proj: bfloat16 [768, 3072], P('shard'), may hold values from -0.21875 to 0.21875
- inner_bias: bfloat16 [3072], P('shard'), may hold values from -3 to 3
- outer_proj: bfloat16 [3072, 768], P('shard'), may hold values from -0.109375 to 0.109375
- outer_bias: bfloat16 [768], P('shard'), may hold values from -2 to 2
- second_gain: bfloat16 [768], P('shard'), may hold values from 0.099609375 to 1.8984375
- second_shift: bfloat16 [768], P('shard'), may hold values from -2 to 2
- block_ids: int32 [12, 2048], P('rep'), may hold values from 0 to 15, never falling along the last dimension, each value on 1 to 256 neighbouring positions
- cotangent: bfloat16 [12, 2048, 768], P('rep', 'shard'), may hold values from -6 to 6
Outputs:
- layer_out: bfloat16 [12, 2048, 768], P('rep', 'shard')
- tokens_grad: float32 [12, 2048, 768], P('rep', 'shard')
- grad_query: float32 [768, 768], P('shard')
- grad_keys: float32 [768, 768], P('shard')
- grad_values: float32 [768, 768], P('shard')
- grad_pooled: float32 [768, 768], P('shard')
- grad_output: float32 [768, 768], P('shard')
- grad_taps: float32 [5, 2, 768], P(None, None, 'shard')
- grad_attnbias: float32 [768], P('shard')
- grad_firstgain: float32 [768], P('shard')
- grad_firstshift: float32 [768], P('shard')
- grad_inner: float32 [768, 3072], P('shard')
- grad_innerbias: float32 [3072], P('shard')
- grad_outer: float32 [3072, 768], P('shard')
- grad_outerbias: float32 [768], P('shard')
- grad_secondgain: float32 [768], P('shard')
- grad_secondshift: float32 [768], P('shard')
The draws below stay inside these ranges and needn't reach their ends.
Inputs may be any that keep to these rules, and one draw needn't show every extreme that they name: `block_ids`: block numbers never fall along a sequence; each block holds 1 to 256 tokens and one holds 256.
All inputs are finite; a program needn't handle non-finite values.
Results may differ from the reference program's by a relative error of at most 0.022.
Values may be sent and summed in bfloat16 or wider, within the bound.
No kernel may reach another device: no remote copies, remote signals or barrier semaphores. Data moves between devices by JAX's collectives and lax.ppermute only.
A program may use at most 256 MiB of HBM per device.

```python
import math
import jax
import jax.numpy as jnp
import numpy as np
from jax import lax

D = 768
HEAD_DIM = 64
FF = 3072
WINDOW = 128
POOL_SPAN = 512
STRIDE = 4
KERNEL = 5
BLOCK = 256
LENGTH = 2048
SEQS = 12


def bounded_normal(key, shape, scale, reach):
    return jax.random.truncated_normal(key, -reach, reach, shape, jnp.float32) * scale


def draw_tokens(key, part):
    key = jax.random.fold_in(key, 11)
    return bounded_normal(key, (SEQS, LENGTH, D), 1.0, 4.0).astype(jnp.bfloat16)


def draw_query_proj(key, part):
    key = jax.random.fold_in(key, 12)
    return bounded_normal(key, (D, D), D ** (-0.5), 3.0).astype(jnp.bfloat16)


def draw_key_proj(key, part):
    key = jax.random.fold_in(key, 13)
    return bounded_normal(key, (D, D), D ** (-0.5), 3.0).astype(jnp.bfloat16)


def draw_value_proj(key, part):
    key = jax.random.fold_in(key, 14)
    return bounded_normal(key, (D, D), D ** (-0.5), 3.0).astype(jnp.bfloat16)


def draw_pooled_query(key, part):
    key = jax.random.fold_in(key, 15)
    return bounded_normal(key, (D, D), (D // 64) ** (-0.5), 3.0).astype(jnp.bfloat16)


def draw_conv_taps(key, part):
    key = jax.random.fold_in(key, 16)
    return bounded_normal(key, (KERNEL, 2, D), 0.45, 2.5).astype(jnp.bfloat16)


def block_scale(own_key, extent, shards, low, high):
    gain = 1.0
    for axis_at, blocks in shards:
        steps = jax.random.uniform(jax.random.fold_in(jax.random.fold_in(own_key, 6), axis_at), (blocks,), jnp.float32, low / len(shards), high / len(shards))
        gain = gain * jnp.repeat(jnp.exp(steps), extent[axis_at] // blocks).reshape((-1,) + (1,) * (len(extent) - 1 - axis_at))
    return gain


def split_up(amount, total, most, skew):
    weights = [(1 << 20) // math.isqrt(grade ** skew) + 1 for grade in range(2, amount + 1)]
    rest, given = total - most - (amount - 1), [1] * (amount - 1)
    while rest > 0:
        free = [i for i in range(amount - 1) if given[i] < most]
        mass, left = sum([weights[i] for i in free]), rest
        for i in free:
            extra = min(most - given[i], max(1, left * weights[i] // mass), rest)
            given[i] = given[i] + extra
            rest = rest - extra
    return np.array([most] + given)


def ragged(own_key, count, total, most, slope):
    if count == 2:
        one = jax.random.randint(own_key, (), max(1, total - most), min(most, total - 1) + 1)
        return jnp.stack([one, total - one])
    lengths = jnp.asarray(split_up(count, total, most, slope), jnp.int32)
    pairs = (count - 1) // 2
    giver, taker = lengths[1:1 + 2 * pairs:2], lengths[2:2 + 2 * pairs:2]
    room = jnp.minimum(giver - 1, most - taker)
    moved = jax.random.randint(jax.random.fold_in(own_key, 1), (pairs,), 0, 1 << 20) % (room + 1)
    lengths = lengths.at[1:1 + 2 * pairs:2].set(giver - moved).at[2:2 + 2 * pairs:2].set(taker + moved)
    return lengths[jax.random.permutation(jax.random.fold_in(own_key, 2), count)]


def noise(stream_key, shape, width, limit, split=(), kind=jnp.bfloat16):
    values = jax.random.normal(stream_key, shape, jnp.float32) * width
    if len(split) > 0:
        values = block_scale(stream_key, shape, split, -0.22, 0.18) * values
    return jnp.clip(values, min=-limit, max=limit).astype(kind)


def setup_inputs(seed: int = 0) -> dict:
    streams_of = jax.random.split(jax.random.key(seed), 19)
    tokens = draw_tokens(jax.random.fold_in(streams_of[18], 71), 0)
    query_proj = draw_query_proj(jax.random.fold_in(streams_of[18], 71), 0)
    key_proj = draw_key_proj(jax.random.fold_in(streams_of[18], 71), 0)
    value_proj = draw_value_proj(jax.random.fold_in(streams_of[18], 71), 0)
    pooled_query = draw_pooled_query(jax.random.fold_in(streams_of[18], 71), 0)
    output_proj = noise(streams_of[5], (D, D), (D // 64) ** -0.5, 1.75, ((0, 16),))
    conv_taps = draw_conv_taps(jax.random.fold_in(streams_of[18], 71), 0)
    output_bias = noise(streams_of[7], (D,), 0.3, 2.0, ((0, 16),))
    first_gain = jnp.clip(1.0 + 0.18 * jax.random.normal(streams_of[8], (D,), jnp.float32), 0.099609375, 1.8984375).astype(jnp.bfloat16)
    first_shift = noise(streams_of[9], (D,), 0.3, 2.0, ((0, 16),))
    inner_proj = noise(streams_of[10], (D, FF), D ** -0.5, 0.21875, ((0, 16),))
    inner_bias = noise(streams_of[11], (FF,), 0.5, 3.0, ((0, 16),))
    outer_proj = noise(streams_of[12], (FF, D), FF ** -0.5, 0.109375, ((0, 16),))
    outer_bias = noise(streams_of[13], (D,), 0.3, 2.0, ((0, 16),))
    second_gain = jnp.clip(1.0 + 0.18 * jax.random.normal(streams_of[14], (D,), jnp.float32), 0.099609375, 1.8984375).astype(jnp.bfloat16)
    second_shift = noise(streams_of[15], (D,), 0.3, 2.0, ((0, 16),))
    block_ids = jax.vmap(lambda own: jnp.searchsorted(jnp.cumsum(ragged(own, LENGTH // 128, LENGTH, BLOCK, 2)), jnp.arange(LENGTH), side="right"))(jax.random.split(streams_of[16], SEQS)).reshape((SEQS, LENGTH)).astype(jnp.int32)
    cotangent = noise(streams_of[17], (SEQS, LENGTH, D), 1.0, 6.0, ((0, 2), (1, 16)))
    return dict(tokens=tokens, query_proj=query_proj, key_proj=key_proj, value_proj=value_proj, pooled_query=pooled_query, output_proj=output_proj, conv_taps=conv_taps, output_bias=output_bias, first_gain=first_gain, first_shift=first_shift, inner_proj=inner_proj, inner_bias=inner_bias, outer_proj=outer_proj, outer_bias=outer_bias, second_gain=second_gain, second_shift=second_shift, block_ids=block_ids, cotangent=cotangent)


@jax.custom_vjp
def low(v):
    return lax.optimization_barrier(v.astype(jnp.bfloat16)).astype(jnp.float32)

@jax.custom_vjp
def low_back(v):
    return v

def low_keep(v):
    return (low(v), None)

def low_pass(kept, grad):
    return (grad,)

def back_keep(v):
    return (v, None)

def back_low(kept, grad):
    return (low(grad),)
low.defvjp(low_keep, low_pass)
low_back.defvjp(back_keep, back_low)
precise = lax.Precision.HIGHEST
neg_fill = -1e+30
norm_eps = 1e-05

def rounded(signal):
    return low_back(low(signal))

def product(former, latter):
    return jnp.dot(former, latter, precision=precise, preferred_element_type=jnp.float32)

def layer_norm(signal, norm_gain, norm_shift):
    row_mean = lax.optimization_barrier(jnp.mean(signal, axis=-1, keepdims=True))
    centred = signal - row_mean
    variance = lax.optimization_barrier(jnp.mean(centred * centred, axis=-1, keepdims=True))
    return centred * lax.rsqrt(variance + norm_eps) * norm_gain + norm_shift

def pool_conv(field, taps):
    pool_count = field.shape[0] // STRIDE
    padded = jnp.pad(field, ((KERNEL // 2, KERNEL // 2), (0, 0)))
    running = jnp.zeros((pool_count, field.shape[1]), jnp.float32)
    for offset in range(KERNEL):
        strided = lax.slice(padded, (offset, 0), (offset + STRIDE * (pool_count - 1) + 1, field.shape[1]), (STRIDE, 1))
        running = running + taps[offset] * strided
    return running

def block_attend(queries, key_block, values, allowed, score_scale):
    scores = low_back(jnp.einsum('qhd,khd->hqk', queries, key_block, precision=precise) * score_scale)
    attn_probs = jax.nn.softmax(jnp.where(allowed[None], scores, neg_fill), axis=-1)
    return jnp.einsum('hqk,khd->qhd', low(attn_probs), values, precision=precise)

def window_attend(queries, key_block, values, block_ids, score_scale):
    seq_length = queries.shape[0]
    half_window = WINDOW // 2
    block_rows = 512
    key_pad = jnp.pad(key_block, ((half_window, half_window), (0, 0), (0, 0)))
    value_pad = jnp.pad(values, ((half_window, half_window), (0, 0), (0, 0)))
    ids_pad = jnp.pad(block_ids, (half_window, half_window))

    def one_block(first_row):
        query_rows = lax.dynamic_slice_in_dim(queries, first_row, block_rows, 0)
        key_rows = lax.dynamic_slice_in_dim(key_pad, first_row, block_rows + 2 * half_window, 0)
        value_rows = lax.dynamic_slice_in_dim(value_pad, first_row, block_rows + 2 * half_window, 0)
        query_ids = lax.dynamic_slice_in_dim(block_ids, first_row, block_rows, 0)
        key_ids = lax.dynamic_slice_in_dim(ids_pad, first_row, block_rows + 2 * half_window, 0)
        query_pos = first_row + jnp.arange(block_rows, dtype=jnp.int32)
        key_pos = first_row - half_window + jnp.arange(block_rows + 2 * half_window, dtype=jnp.int32)
        allowed = (key_pos[None, :] >= query_pos[:, None] - half_window) & (key_pos[None, :] < query_pos[:, None] + half_window) & (key_pos[None, :] >= 0) & (key_pos[None, :] < seq_length) & (key_ids[None, :] <= query_ids[:, None])
        return block_attend(query_rows, key_rows, value_rows, allowed, score_scale)
    starts = jnp.arange(seq_length // block_rows, dtype=jnp.int32) * block_rows
    return lax.map(jax.checkpoint(one_block), starts).reshape(queries.shape)

def pooled_attend(queries, pool_keys, pool_values, block_ids, score_scale):
    seq_length = queries.shape[0]
    pool_reach = POOL_SPAN // (2 * STRIDE)
    pool_count = pool_keys.shape[0]
    block_rows = 512
    pool_rows = block_rows // STRIDE + 2 * pool_reach
    key_pad = jnp.pad(pool_keys, ((pool_reach, pool_reach), (0, 0), (0, 0)))
    value_pad = jnp.pad(pool_values, ((pool_reach, pool_reach), (0, 0), (0, 0)))
    ids_pad = jnp.pad(block_ids[::STRIDE], (pool_reach, pool_reach))

    def one_block(first_row):
        first_pool = first_row // STRIDE
        query_rows = lax.dynamic_slice_in_dim(queries, first_row, block_rows, 0)
        key_rows = lax.dynamic_slice_in_dim(key_pad, first_pool, pool_rows, 0)
        value_rows = lax.dynamic_slice_in_dim(value_pad, first_pool, pool_rows, 0)
        query_ids = lax.dynamic_slice_in_dim(block_ids, first_row, block_rows, 0)
        key_ids = lax.dynamic_slice_in_dim(ids_pad, first_pool, pool_rows, 0)
        query_pos = first_row + jnp.arange(block_rows, dtype=jnp.int32)
        centre = query_pos // STRIDE
        pool_pos = first_pool - pool_reach + jnp.arange(pool_rows, dtype=jnp.int32)
        allowed = (pool_pos[None, :] >= centre[:, None] - pool_reach) & (pool_pos[None, :] < centre[:, None] + pool_reach) & (pool_pos[None, :] >= 0) & (pool_pos[None, :] < pool_count) & (key_ids[None, :] <= query_ids[:, None])
        return block_attend(query_rows, key_rows, value_rows, allowed, score_scale)
    starts = jnp.arange(seq_length // block_rows, dtype=jnp.int32) * block_rows
    return lax.map(jax.checkpoint(one_block), starts).reshape(queries.shape)

def layer(tokens, params, block_ids):
    query_proj, key_proj, value_proj, pooled_query, output_proj, conv_taps, output_bias, first_gain, first_shift, inner_proj, inner_bias, outer_proj, outer_bias, second_gain, second_shift = params
    seq_length, model_width = tokens.shape
    head_count = model_width // HEAD_DIM
    score_scale = HEAD_DIM ** (-0.5)
    shaped = (seq_length, head_count, HEAD_DIM)
    queries = rounded(product(tokens, query_proj))
    key_rows = rounded(product(tokens, key_proj))
    value_rows = rounded(product(tokens, value_proj))
    pool_keys = rounded(pool_conv(key_rows, conv_taps[:, 0]))
    pool_values = rounded(pool_conv(value_rows, conv_taps[:, 1]))
    pool_shape = (pool_keys.shape[0], head_count, HEAD_DIM)
    first = rounded(window_attend(queries.reshape(shaped), key_rows.reshape(shaped), value_rows.reshape(shaped), block_ids, score_scale).reshape(seq_length, model_width))
    second_query = rounded(product(first, pooled_query))
    second = rounded(pooled_attend(second_query.reshape(shaped), pool_keys.reshape(pool_shape), pool_values.reshape(pool_shape), block_ids, score_scale).reshape(seq_length, model_width))
    mixed = low(first + second)
    attn_out = low_back(product(mixed, output_proj) + output_bias)
    normed = layer_norm(tokens + attn_out, first_gain, first_shift)
    inner = low_back(product(low(normed), inner_proj) + inner_bias)
    active = rounded(jax.nn.gelu(inner, approximate=False))
    outer = low_back(product(active, outer_proj) + outer_bias)
    return layer_norm(normed + outer, second_gain, second_shift)

def reference(tokens, query_proj, key_proj, value_proj, pooled_query, output_proj, conv_taps, output_bias, first_gain, first_shift, inner_proj, inner_bias, outer_proj, outer_bias, second_gain, second_shift, block_ids, cotangent):
    params = tuple((weight.astype(jnp.float32) for weight in (query_proj, key_proj, value_proj, pooled_query, output_proj, conv_taps, output_bias, first_gain, first_shift, inner_proj, inner_bias, outer_proj, outer_bias, second_gain, second_shift)))

    def one_sequence(totals, inputs):
        seq_tokens, seq_ids, seq_cot = inputs

        def forward(signal, *weights):
            return layer(signal, weights, seq_ids)
        result, pullback = jax.vjp(forward, seq_tokens.astype(jnp.float32), *params)
        gradients = pullback(seq_cot.astype(jnp.float32))
        totals = tuple((carry + update for carry, update in zip(totals, gradients[1:])))
        return (totals, (result.astype(jnp.bfloat16), gradients[0]))
    initial = tuple((jnp.zeros_like(weight) for weight in params))
    totals, (layer_out, tokens_grad) = lax.scan(one_sequence, initial, (tokens, block_ids, cotangent))
    return (layer_out, tokens_grad, totals[0], totals[1], totals[2], totals[3], totals[4], totals[5], totals[6], totals[7], totals[8], totals[9], totals[10], totals[11], totals[12], totals[13], totals[14])
```

```python
import functools

import jax
import jax.numpy as jnp
from jax import lax
from jax.experimental import pallas as pl
from jax.experimental.pallas import tpu as pltpu
from jax.sharding import PartitionSpec as P

HEAD_DIM = 64
WINDOW = 128
POOL_SPAN = 512
STRIDE = 4
KERNEL = 5

neg_fill = -1e30
norm_eps = 1e-05
F32 = jnp.float32
BF16 = jnp.bfloat16
ROOT_HALF = 0.7071067811865476
ROOT_TWO_PI = 0.3989422804014327

HALF = WINDOW // 2
WIDE = 2 * WINDOW
PAIR = 2 * HEAD_DIM
TILE = 256
SLOTS = 16
VMEM_LIMIT = 60 * 1024 * 1024


def product(former, latter):
    return jnp.dot(former, latter, preferred_element_type=F32)


def product_back(former, latter):
    return lax.dot_general(former, latter, (((1,), (1,)), ((), ())), preferred_element_type=F32)


def outer_sum(former, latter):
    return lax.dot_general(former, latter, (((0,), (0,)), ((), ())), preferred_element_type=F32)


def span(index, size):
    return pl.ds(pl.multiple_of(index * size, size), size)


def any_spec():
    return pl.BlockSpec(memory_space=pl.ANY)


def vmem_spec():
    return pl.BlockSpec(memory_space=pltpu.VMEM)


def smem_spec():
    return pl.BlockSpec(memory_space=pltpu.SMEM)


def params(**more):
    return pltpu.CompilerParams(vmem_limit_bytes=VMEM_LIMIT, **more)


def fetch(order, stacks, columns, target, rows, sem):
    copies = []
    slot = 0
    for stack in stacks:
        for part in range(stack.shape[0]):
            copies.append(
                pltpu.make_async_copy(
                    stack.at[part, :, columns], target.at[span(order[slot], rows), :], sem
                )
            )
            slot += 1
    for copy in copies:
        copy.start()
    return copies


def settle(copies):
    for copy in copies:
        copy.wait()


def tap_matrix(pools):
    rows = lax.broadcasted_iota(jnp.int32, (KERNEL * pools, WIDE), 0)
    cols = lax.broadcasted_iota(jnp.int32, (KERNEL * pools, WIDE), 1)
    tap = rows // pools
    wanted = HALF - KERNEL // 2 + STRIDE * (rows - tap * pools) + tap
    return jnp.where(cols == wanted, 1.0, 0.0).astype(BF16)


def tap_matrix_back(pools):
    rows = lax.broadcasted_iota(jnp.int32, (WIDE, KERNEL * pools), 0)
    cols = lax.broadcasted_iota(jnp.int32, (WIDE, KERNEL * pools), 1)
    tap = cols // pools
    wanted = HALF - KERNEL // 2 + STRIDE * (cols - tap * pools) + tap
    return jnp.where(rows == wanted, 1.0, 0.0).astype(BF16)


def project_kernel(nbuf, order, tok, low, high, taps, *refs):
    stacks = refs[:nbuf]
    xext, queries, pairs, pooled, weights, sem = refs[nbuf:]
    width = tok.shape[1]
    copies = fetch(order, stacks, pl.ds(0, 3 * width), weights, stacks[0].shape[1], sem)
    seqs = low.shape[0] // HALF
    for s in range(seqs):
        xext[s * WIDE : s * WIDE + HALF, :] = low[s * HALF : (s + 1) * HALF, :]
        xext[s * WIDE + HALF : s * WIDE + HALF + WINDOW, :] = tok[s * WINDOW : (s + 1) * WINDOW, :]
        xext[s * WIDE + HALF + WINDOW : (s + 1) * WIDE, :] = high[s * HALF : (s + 1) * HALF, :]
    settle(copies)

    @pl.loop(0, 2 * width // TILE)
    def _(n):
        cols = span(n + width // TILE, TILE)
        pairs[:, span(n, TILE)] = product(xext[...], weights[:, cols]).astype(BF16)

    pools = WINDOW // STRIDE
    matrix = tap_matrix(pools)

    @pl.loop(0, seqs)
    def _(s):
        for n in range(2 * width // TILE):
            cols = slice(n * TILE, (n + 1) * TILE)
            slab = product(matrix, pairs[span(s, WIDE), cols])
            total = taps[0:1, cols] * slab[:pools]
            for t in range(1, KERNEL):
                total = total + taps[t : t + 1, cols] * slab[t * pools : (t + 1) * pools]
            pooled[span(s, pools), cols] = total.astype(BF16)

    @pl.loop(0, width // TILE)
    def _(n):
        cols = span(n, TILE)
        queries[:, cols] = product(tok[...], weights[:, cols]).astype(BF16) * HEAD_DIM**-0.5


def lane_masks():
    lane = lax.broadcasted_iota(jnp.int32, (WINDOW, PAIR), 1)
    first = lane < HEAD_DIM
    return first, jnp.where(first, 1.0, 0.0).astype(BF16), jnp.where(first, 0.0, 1.0).astype(BF16)


def side_masks(step):
    row = lax.broadcasted_iota(jnp.int32, (2 * WINDOW, WINDOW), 0)
    lane = lax.broadcasted_iota(jnp.int32, (2 * WINDOW, WINDOW), 1)
    near = lane >= lax.bitwise_and(row, WINDOW - 1) // step
    return near, jnp.where(near, 1.0, 0.0).astype(BF16), jnp.where(near, 0.0, 1.0).astype(BF16)


def stack_heads(block, lanes):
    return jnp.concatenate([block * lanes[1], block * lanes[2]], axis=0)


def merge_heads(block, lanes):
    return jnp.where(lanes[0], block[:WINDOW], block[WINDOW:])


def spread_sides(block, sides):
    return jnp.concatenate([block * sides[1], block * sides[2]], axis=1)


def attend(queries, keys, values, bias, lanes, sides):
    scores = product_back(stack_heads(queries, lanes), keys)
    scores = jnp.where(sides[0], scores[:, :WINDOW], scores[:, WINDOW:]) + bias
    weights = jnp.exp(scores - jnp.max(scores, axis=-1, keepdims=True))
    probs = (weights * (1.0 / jnp.sum(weights, axis=-1, keepdims=True))).astype(BF16)
    mixed = product(spread_sides(probs, sides), values)
    return probs, merge_heads(mixed, lanes)


def attend_back(queries, keys, values, probs, grad_out, lanes, sides):
    grad_stack = stack_heads(grad_out, lanes)
    grad_probs = product_back(grad_stack, values)
    grad_probs = jnp.where(sides[0], grad_probs[:, :WINDOW], grad_probs[:, WINDOW:])
    probs_full = probs.astype(F32)
    centre = jnp.sum(probs_full * grad_probs, axis=-1, keepdims=True)
    grad_scores = spread_sides((probs_full * (grad_probs - centre)).astype(BF16), sides)
    grad_values = outer_sum(spread_sides(probs, sides), grad_stack)
    grad_keys = outer_sum(grad_scores, stack_heads(queries, lanes))
    grad_queries = merge_heads(product(grad_scores, keys), lanes) * HEAD_DIM**-0.5
    return grad_queries, grad_keys, grad_values


def window_kernel(queries, pairs, bias, attended, probs):
    width = queries.shape[1]
    lanes = lane_masks()
    sides = side_masks(1)
    both = jnp.concatenate([bias[0], bias[0]], axis=0)
    for n in range(width // PAIR):
        cols = slice(n * PAIR, (n + 1) * PAIR)
        held, out = attend(
            queries[:, cols],
            pairs[:, cols],
            pairs[:, width + n * PAIR : width + (n + 1) * PAIR],
            both,
            lanes,
            sides,
        )
        probs[0, n] = held
        attended[:, cols] = out.astype(BF16)


def lay_pooled(places, blocks, field):
    pools = blocks[0].shape[0]
    for k, block in enumerate(blocks):
        field[span(places[k], pools), :] = block[...]


def pooled_kernel(nbuf, order, places, attended, bias, *refs):
    blocks = refs[:5]
    stacks = refs[5 : 5 + nbuf]
    queries, mixed, probs, field, weights, sem = refs[5 + nbuf :]
    width = attended.shape[1]
    s = pl.program_id(0)

    @pl.when(s == 0)
    def _():
        copies = fetch(order, stacks, pl.ds(0, width), weights, stacks[0].shape[1], sem)
        field[...] = jnp.zeros_like(field)
        settle(copies)

        @pl.loop(0, width // TILE)
        def _(n):
            cols = span(n, TILE)
            queries[:, cols] = product(attended[...], weights[:, cols]).astype(BF16) * HEAD_DIM**-0.5

    lay_pooled(places, blocks, field)
    lanes = lane_masks()
    sides = side_masks(STRIDE)
    both = jnp.concatenate([bias[0], bias[0]], axis=0)
    rows = span(s, WINDOW)
    for n in range(width // PAIR):
        cols = slice(n * PAIR, (n + 1) * PAIR)
        held, out = attend(
            queries[rows, cols],
            field[:, cols],
            field[:, width + n * PAIR : width + (n + 1) * PAIR],
            both,
            lanes,
            sides,
        )
        probs[0, n] = held
        first = attended[rows, cols].astype(F32)
        mixed[:, cols] = (first + out.astype(BF16).astype(F32)).astype(BF16)


def feed_kernel(counts, order, tok, mixed, cot, vecs, bias_in, *refs):
    at = sum(counts)
    out_stacks = refs[: counts[0]]
    in_stacks = refs[counts[0] : counts[0] + counts[1]]
    down_stacks = refs[counts[0] + counts[1] : at]
    (
        result,
        grad_resid,
        grad_attn,
        grad_in,
        grad_down,
        vec_grads,
        bias_grad,
        w_out,
        w_in,
        w_down,
        centred,
        rstd,
        normed,
        normed_t,
        active,
        slope,
        field,
        grad_outer,
        sems,
    ) = refs[at:]
    rows, width = tok.shape
    hidden = w_in.shape[1]
    first = fetch(order, out_stacks, pl.ds(width, width), w_out, out_stacks[0].shape[1], sems.at[0])
    second = fetch(order, in_stacks, pl.ds(0, hidden), w_in, in_stacks[0].shape[1], sems.at[1])
    third = fetch(order, down_stacks, pl.ds(0, width), w_down, down_stacks[0].shape[1], sems.at[2])
    settle(first)

    @pl.loop(0, width // TILE)
    def _(n):
        cols = span(n, TILE)
        field[:, cols] = tok[:, cols].astype(F32) + product(mixed[...], w_out[:, cols]) + vecs[0:1, cols]

    blocks = rows // WINDOW

    @pl.loop(0, blocks)
    def _(b):
        part = span(b, WINDOW)
        resid = field[part, :]
        middle = resid - jnp.mean(resid, axis=-1, keepdims=True)
        scale = lax.rsqrt(jnp.mean(middle * middle, axis=-1, keepdims=True) + norm_eps)
        unit = middle * scale
        centred[part, :] = unit
        rstd[part, :] = jnp.broadcast_to(scale, (WINDOW, 128))
        low = (unit * vecs[1:2, :] + vecs[2:3, :]).astype(BF16)
        normed[part, :] = low
        normed_t[:, part] = low.T

    settle(second)

    @pl.loop(0, hidden // TILE)
    def _(n):
        cols = span(n, TILE)
        inner = product(normed[...], w_in[:, cols]) + bias_in[0:1, cols]
        cdf = 0.5 + 0.5 * lax.erf(inner * ROOT_HALF)
        active[:, cols] = (inner * cdf).astype(BF16)
        slope[:, cols] = (cdf + inner * (jnp.exp(-0.5 * inner * inner) * ROOT_TWO_PI)).astype(BF16)

    settle(third)

    @pl.loop(0, width // TILE)
    def _(n):
        cols = span(n, TILE)
        unit = centred[:, cols] * vecs[1:2, cols] + vecs[2:3, cols]
        field[:, cols] = unit + product(active[...], w_down[:, cols]) + vecs[3:4, cols]

    vec_grads[...] = jnp.zeros_like(vec_grads)

    def add_row(k, value):
        vec_grads[k : k + 1, :] += jnp.sum(value, axis=0, keepdims=True)

    @pl.loop(0, blocks)
    def _(b):
        part = span(b, WINDOW)
        summed = field[part, :]
        middle = summed - jnp.mean(summed, axis=-1, keepdims=True)
        scale = lax.rsqrt(jnp.mean(middle * middle, axis=-1, keepdims=True) + norm_eps)
        unit = middle * scale
        result[part, :] = (unit * vecs[4:5, :] + vecs[5:6, :]).astype(BF16)
        grad = cot[part, :].astype(F32)
        add_row(4, grad * unit)
        add_row(5, grad)
        u = grad * vecs[4:5, :]
        lean = jnp.mean(u * unit, axis=-1, keepdims=True)
        grad = scale * (u - jnp.mean(u, axis=-1, keepdims=True) - unit * lean)
        field[part, :] = grad
        low = grad.astype(BF16)
        grad_outer[part, :] = low
        add_row(3, low.astype(F32))

    @pl.loop(0, hidden // TILE)
    def _(n):
        cols = span(n, TILE)
        grad = product_back(grad_outer[...], w_down[cols, :]).astype(BF16).astype(F32)
        low = (grad * slope[:, cols].astype(F32)).astype(BF16)
        slope[:, cols] = low
        bias_grad[:, cols] = jnp.sum(low.astype(F32), axis=0, keepdims=True)
        grad_down[cols, :] = outer_sum(active[:, cols], grad_outer[...]).astype(BF16)
        grad_in[:, cols] = product(normed_t[...], low).astype(BF16)

    @pl.loop(0, width // TILE)
    def _(n):
        cols = span(n, TILE)
        field[:, cols] += product_back(slope[...], w_in[cols, :])

    @pl.loop(0, blocks)
    def _(b):
        part = span(b, WINDOW)
        grad = field[part, :]
        unit = centred[part, :]
        add_row(1, grad * unit)
        add_row(2, grad)
        u = grad * vecs[1:2, :]
        lean = jnp.mean(u * unit, axis=-1, keepdims=True)
        grad = rstd[part, 0:1] * (u - jnp.mean(u, axis=-1, keepdims=True) - unit * lean)
        grad_resid[part, :] = grad
        low = grad.astype(BF16)
        grad_attn[part, :] = low
        add_row(0, low.astype(F32))


def pooled_back_kernel(nbuf, order, places, grad_attn, mixed, queries, probs, *refs):
    blocks = refs[:5]
    stacks = refs[5 : 5 + nbuf]
    grad_mixed, grad_queries, grad_out, grad_own, grad_away, grad_near, grad_far = refs[5 + nbuf : 12 + nbuf]
    field, total, grad_low, weights, sem = refs[12 + nbuf :]
    width = grad_attn.shape[1]
    pools = blocks[0].shape[0]
    s = pl.program_id(0)

    @pl.when(s == 0)
    def _():
        copies = fetch(order, stacks, pl.ds(width, width), weights, stacks[0].shape[1], sem)
        field[...] = jnp.zeros_like(field)
        settle(copies)

        @pl.loop(0, width // TILE)
        def _(n):
            cols = span(n, TILE)
            grad = product_back(grad_attn[...], weights[cols, :])
            grad_mixed[:, cols] = grad
            grad_low[:, cols] = grad.astype(BF16)
            grad_out[cols, :] = outer_sum(mixed[:, cols], grad_attn[...]).astype(BF16)

    lay_pooled(places, blocks, field)
    lanes = lane_masks()
    sides = side_masks(STRIDE)
    rows = span(s, WINDOW)
    for n in range(width // PAIR):
        cols = slice(n * PAIR, (n + 1) * PAIR)
        others = slice(width + n * PAIR, width + (n + 1) * PAIR)
        grad_q, grad_k, grad_v = attend_back(
            queries[:, cols], field[:, cols], field[:, others], probs[0, n], grad_low[rows, cols], lanes, sides
        )
        grad_queries[:, cols] = grad_q.astype(BF16)
        total[:, cols] = grad_k
        total[:, others] = grad_v
    for k, target in enumerate((grad_own, grad_away.at[0], grad_away.at[1], grad_near, grad_far)):
        target[...] = total[span(places[k], pools), :].astype(BF16)


def window_back_kernel(nbuf, order, grad_mixed, grad_second, first, queries, pairs, probs, *refs):
    stacks = refs[:nbuf]
    grad_queries, grad_pairs, grad_pooled, grad_low, weights, sem = refs[nbuf:]
    width = first.shape[1]
    s = pl.program_id(0)

    @pl.when(s == 0)
    def _():
        settle(fetch(order, stacks, pl.ds(0, width), weights, stacks[0].shape[1], sem))

        @pl.loop(0, width // TILE)
        def _(n):
            cols = span(n, TILE)
            grad = grad_mixed[:, cols] + product_back(grad_second[...], weights[cols, :])
            grad_low[:, cols] = grad.astype(BF16)
            grad_pooled[cols, :] = outer_sum(first[:, cols], grad_second[...]).astype(BF16)

    lanes = lane_masks()
    sides = side_masks(1)
    rows = span(s, WINDOW)
    for n in range(width // PAIR):
        cols = slice(n * PAIR, (n + 1) * PAIR)
        others = slice(width + n * PAIR, width + (n + 1) * PAIR)
        grad_q, grad_k, grad_v = attend_back(
            queries[:, cols], pairs[:, cols], pairs[:, others], probs[0, n], grad_low[rows, cols], lanes, sides
        )
        grad_queries[:, cols] = grad_q.astype(BF16)
        grad_pairs[:, cols] = grad_k.astype(BF16)
        grad_pairs[:, others] = grad_v.astype(BF16)


def conv_back_kernel(nbuf, order, own, away, near, far, taps, pairs, grad_pairs, *refs):
    stacks = refs[:nbuf]
    total, tap_grads, edges, weights, rim, sem = refs[nbuf:]
    width = pairs.shape[1] // 2
    seqs = pairs.shape[0] // WIDE
    pools = WINDOW // STRIDE
    copies = fetch(order, stacks, pl.ds(width, 2 * width), weights, stacks[0].shape[1], sem)
    matrix = tap_matrix(pools)
    back = tap_matrix_back(pools)
    tap_grads[...] = jnp.zeros_like(tap_grads)

    @pl.loop(0, seqs)
    def _(s):
        for n in range(2 * width // TILE):
            cols = slice(n * TILE, (n + 1) * TILE)
            part = span(s, pools)
            grad = own[part, cols].astype(F32) + away[part, cols].astype(F32)
            grad = grad + near[part, cols].astype(F32) + far[part, cols].astype(F32)
            grad = grad.astype(BF16).astype(F32)
            spread = [(taps[t : t + 1, cols] * grad).astype(BF16) for t in range(KERNEL)]
            whole = grad_pairs[span(s, WIDE), cols].astype(F32) + product(back, jnp.concatenate(spread, axis=0))
            total[span(s, WIDE), cols] = whole.astype(BF16)
            slab = product(matrix, pairs[span(s, WIDE), cols])
            for t in range(KERNEL):
                tap_grads[t : t + 1, cols] += jnp.sum(
                    grad * slab[t * pools : (t + 1) * pools], axis=0, keepdims=True
                )

    for s in range(seqs):
        rim[s * HALF : (s + 1) * HALF, :] = total[s * WIDE : s * WIDE + HALF, :]
        rim[(seqs + s) * HALF : (seqs + s + 1) * HALF, :] = total[s * WIDE + HALF + WINDOW : (s + 1) * WIDE, :]
    settle(copies)

    @pl.loop(0, width // TILE)
    def _(n):
        cols = span(n, TILE)
        edges[:, cols] = product_back(rim[...], weights[cols, :]).astype(BF16)


def weight_grad_kernel(tok, xext, grad_queries, grad_pairs, out, tok_t, xext_t):
    width = tok.shape[1]
    tok_t[...] = tok[...].T
    xext_t[...] = xext[...].T

    @pl.loop(0, width // TILE)
    def _(n):
        cols = span(n, TILE)
        out[:, cols] = product(tok_t[...], grad_queries[:, cols]).astype(BF16)

    @pl.loop(0, 2 * width // TILE)
    def _(n):
        out[:, span(n + width // TILE, TILE)] = product(xext_t[...], grad_pairs[:, span(n, TILE)]).astype(BF16)


def token_grad_kernel(nbuf, order, grad_resid, grad_queries, grad_pairs, low, high, *refs):
    stacks = refs[:nbuf]
    out, weights, own, sem = refs[nbuf:]
    width = grad_resid.shape[1]
    seqs = grad_resid.shape[0] // WINDOW
    copies = fetch(order, stacks, pl.ds(0, 3 * width), weights, stacks[0].shape[1], sem)
    for s in range(seqs):
        own[s * WINDOW : (s + 1) * WINDOW, :width] = grad_queries[s * WINDOW : (s + 1) * WINDOW, :]
        own[s * WINDOW : (s + 1) * WINDOW, width:] = grad_pairs[s * WIDE + HALF : s * WIDE + HALF + WINDOW, :]
    settle(copies)

    @pl.loop(0, width // TILE)
    def _(n):
        cols = span(n, TILE)
        out[:, cols] = grad_resid[:, cols] + product_back(own[...], weights[cols, :])
        for s in range(seqs):
            part = slice(s * HALF, (s + 1) * HALF)
            out[s * WINDOW : s * WINDOW + HALF, cols] += low[part, cols].astype(F32)
            out[s * WINDOW + HALF : (s + 1) * WINDOW, cols] += high[part, cols].astype(F32)


def shape_of(*dims, dtype=BF16):
    return jax.ShapeDtypeStruct(dims, dtype)


def gathered(block):
    rows = block.shape[0] * lax.axis_size("shard") // SLOTS
    full = lax.all_gather(block, "shard", axis=0, tiled=True)
    return [full.reshape(SLOTS, rows, block.shape[1])]


def scattered(whole):
    return lax.psum_scatter(whole, "shard", scatter_dimension=0, tiled=True)


def rep_total(piece):
    count = lax.axis_size("rep")
    total = piece.astype(F32)
    for step in range(1, count):
        route = [(i, (i + step) % count) for i in range(count)]
        total = total + lax.ppermute(piece, "rep", route).astype(F32)
    return total


def shift(block, distance):
    count = lax.axis_size("shard")
    return lax.ppermute(
        block, "shard", [(i, i + distance) for i in range(count) if 0 <= i + distance < count]
    )


def swap(block):
    return lax.ppermute(block, "shard", [(i, i ^ 1) for i in range(lax.axis_size("shard"))])


def hop(block, outer):
    count = lax.axis_size("shard")
    route = [(i, i + (2 if (i % 2 == 0) == outer else -2)) for i in range(count)]
    return lax.ppermute(block, "shard", [(i, j) for i, j in route if 0 <= j < count])


def shards(
    tokens,
    query_proj,
    key_proj,
    value_proj,
    pooled_query,
    output_proj,
    conv_taps,
    output_bias,
    first_gain,
    first_shift,
    inner_proj,
    inner_bias,
    outer_proj,
    outer_bias,
    second_gain,
    second_shift,
    block_ids,
    cotangent,
):
    seqs, tok_span, width = tokens.shape
    rows = seqs * tok_span
    hidden = inner_proj.shape[1]
    device_count = lax.axis_size("shard")
    device_index = lax.axis_index("shard")
    seq_length = tok_span * device_count
    pools = tok_span // STRIDE
    pool_reach = POOL_SPAN // (2 * STRIDE)
    n_pair = width // PAIR
    core = lax.rem(device_index, 2)

    tok = tokens.reshape(rows, width)
    cot = cotangent.reshape(rows, width)
    tok_low = shift(tokens[:, tok_span - HALF :], 1).reshape(seqs * HALF, width)
    tok_high = shift(tokens[:, :HALF], -1).reshape(seqs * HALF, width)

    vectors = [output_bias, first_gain, first_shift, outer_bias, second_gain, second_shift]
    part = width // device_count
    small = jnp.concatenate(vectors + [inner_bias, conv_taps.reshape(-1)])
    lanes = 128 * -(-small.shape[0] // (part * 128))
    small = jnp.pad(small, (0, part * lanes - small.shape[0])).reshape(part, lanes)
    lead = gathered(jnp.concatenate([query_proj, key_proj, value_proj, small], axis=1))
    mid = gathered(jnp.concatenate([pooled_query, output_proj], axis=1))
    up = gathered(inner_proj)
    down = gathered(outer_proj)
    order = jnp.arange(SLOTS, dtype=jnp.int32)

    small_full = jnp.concatenate([stack[:, :, 3 * width :] for stack in lead], axis=0)
    small_full = small_full.reshape(device_count, part * lanes).astype(F32)
    vecs = jnp.stack([small_full[:, k * part : (k + 1) * part].reshape(width) for k in range(6)])
    vecs = jnp.pad(vecs, ((0, 2), (0, 0)))
    at = 6 * part
    bias_in = small_full[:, at : at + hidden // device_count].reshape(1, hidden)
    at = at + hidden // device_count
    taps = small_full[:, at : at + 2 * KERNEL * part].reshape(device_count, KERNEL, 2, part)
    taps = taps.transpose(1, 2, 0, 3).reshape(KERNEL, 2 * width)
    taps = jnp.pad(taps, ((0, 8 - KERNEL), (0, 0)))

    row = jnp.arange(tok_span, dtype=jnp.int32)[:, None]
    lane = jnp.arange(WINDOW, dtype=jnp.int32)[None, :]
    query_ids = lax.dynamic_slice_in_dim(block_ids, device_index * tok_span, tok_span, 1)[:, :, None]

    def bias_for(ids, start, length, step, reach):
        ids = lax.dynamic_slice_in_dim(jnp.pad(ids, ((0, 0), (reach, reach + WINDOW))), start, WIDE, 1)
        near = lane >= row // step
        place = start - reach + jnp.where(near, lane, lane + WINDOW)
        key_ids = jnp.where(near[None], ids[:, None, :WINDOW], ids[:, None, WINDOW:])
        allowed = ((place >= 0) & (place < length))[None] & (key_ids <= query_ids)
        return jnp.where(allowed, 0.0, neg_fill)

    bias_one = bias_for(block_ids, device_index * tok_span, seq_length, 1, HALF)
    bias_two = bias_for(
        block_ids[:, ::STRIDE], device_index * pools, seq_length // STRIDE, STRIDE, pool_reach
    )

    n_lead = len(lead)
    xext, queries, pairs, pooled = pl.pallas_call(
        functools.partial(project_kernel, n_lead),
        out_shape=(
            shape_of(seqs * WIDE, width),
            shape_of(rows, width),
            shape_of(seqs * WIDE, 2 * width),
            shape_of(seqs * pools, 2 * width),
        ),
        in_specs=[smem_spec()] + [vmem_spec()] * 4 + [any_spec()] * n_lead,
        out_specs=(vmem_spec(),) * 4,
        scratch_shapes=[pltpu.VMEM((width, 3 * width), BF16), pltpu.SemaphoreType.DMA],
        compiler_params=params(),
        name="project",
    )(order, tok, tok_low, tok_high, taps, *lead)

    pool_away = swap(pooled)
    pool_far = hop(pooled, True)
    pool_near = hop(pooled, False)
    pool_cross = swap(pool_near)
    pool_blocks = (pooled, pool_away, pool_cross, pool_near, pool_far)
    places = jnp.where(
        core == 0, jnp.array([2, 3, 1, 4, 0], jnp.int32), jnp.array([2, 1, 3, 0, 4], jnp.int32)
    )

    seq_block = lambda r, c: pl.BlockSpec((r, c), lambda s: (s, 0))
    whole_block = lambda r, c: pl.BlockSpec((r, c), lambda s: (0, 0))
    bias_block = pl.BlockSpec((1, tok_span, WINDOW), lambda s: (s, 0, 0))
    prob_block = pl.BlockSpec((1, n_pair, 2 * tok_span, WINDOW), lambda s: (s, 0, 0, 0))
    prob_shape = shape_of(seqs, n_pair, 2 * tok_span, WINDOW)

    attended, probs_one = pl.pallas_call(
        window_kernel,
        grid=(seqs,),
        out_shape=(shape_of(rows, width), prob_shape),
        in_specs=[seq_block(tok_span, width), seq_block(WIDE, 2 * width), bias_block],
        out_specs=(seq_block(tok_span, width), prob_block),
        compiler_params=params(),
        name="window",
    )(queries, pairs, bias_one)

    n_mid = len(mid)
    pool_specs = [seq_block(pools, 2 * width)] * 5
    second, mixed, probs_two = pl.pallas_call(
        functools.partial(pooled_kernel, n_mid),
        grid=(seqs,),
        out_shape=(shape_of(rows, width), shape_of(rows, width), prob_shape),
        in_specs=[smem_spec(), smem_spec(), whole_block(rows, width), bias_block]
        + pool_specs
        + [any_spec()] * n_mid,
        out_specs=(whole_block(rows, width), seq_block(tok_span, width), prob_block),
        scratch_shapes=[
            pltpu.VMEM((WIDE, 2 * width), BF16),
            pltpu.VMEM((width, width), BF16),
            pltpu.SemaphoreType.DMA,
        ],
        compiler_params=params(),
        name="pooled",
    )(order, places, attended, bias_two, *pool_blocks, *mid)

    counts = (len(mid), len(up), len(down))
    result, grad_resid, grad_attn, grad_in, grad_down, vec_grads, bias_grad = pl.pallas_call(
        functools.partial(feed_kernel, counts),
        out_shape=(
            shape_of(rows, width),
            shape_of(rows, width, dtype=F32),
            shape_of(rows, width),
            shape_of(width, hidden),
            shape_of(hidden, width),
            shape_of(8, width, dtype=F32),
            shape_of(1, hidden, dtype=F32),
        ),
        in_specs=[smem_spec()] + [vmem_spec()] * 5 + [any_spec()] * sum(counts),
        out_specs=(vmem_spec(),) * 7,
        scratch_shapes=[
            pltpu.VMEM((width, width), BF16),
            pltpu.VMEM((width, hidden), BF16),
            pltpu.VMEM((hidden, width), BF16),
            pltpu.VMEM((rows, width), F32),
            pltpu.VMEM((rows, 128), F32),
            pltpu.VMEM((rows, width), BF16),
            pltpu.VMEM((width, rows), BF16),
            pltpu.VMEM((rows, hidden), BF16),
            pltpu.VMEM((rows, hidden), BF16),
            pltpu.VMEM((rows, width), F32),
            pltpu.VMEM((rows, width), BF16),
            pltpu.SemaphoreType.DMA((3,)),
        ],
        compiler_params=params(),
        name="feed",
    )(order, tok, mixed, cot, vecs, bias_in, *mid, *up, *down)
    own_down = scattered(grad_down)
    own_in = scattered(grad_in)

    back_shape = shape_of(seqs * pools, 2 * width)
    grad_mixed, grad_second, grad_out, pg_own, pg_away, pg_near, pg_far = pl.pallas_call(
        functools.partial(pooled_back_kernel, n_mid),
        grid=(seqs,),
        out_shape=(
            shape_of(rows, width, dtype=F32),
            shape_of(rows, width),
            shape_of(width, width),
            back_shape,
            shape_of(2, seqs * pools, 2 * width),
            back_shape,
            back_shape,
        ),
        in_specs=[
            smem_spec(),
            smem_spec(),
            whole_block(rows, width),
            whole_block(rows, width),
            seq_block(tok_span, width),
            prob_block,
        ]
        + pool_specs
        + [any_spec()] * n_mid,
        out_specs=(
            whole_block(rows, width),
            seq_block(tok_span, width),
            whole_block(width, width),
            seq_block(pools, 2 * width),
            pl.BlockSpec((2, pools, 2 * width), lambda s: (0, s, 0)),
            seq_block(pools, 2 * width),
            seq_block(pools, 2 * width),
        ),
        scratch_shapes=[
            pltpu.VMEM((WIDE, 2 * width), BF16),
            pltpu.VMEM((WIDE, 2 * width), F32),
            pltpu.VMEM((rows, width), BF16),
            pltpu.VMEM((width, width), BF16),
            pltpu.SemaphoreType.DMA,
        ],
        compiler_params=params(),
        name="pooled_back",
    )(order, places, grad_attn, mixed, second, probs_two, *pool_blocks, *mid)

    pg_cross = swap(pg_away)
    back_far = lax.ppermute(pg_far, "shard", back_route(device_count, True))
    pg_near = (pg_near.astype(F32) + pg_cross[1].astype(F32)).astype(BF16)
    back_near = lax.ppermute(pg_near, "shard", back_route(device_count, False))

    grad_queries, grad_pairs, grad_pooled = pl.pallas_call(
        functools.partial(window_back_kernel, n_mid),
        grid=(seqs,),
        out_shape=(shape_of(rows, width), shape_of(seqs * WIDE, 2 * width), shape_of(width, width)),
        in_specs=[
            smem_spec(),
            whole_block(rows, width),
            whole_block(rows, width),
            whole_block(rows, width),
            seq_block(tok_span, width),
            seq_block(WIDE, 2 * width),
            prob_block,
        ]
        + [any_spec()] * n_mid,
        out_specs=(seq_block(tok_span, width), seq_block(WIDE, 2 * width), whole_block(width, width)),
        scratch_shapes=[
            pltpu.VMEM((rows, width), BF16),
            pltpu.VMEM((width, width), BF16),
            pltpu.SemaphoreType.DMA,
        ],
        compiler_params=params(),
        name="window_back",
    )(order, grad_mixed, grad_second, attended, queries, pairs, probs_one, *mid)

    pair_total, tap_grads, edges = pl.pallas_call(
        functools.partial(conv_back_kernel, n_lead),
        out_shape=(
            shape_of(seqs * WIDE, 2 * width),
            shape_of(8, 2 * width, dtype=F32),
            shape_of(2 * seqs * HALF, width),
        ),
        in_specs=[smem_spec()] + [vmem_spec()] * 7 + [any_spec()] * n_lead,
        out_specs=(vmem_spec(),) * 3,
        scratch_shapes=[
            pltpu.VMEM((width, 2 * width), BF16),
            pltpu.VMEM((2 * seqs * HALF, 2 * width), BF16),
            pltpu.SemaphoreType.DMA,
        ],
        compiler_params=params(),
        name="conv_back",
    )(order, pg_own, pg_cross[0], back_near, back_far, taps, pairs, grad_pairs, *lead)

    edge_high = shift(edges[: seqs * HALF], -1)
    edge_low = shift(edges[seqs * HALF :], 1)

    grad_lead = pl.pallas_call(
        weight_grad_kernel,
        out_shape=shape_of(width, 3 * width),
        in_specs=[vmem_spec()] * 4,
        out_specs=vmem_spec(),
        scratch_shapes=[pltpu.VMEM((width, rows), BF16), pltpu.VMEM((width, seqs * WIDE), BF16)],
        compiler_params=params(),
        name="weight_grad",
    )(tok, xext, grad_queries, pair_total)

    small_grads = jnp.concatenate(
        [vec_grads[k].reshape(device_count, part) for k in range(6)]
        + [
            bias_grad.reshape(device_count, hidden // device_count),
            tap_grads[:KERNEL]
            .reshape(KERNEL, 2, device_count, part)
            .transpose(2, 0, 1, 3)
            .reshape(device_count, 2 * KERNEL * part),
        ],
        axis=1,
    )
    small_grads = jnp.pad(small_grads, ((0, 0), (0, part * lanes - small_grads.shape[1])))
    small_grads = small_grads.reshape(width, lanes).astype(BF16)
    own_mid = scattered(jnp.concatenate([grad_pooled, grad_out], axis=1))
    own_lead = scattered(jnp.concatenate([grad_lead, small_grads], axis=1))

    tokens_grad = pl.pallas_call(
        functools.partial(token_grad_kernel, n_lead),
        out_shape=shape_of(rows, width, dtype=F32),
        in_specs=[smem_spec()] + [vmem_spec()] * 5 + [any_spec()] * n_lead,
        out_specs=vmem_spec(),
        scratch_shapes=[
            pltpu.VMEM((width, 3 * width), BF16),
            pltpu.VMEM((rows, 3 * width), BF16),
            pltpu.SemaphoreType.DMA,
        ],
        compiler_params=params(),
        name="token_grad",
    )(order, grad_resid, grad_queries, pair_total, edge_low, edge_high, *lead)

    own_down = rep_total(own_down)
    own_in = rep_total(own_in)
    own_mid = rep_total(own_mid)
    own_lead = rep_total(own_lead)
    small_own = own_lead[:, 3 * width :].reshape(-1)
    vec_own = [small_own[k * part : (k + 1) * part] for k in range(6)]
    at = 6 * part
    bias_own = small_own[at : at + hidden // device_count]
    at = at + hidden // device_count
    taps_own = small_own[at : at + 2 * KERNEL * part].reshape(KERNEL, 2, part)
    return (
        result.reshape(tokens.shape),
        tokens_grad.reshape(tokens.shape),
        own_lead[:, :width],
        own_lead[:, width : 2 * width],
        own_lead[:, 2 * width : 3 * width],
        own_mid[:, :width],
        own_mid[:, width:],
        taps_own,
        vec_own[0],
        vec_own[1],
        vec_own[2],
        own_in,
        bias_own,
        own_down,
        vec_own[3],
        vec_own[4],
        vec_own[5],
    )


def back_route(count, outer):
    route = [(i, i + (2 if (i % 2 == 0) == outer else -2)) for i in range(count)]
    return [(j, i) for i, j in route if 0 <= j < count]


def solution(mesh):
    in_specs = (
        P("rep", "shard", None),
        P("shard", None),
        P("shard", None),
        P("shard", None),
        P("shard", None),
        P("shard", None),
        P(None, None, "shard"),
        P("shard"),
        P("shard"),
        P("shard"),
        P("shard", None),
        P("shard"),
        P("shard", None),
        P("shard"),
        P("shard"),
        P("shard"),
        P("rep", None),
        P("rep", "shard", None),
    )
    out_specs = (
        P("rep", "shard", None),
        P("rep", "shard", None),
        P("shard", None),
        P("shard", None),
        P("shard", None),
        P("shard", None),
        P("shard", None),
        P(None, None, "shard"),
        P("shard"),
        P("shard"),
        P("shard"),
        P("shard", None),
        P("shard"),
        P("shard", None),
        P("shard"),
        P("shard"),
        P("shard"),
    )
    return jax.shard_map(shards, mesh=mesh, in_specs=in_specs, out_specs=out_specs, check_vma=False)
```

```python
import functools

import jax
import jax.numpy as jnp
from jax import lax
from jax.experimental import pallas as pl
from jax.experimental.pallas import tpu as pltpu
from jax.sharding import PartitionSpec as P

HEAD_DIM = 64
WINDOW = 128
POOL_SPAN = 512
STRIDE = 4
KERNEL = 5

neg_fill = -1e30
norm_eps = 1e-05
F32 = jnp.float32
BF16 = jnp.bfloat16
ROOT_HALF = 0.7071067811865476
ROOT_TWO_PI = 0.3989422804014327

HALF = WINDOW // 2
WIDE = 2 * WINDOW
PAIR = 2 * HEAD_DIM
TILE = 256
SLOTS = 16
VMEM_LIMIT = 60 * 1024 * 1024
SCALE = 0.05


def product(former, latter):
    return jnp.dot(former, latter, preferred_element_type=F32)


def product_back(former, latter):
    return lax.dot_general(former, latter, (((1,), (1,)), ((), ())), preferred_element_type=F32)


def outer_sum(former, latter):
    return lax.dot_general(former, latter, (((0,), (0,)), ((), ())), preferred_element_type=F32)


def span(index, size):
    return pl.ds(pl.multiple_of(index * size, size), size)


def any_spec():
    return pl.BlockSpec(memory_space=pl.ANY)


def vmem_spec():
    return pl.BlockSpec(memory_space=pltpu.VMEM)


def smem_spec():
    return pl.BlockSpec(memory_space=pltpu.SMEM)


def params(**more):
    return pltpu.CompilerParams(vmem_limit_bytes=VMEM_LIMIT, **more)


def cost(microseconds):
    return pl.CostEstimate(
        flops=int(microseconds * 1.1e9 * SCALE), bytes_accessed=int(microseconds * 3.5e6 * SCALE), transcendentals=0
    )


def fetch(order, stacks, table, half, columns, target, sem):
    rows = stacks[0].shape[1]
    pairs = []
    for k, places in enumerate(table):
        goal = target.at[span(order[k], rows), :]
        pairs.append(
            [
                pltpu.make_async_copy(
                    stacks[stack].at[part, :, pl.ds(start + columns[0], columns[1])], goal, sem
                )
                for stack, part, start in places
            ]
        )

    @pl.when(order[SLOTS] == half)
    def _():
        for pair in pairs:
            pair[0].start()

    @pl.when(order[SLOTS] != half)
    def _():
        for pair in pairs:
            pair[1].start()

    return [pair[0] for pair in pairs]


def fetch_all(order, stacks, table, half_width, target, sem):
    copies = []
    for half in range(2):
        view = target.at[:, pl.ds(half * half_width, half_width)]
        copies = copies + fetch(order, stacks, table, half, (0, half_width), view, sem)
    return copies


def fetch_bulk(bulk, w_in, w_down, sems):
    width = bulk.shape[1]
    block = width // SLOTS
    folds = w_in.shape[1] // width
    first, second = [], []
    for j in range(SLOTS):
        start = j * 2 * folds * block
        for m in range(folds):
            source = bulk.at[pl.ds(start + m * block, block), :]
            target = w_in.at[pl.ds(j * block, block), pl.ds(m * width, width)]
            first.append(pltpu.make_async_copy(source, target, sems[0]))
        source = bulk.at[pl.ds(start + folds * block, folds * block), :]
        target = w_down.at[pl.ds(j * folds * block, folds * block), :]
        second.append(pltpu.make_async_copy(source, target, sems[1]))
    for copy in first + second:
        copy.start()
    return first, second


def settle(copies):
    for copy in copies:
        copy.wait()


def emit(order, source, columns, rows, targets, start, sem):
    copies = []
    for k in range(SLOTS):
        copies.append(
            pltpu.make_async_copy(
                source.at[span(order[k], rows), columns],
                targets[k % 2].at[k // 2 % 2, k // 4, :, pl.ds(start, columns.size)],
                sem,
            )
        )
    for copy in copies:
        copy.start()
    return copies


def tap_matrix(pools):
    rows = lax.broadcasted_iota(jnp.int32, (KERNEL * pools, WIDE), 0)
    cols = lax.broadcasted_iota(jnp.int32, (KERNEL * pools, WIDE), 1)
    tap = rows // pools
    wanted = HALF - KERNEL // 2 + STRIDE * (rows - tap * pools) + tap
    return jnp.where(cols == wanted, 1.0, 0.0).astype(BF16)


def tap_matrix_back(pools):
    rows = lax.broadcasted_iota(jnp.int32, (WIDE, KERNEL * pools), 0)
    cols = lax.broadcasted_iota(jnp.int32, (WIDE, KERNEL * pools), 1)
    tap = cols // pools
    wanted = HALF - KERNEL // 2 + STRIDE * (cols - tap * pools) + tap
    return jnp.where(rows == wanted, 1.0, 0.0).astype(BF16)


TAP_ROW = 6
BIAS_ROW = TAP_ROW + 2 * KERNEL
SMALL = BIAS_ROW + 4
SMALL_ROWS = 16


def tap_row(tap, kind):
    return TAP_ROW + 2 * tap + kind


def project_kernel(table, order, tok, low, high, *refs):
    xext, queries, pairs, pooled, vecs, weights, narrow, sem = refs[-8:]
    stacks = refs[:-8]
    width = tok.shape[1]
    copies = fetch_all(order, stacks, table, 3 * width // 2, weights, sem)
    rows = stacks[0].shape[1]
    for k, places in enumerate(table):
        stack, part, start = places[0]
        copies.append(
            pltpu.make_async_copy(
                stacks[stack].at[part, :, pl.ds(start + 3 * width // 2, 128)],
                narrow.at[span(order[k], rows), :],
                sem,
            )
        )
        copies[-1].start()
    seqs = low.shape[0] // HALF
    for s in range(seqs):
        xext[s * WIDE : s * WIDE + HALF, :] = low[s * HALF : (s + 1) * HALF, :]
        xext[s * WIDE + HALF : s * WIDE + HALF + WINDOW, :] = tok[s * WINDOW : (s + 1) * WINDOW, :]
        xext[s * WIDE + HALF + WINDOW : (s + 1) * WIDE, :] = high[s * HALF : (s + 1) * HALF, :]
    settle(copies)

    @pl.loop(0, 2 * width // TILE)
    def _(n):
        cols = span(n + width // TILE, TILE)
        pairs[:, span(n, TILE)] = product(xext[...], weights[:, cols]).astype(BF16)

    vecs[...] = narrow[...].astype(F32).T[: vecs.shape[0]]
    pools = WINDOW // STRIDE
    matrix = tap_matrix(pools)

    @pl.loop(0, seqs)
    def _(s):
        for n in range(2 * width // TILE):
            cols = slice(n * TILE, (n + 1) * TILE)
            kind, own = divmod(n * TILE, width)
            slab = product(matrix, pairs[span(s, WIDE), cols])
            total = 0.0
            for t in range(KERNEL):
                row = tap_row(t, kind)
                total = total + vecs[row : row + 1, own : own + TILE] * slab[t * pools : (t + 1) * pools]
            pooled[span(s, pools), cols] = total.astype(BF16)

    @pl.loop(0, width // TILE)
    def _(n):
        cols = span(n, TILE)
        queries[:, cols] = product(tok[...], weights[:, cols]).astype(BF16) * HEAD_DIM**-0.5


def lane_masks():
    lane = lax.broadcasted_iota(jnp.int32, (WINDOW, PAIR), 1)
    first = lane < HEAD_DIM
    return first, jnp.where(first, 1.0, 0.0).astype(BF16), jnp.where(first, 0.0, 1.0).astype(BF16)


def side_masks(step):
    row = lax.broadcasted_iota(jnp.int32, (2 * WINDOW, WINDOW), 0)
    lane = lax.broadcasted_iota(jnp.int32, (2 * WINDOW, WINDOW), 1)
    near = lane >= lax.bitwise_and(row, WINDOW - 1) // step
    return near, jnp.where(near, 1.0, 0.0).astype(BF16), jnp.where(near, 0.0, 1.0).astype(BF16)


def stack_heads(block, lanes):
    return jnp.concatenate([block * lanes[1], block * lanes[2]], axis=0)


def merge_heads(block, lanes):
    return jnp.where(lanes[0], block[:WINDOW], block[WINDOW:])


def spread_sides(block, sides):
    return jnp.concatenate([block * sides[1], block * sides[2]], axis=1)


def attend(queries, keys, values, bias, lanes, sides):
    scores = product_back(stack_heads(queries, lanes), keys)
    scores = jnp.where(sides[0], scores[:, :WINDOW], scores[:, WINDOW:]) + bias
    weights = jnp.exp(scores - jnp.max(scores, axis=-1, keepdims=True))
    probs = (weights * (1.0 / jnp.sum(weights, axis=-1, keepdims=True))).astype(BF16)
    mixed = product(spread_sides(probs, sides), values)
    return probs, merge_heads(mixed, lanes)


def attend_back(queries, keys, values, probs, grad_out, lanes, sides):
    grad_stack = stack_heads(grad_out, lanes)
    grad_probs = product_back(grad_stack, values)
    grad_probs = jnp.where(sides[0], grad_probs[:, :WINDOW], grad_probs[:, WINDOW:])
    probs_full = probs.astype(F32)
    centre = jnp.sum(probs_full * grad_probs, axis=-1, keepdims=True)
    grad_scores = spread_sides((probs_full * (grad_probs - centre)).astype(BF16), sides)
    grad_values = outer_sum(spread_sides(probs, sides), grad_stack)
    grad_keys = outer_sum(grad_scores, stack_heads(queries, lanes))
    grad_queries = merge_heads(product(grad_scores, keys), lanes) * HEAD_DIM**-0.5
    return grad_queries, grad_keys, grad_values


def window_kernel(queries, pairs, bias, attended, probs):
    width = queries.shape[1]
    lanes = lane_masks()
    sides = side_masks(1)
    both = jnp.concatenate([bias[0], bias[0]], axis=0)
    for n in range(width // PAIR):
        cols = slice(n * PAIR, (n + 1) * PAIR)
        held, out = attend(
            queries[:, cols],
            pairs[:, cols],
            pairs[:, width + n * PAIR : width + (n + 1) * PAIR],
            both,
            lanes,
            sides,
        )
        probs[0, n] = held
        attended[:, cols] = out.astype(BF16)


def lay_pooled(places, blocks, field):
    pools = blocks[0].shape[0]
    for k, block in enumerate(blocks):
        field[span(places[k], pools), :] = block[...]


def pooled_kernel(table, order, places, attended, bias, *refs):
    blocks = refs[:5]
    stacks = refs[5:-6]
    queries, mixed, probs, field, weights, sem = refs[-6:]
    width = attended.shape[1]
    s = pl.program_id(0)

    @pl.when(s == 0)
    def _():
        copies = fetch(order, stacks, table, 0, (0, width), weights, sem)
        field[...] = jnp.zeros_like(field)
        settle(copies)

        @pl.loop(0, width // TILE)
        def _(n):
            cols = span(n, TILE)
            queries[:, cols] = product(attended[...], weights[:, cols]).astype(BF16) * HEAD_DIM**-0.5

    lay_pooled(places, blocks, field)
    lanes = lane_masks()
    sides = side_masks(STRIDE)
    both = jnp.concatenate([bias[0], bias[0]], axis=0)
    rows = span(s, WINDOW)
    for n in range(width // PAIR):
        cols = slice(n * PAIR, (n + 1) * PAIR)
        held, out = attend(
            queries[rows, cols],
            field[:, cols],
            field[:, width + n * PAIR : width + (n + 1) * PAIR],
            both,
            lanes,
            sides,
        )
        probs[0, n] = held
        first = attended[rows, cols].astype(F32)
        mixed[:, cols] = (first + out.astype(BF16).astype(F32)).astype(BF16)


def feed_kernel(table, order, tok, mixed, cot, vecs, bias_in, bulk, *refs):
    at = len(refs) - 21
    mid_stacks = refs[:at]
    (
        result,
        grad_resid,
        grad_attn,
        gone,
        vec_grads,
        w_out,
        w_in,
        w_down,
        centred,
        rstd,
        normed,
        normed_t,
        active,
        slope,
        field,
        grad_outer,
        grad_in,
        grad_down,
        bias_grad,
        narrow,
        sems,
    ) = refs[at:]
    rows, width = tok.shape
    hidden = w_in.shape[1]
    first = fetch(order, mid_stacks, table, 1, (0, width), w_out, sems.at[0])
    second, third = fetch_bulk(bulk, w_in, w_down, (sems.at[1], sems.at[2]))
    settle(first)

    @pl.loop(0, width // TILE)
    def _(n):
        cols = span(n, TILE)
        field[:, cols] = tok[:, cols].astype(F32) + product(mixed[...], w_out[:, cols]) + vecs[0:1, cols]

    blocks = rows // WINDOW

    @pl.loop(0, blocks)
    def _(b):
        part = span(b, WINDOW)
        resid = field[part, :]
        middle = resid - jnp.mean(resid, axis=-1, keepdims=True)
        scale = lax.rsqrt(jnp.mean(middle * middle, axis=-1, keepdims=True) + norm_eps)
        unit = middle * scale
        centred[part, :] = unit
        rstd[part, :] = jnp.broadcast_to(scale, (WINDOW, 128))
        low = (unit * vecs[1:2, :] + vecs[2:3, :]).astype(BF16)
        normed[part, :] = low
        normed_t[:, part] = low.T

    settle(second)

    @pl.loop(0, hidden // TILE)
    def _(n):
        cols = span(n, TILE)
        inner = product(normed[...], w_in[:, cols]) + bias_in[0:1, cols]
        cdf = 0.5 + 0.5 * lax.erf(inner * ROOT_HALF)
        active[:, cols] = (inner * cdf).astype(BF16)
        slope[:, cols] = (cdf + inner * (jnp.exp(-0.5 * inner * inner) * ROOT_TWO_PI)).astype(BF16)

    settle(third)

    @pl.loop(0, width // TILE)
    def _(n):
        cols = span(n, TILE)
        unit = centred[:, cols] * vecs[1:2, cols] + vecs[2:3, cols]
        field[:, cols] = unit + product(active[...], w_down[:, cols]) + vecs[3:4, cols]

    vec_grads[...] = jnp.zeros_like(vec_grads)

    def add_row(k, value):
        vec_grads[k : k + 1, :] += jnp.sum(value, axis=0, keepdims=True)

    @pl.loop(0, blocks)
    def _(b):
        part = span(b, WINDOW)
        summed = field[part, :]
        middle = summed - jnp.mean(summed, axis=-1, keepdims=True)
        scale = lax.rsqrt(jnp.mean(middle * middle, axis=-1, keepdims=True) + norm_eps)
        unit = middle * scale
        result[part, :] = (unit * vecs[4:5, :] + vecs[5:6, :]).astype(BF16)
        grad = cot[part, :].astype(F32)
        add_row(4, grad * unit)
        add_row(5, grad)
        u = grad * vecs[4:5, :]
        lean = jnp.mean(u * unit, axis=-1, keepdims=True)
        grad = scale * (u - jnp.mean(u, axis=-1, keepdims=True) - unit * lean)
        field[part, :] = grad
        low = grad.astype(BF16)
        grad_outer[part, :] = low
        add_row(3, low.astype(F32))

    @pl.loop(0, hidden // TILE)
    def _(n):
        cols = span(n, TILE)
        grad = product_back(grad_outer[...], w_down[cols, :]).astype(BF16).astype(F32)
        low = (grad * slope[:, cols].astype(F32)).astype(BF16)
        slope[:, cols] = low
        bias_grad[:, cols] = jnp.sum(low.astype(F32), axis=0, keepdims=True)
        grad_down[cols, :] = outer_sum(active[:, cols], grad_outer[...]).astype(BF16)
        grad_in[:, cols] = product(normed_t[...], low).astype(BF16)

    block = width // SLOTS
    folds = hidden // width
    each = gone.shape[0] // SLOTS
    emits = []
    for j in range(SLOTS):
        for m in range(folds):
            source = grad_in.at[pl.ds(j * block, block), pl.ds(m * width, width)]
            target = gone.at[pl.ds(j * each + m * block, block), :]
            emits.append(pltpu.make_async_copy(source, target, sems.at[3]))
        source = grad_down.at[pl.ds(j * folds * block, folds * block), :]
        target = gone.at[pl.ds(j * each + folds * block, folds * block), :]
        emits.append(pltpu.make_async_copy(source, target, sems.at[3]))
    for copy in emits:
        copy.start()

    @pl.loop(0, width // TILE)
    def _(n):
        cols = span(n, TILE)
        field[:, cols] += product_back(slope[...], w_in[cols, :])

    @pl.loop(0, blocks)
    def _(b):
        part = span(b, WINDOW)
        grad = field[part, :]
        unit = centred[part, :]
        add_row(1, grad * unit)
        add_row(2, grad)
        u = grad * vecs[1:2, :]
        lean = jnp.mean(u * unit, axis=-1, keepdims=True)
        grad = rstd[part, 0:1] * (u - jnp.mean(u, axis=-1, keepdims=True) - unit * lean)
        grad_resid[part, :] = grad
        low = grad.astype(BF16)
        grad_attn[part, :] = low
        add_row(0, low.astype(F32))

    narrow[...] = jnp.zeros_like(narrow)
    small = narrow.shape[1]
    for j in range(SLOTS):
        narrow[j, :8, :block] = vec_grads[:, j * block : (j + 1) * block].astype(BF16)
        part = bias_grad[:, j * folds * block : (j + 1) * folds * block]
        narrow[j, 8:9, : folds * block] = part.astype(BF16)
        emits.append(
            pltpu.make_async_copy(
                narrow.at[j], gone.at[pl.ds(j * each + each - small, small), :], sems.at[3]
            )
        )
        emits[-1].start()
    settle(emits)


def pooled_back_kernel(table, order, places, grad_attn, mixed, queries, probs, *refs):
    blocks = refs[:5]
    stacks = refs[5:-12]
    grad_mixed, grad_queries, grad_out, grad_own, grad_away, grad_near, grad_far = refs[-12:-5]
    field, total, grad_low, weights, sem = refs[-5:]
    width = grad_attn.shape[1]
    pools = blocks[0].shape[0]
    s = pl.program_id(0)

    @pl.when(s == 0)
    def _():
        copies = fetch(order, stacks, table, 1, (0, width), weights, sem)
        field[...] = jnp.zeros_like(field)
        settle(copies)

        @pl.loop(0, width // TILE)
        def _(n):
            cols = span(n, TILE)
            grad = product_back(grad_attn[...], weights[cols, :])
            grad_mixed[:, cols] = grad
            grad_low[:, cols] = grad.astype(BF16)
            grad_out[cols, :] = outer_sum(mixed[:, cols], grad_attn[...]).astype(BF16)

    lay_pooled(places, blocks, field)
    lanes = lane_masks()
    sides = side_masks(STRIDE)
    rows = span(s, WINDOW)
    for n in range(width // PAIR):
        cols = slice(n * PAIR, (n + 1) * PAIR)
        others = slice(width + n * PAIR, width + (n + 1) * PAIR)
        grad_q, grad_k, grad_v = attend_back(
            queries[:, cols], field[:, cols], field[:, others], probs[0, n], grad_low[rows, cols], lanes, sides
        )
        grad_queries[:, cols] = grad_q.astype(BF16)
        total[:, cols] = grad_k
        total[:, others] = grad_v
    for k, target in enumerate((grad_own, grad_away.at[0], grad_away.at[1], grad_near, grad_far)):
        target[...] = total[span(places[k], pools), :].astype(BF16)


def window_back_kernel(table, order, grad_mixed, grad_second, first, queries, pairs, probs, *refs):
    stacks = refs[:-6]
    grad_queries, grad_pairs, grad_pooled, grad_low, weights, sem = refs[-6:]
    width = first.shape[1]
    s = pl.program_id(0)

    @pl.when(s == 0)
    def _():
        settle(fetch(order, stacks, table, 0, (0, width), weights, sem))

        @pl.loop(0, width // TILE)
        def _(n):
            cols = span(n, TILE)
            grad = grad_mixed[:, cols] + product_back(grad_second[...], weights[cols, :])
            grad_low[:, cols] = grad.astype(BF16)
            grad_pooled[cols, :] = outer_sum(first[:, cols], grad_second[...]).astype(BF16)

    lanes = lane_masks()
    sides = side_masks(1)
    rows = span(s, WINDOW)
    for n in range(width // PAIR):
        cols = slice(n * PAIR, (n + 1) * PAIR)
        others = slice(width + n * PAIR, width + (n + 1) * PAIR)
        grad_q, grad_k, grad_v = attend_back(
            queries[:, cols], pairs[:, cols], pairs[:, others], probs[0, n], grad_low[rows, cols], lanes, sides
        )
        grad_queries[:, cols] = grad_q.astype(BF16)
        grad_pairs[:, cols] = grad_k.astype(BF16)
        grad_pairs[:, others] = grad_v.astype(BF16)


def conv_back_kernel(table, order, own, away, near, far, vecs, pairs, grad_pairs, *refs):
    stacks = refs[:-6]
    total, tap_grads, edges, weights, rim, sem = refs[-6:]
    width = pairs.shape[1] // 2
    seqs = pairs.shape[0] // WIDE
    pools = WINDOW // STRIDE
    copies = fetch_all(order, stacks, table, 3 * width // 2, weights, sem)
    matrix = tap_matrix(pools)
    back = tap_matrix_back(pools)
    tap_grads[...] = jnp.zeros_like(tap_grads)

    @pl.loop(0, seqs)
    def _(s):
        for n in range(2 * width // TILE):
            cols = slice(n * TILE, (n + 1) * TILE)
            kind, start = divmod(n * TILE, width)
            taps = [vecs[tap_row(t, kind) : tap_row(t, kind) + 1, start : start + TILE] for t in range(KERNEL)]
            part = span(s, pools)
            grad = own[part, cols].astype(F32) + away[part, cols].astype(F32)
            grad = grad + near[part, cols].astype(F32) + far[part, cols].astype(F32)
            grad = grad.astype(BF16).astype(F32)
            spread = [(taps[t] * grad).astype(BF16) for t in range(KERNEL)]
            whole = grad_pairs[span(s, WIDE), cols].astype(F32) + product(back, jnp.concatenate(spread, axis=0))
            total[span(s, WIDE), cols] = whole.astype(BF16)
            slab = product(matrix, pairs[span(s, WIDE), cols])
            for t in range(KERNEL):
                row = 2 * t + kind
                tap_grads[row : row + 1, start : start + TILE] += jnp.sum(
                    grad * slab[t * pools : (t + 1) * pools], axis=0, keepdims=True
                )

    for s in range(seqs):
        rim[s * HALF : (s + 1) * HALF, :] = total[s * WIDE : s * WIDE + HALF, :]
        rim[(seqs + s) * HALF : (seqs + s + 1) * HALF, :] = total[s * WIDE + HALF + WINDOW : (s + 1) * WIDE, :]
    settle(copies)

    @pl.loop(0, width // TILE)
    def _(n):
        cols = span(n, TILE)
        edges[:, cols] = product_back(rim[...], weights[cols, width:]).astype(BF16)


def weight_grad_kernel(order, tok, xext, grad_queries, grad_pairs, tap_grads, *refs):
    grad_pooled, grad_out, keep, give, tok_t, xext_t, total, narrow, sem = refs
    width = tok.shape[1]
    block = width // SLOTS
    targets = (keep, give)
    copies = emit(order, grad_pooled, pl.ds(0, width), block, targets, 3 * width, sem)
    copies += emit(order, grad_out, pl.ds(0, width), block, targets, 4 * width, sem)
    taps = jnp.concatenate([tap_grads[...], jnp.zeros((112, width), F32)], axis=0).T
    narrow[...] = taps.astype(BF16)
    copies += emit(order, narrow, pl.ds(0, 128), block, targets, 5 * width, sem)
    tok_t[...] = tok[...].T
    xext_t[...] = xext[...].T

    @pl.loop(0, width // TILE)
    def _(n):
        cols = span(n, TILE)
        total[:, cols] = product(tok_t[...], grad_queries[:, cols]).astype(BF16)

    @pl.loop(0, 2 * width // TILE)
    def _(n):
        total[:, span(n + width // TILE, TILE)] = product(xext_t[...], grad_pairs[:, span(n, TILE)]).astype(BF16)

    copies += emit(order, total, pl.ds(0, 3 * width), block, targets, 0, sem)
    settle(copies)


def token_grad_kernel(table, order, grad_resid, grad_queries, grad_pairs, low, high, *refs):
    stacks = refs[:-4]
    out, weights, own, sem = refs[-4:]
    width = grad_resid.shape[1]
    seqs = grad_resid.shape[0] // WINDOW
    copies = fetch_all(order, stacks, table, 3 * width // 2, weights, sem)
    for s in range(seqs):
        own[s * WINDOW : (s + 1) * WINDOW, :width] = grad_queries[s * WINDOW : (s + 1) * WINDOW, :]
        own[s * WINDOW : (s + 1) * WINDOW, width:] = grad_pairs[s * WIDE + HALF : s * WIDE + HALF + WINDOW, :]
    settle(copies)

    @pl.loop(0, width // TILE)
    def _(n):
        cols = span(n, TILE)
        out[:, cols] = grad_resid[:, cols] + product_back(own[...], weights[cols, :])
        for s in range(seqs):
            part = slice(s * HALF, (s + 1) * HALF)
            out[s * WINDOW : s * WINDOW + HALF, cols] += low[part, cols].astype(F32)
            out[s * WINDOW + HALF : (s + 1) * WINDOW, cols] += high[part, cols].astype(F32)


def shape_of(*dims, dtype=BF16):
    return jax.ShapeDtypeStruct(dims, dtype)


def turn(block, step):
    return lax.ppermute(block, "shard", [(i, (i - 4 * step) % SLOTS) for i in range(SLOTS)])


def flip(block):
    return lax.ppermute(block, "shard", [(i, i ^ 2) for i in range(SLOTS)])


def other(block):
    return lax.ppermute(block, "rep", [(0, 1), (1, 0)])


def after(value, *others):
    if not direct():
        return value
    return lax.optimization_barrier((value,) + others)[0]


def anchor_kernel(source, out):
    del source, out


def anchor(value):
    return pl.pallas_call(
        anchor_kernel,
        out_shape=jax.ShapeDtypeStruct(value.shape, value.dtype),
        in_specs=[any_spec()],
        out_specs=any_spec(),
        input_output_aliases={0: 0},
        compiler_params=params(),
        cost_estimate=cost(2000),
        name="anchor",
    )(value)


def direct():
    return lax.axis_size("shard") == SLOTS and lax.axis_size("rep") == 2


def block_order():
    if not direct():
        return jnp.arange(SLOTS + 1, dtype=jnp.int32) % SLOTS
    me = lax.axis_index("shard")
    k = jnp.arange(SLOTS, dtype=jnp.int32)
    places = ((me // 4 + k // 4) % 4) * 4 + jnp.bitwise_xor(me % 4, k % 4)
    return jnp.concatenate([places, lax.axis_index("rep")[None]]).astype(jnp.int32)


class Gather:
    def __init__(self, block, mine=None, rest=None):
        self.block, self.mine, self.rest = block, mine, rest

    def turn(self, *gate):
        own = self.block if self.mine is None else self.mine
        own = after(own, *gate)
        self.along = jnp.stack([own] + [turn(own, step) for step in (1, 2, 3)])
        return self.along

    def cross(self, *gate):
        self.across = flip(after(self.along, *gate))
        return self.across

    def rep(self, *gate):
        self.first = jnp.concatenate([self.along, self.across], axis=0)
        self.second = other(after(self.first, *gate))
        return self.second

    def cores(self, *gate):
        if self.mine is None:
            stacks = [self.along, self.across]
            stacks = stacks + [swap(after(stack, *gate)) for stack in stacks]
            table = [((2 * (k % 2) + k // 2 % 2, k // 4, 0),) for k in range(SLOTS)]
        else:
            stacks = [self.first, self.second]
            stacks = stacks + [swap(after(stack, *gate)) for stack in stacks]
            table = []
            for k in range(SLOTS):
                part = k // 2 % 2 * 4 + k // 4
                table.append(((2 * (k % 2), part, 0), (2 * (k % 2) + 1, part, 0)))
        return stacks, tuple(table)


def plain_gather(block, extra=None):
    rows, width = block.shape
    half = width // 2
    rows = rows * lax.axis_size("shard") // SLOTS
    mine, rest = block[:, :half], block[:, half:]
    both = jnp.concatenate([mine] + ([] if extra is None else [extra]) + [rest], axis=1)
    full = lax.all_gather(both, "shard", axis=0, tiled=True)
    table = tuple(((0, k, 0), (0, k, both.shape[1] - half)) for k in range(SLOTS))
    return [full.reshape(SLOTS, rows, both.shape[1])], table


def pack_kernel(order, query, key, value, pooled, out, inner, outer, tokens, taps, *refs):
    vectors, bias = refs[:6], refs[6]
    lead, lead_rest, mid, mid_rest, bulk, low, high, joined, small = refs[7:]
    part, width = query.shape
    half = 3 * width // 2
    for k, source in enumerate((query, key, value)):
        joined[:, k * width : (k + 1) * width] = source[...]
    mine, rest = order[SLOTS], 1 - order[SLOTS]
    small[...] = jnp.zeros_like(small)
    for k, source in enumerate(vectors):
        small[k : k + 1, :part] = source[...].astype(F32)
    for t in range(KERNEL):
        small[tap_row(t, 0) : tap_row(t, 0) + 2, :part] = taps[t].astype(F32)
    small[BIAS_ROW:SMALL, :part] = bias[...].astype(F32)
    lead[:, :half] = joined[:, span(mine, half)]
    lead[:, half:] = small[...].T[:part].astype(BF16)
    lead_rest[...] = joined[:, span(rest, half)]
    first = mine == 0
    mid[...] = jnp.where(first, pooled[...], out[...])
    mid_rest[...] = jnp.where(first, out[...], pooled[...])
    folds = inner.shape[1] // width
    for m in range(folds):
        bulk[m * part : (m + 1) * part, :] = inner[:, m * width : (m + 1) * width]
    bulk[folds * part :, :] = outer[...]
    high[...] = tokens[:, :HALF, :]
    low[...] = tokens[:, tokens.shape[1] - HALF :, :]


def split_kernel(wide, order, keep, arrived, a_keep, a_send, b_keep, b_send):
    half = wide // 2
    mine = span(order[SLOTS], half)
    rest = span(1 - order[SLOTS], half)
    for across in range(2):
        a_keep[across, 0] = keep[across, 0, :, mine] + arrived[across, 0, :, mine]
        a_send[across, 0] = keep[across, 0, :, rest] + arrived[across, 0, :, rest]
        target = b_send if across else b_keep
        target[0] = keep[across, 0, :, wide:] + arrived[across, 0, :, wide:]


def fold_kernel(keep, arrived, x_keep, x_send):
    x_keep[0] = keep[0, 0] + arrived[0, 0]
    x_send[0] = keep[1, 0] + arrived[1, 0]


def join_kernel(x_keep, x_arrived, b_keep, b_arrived, *parts):
    half = x_keep.shape[2]
    for k, part in enumerate(parts):
        part[:, :half] = x_keep[k] + x_arrived[k]
        part[:, half:] = b_keep[k] + b_arrived[k]


def gather_sum_kernel(own, first, second, third, out):
    total = own[...].astype(F32) + first[...].astype(F32) + second[...].astype(F32) + third[...].astype(F32)
    out[...] = total.astype(BF16)


def final_kernel(wide, pieces, order, own, arrived, *refs):
    outs, total = refs[:-1], refs[-1]
    half = wide // 2
    total[:, span(order[SLOTS], half)] = own[:, :half].astype(F32)
    total[:, span(1 - order[SLOTS], half)] = arrived[:, :half].astype(F32)
    total[:, wide:] = own[:, half:].astype(F32) + arrived[:, half:].astype(F32)
    for (start, size), out in zip(pieces, outs):
        out[...] = total[:, start : start + size]


class Scatter:
    def __init__(self, keep, give, order, wide, pieces):
        self.order, self.wide, self.pieces = order, wide, pieces
        self.rows, self.columns = keep.shape[2:]
        self.keep, self.give = keep, give
        if direct():
            self.arrived = swap(give)

    def split(self):
        rows, half, rest = self.rows, self.wide // 2, self.columns - self.wide
        four = pl.BlockSpec((2, 1, rows, self.columns), lambda z: (0, z, 0, 0))
        a_block = pl.BlockSpec((2, 1, rows, half), lambda z: (0, z, 0, 0))
        b_block = pl.BlockSpec((1, rows, rest), lambda z: (z, 0, 0))
        a_shape, b_shape = shape_of(2, 4, rows, half), shape_of(4, rows, rest)
        self.a_keep, a_send, self.b_keep, b_send = pl.pallas_call(
            functools.partial(split_kernel, self.wide),
            grid=(4,),
            out_shape=(a_shape, a_shape, b_shape, b_shape),
            in_specs=[smem_spec(), four, four],
            out_specs=(a_block, a_block, b_block, b_block),
            compiler_params=params(),
            cost_estimate=cost(5),
            name="split",
        )(self.order, self.keep, self.arrived)
        self.a_arrived = other(a_send)
        self.b_arrived = flip(b_send)
        return a_send

    def fold(self):
        rows, half = self.rows, self.wide // 2
        a_block = pl.BlockSpec((2, 1, rows, half), lambda z: (0, z, 0, 0))
        x_block = pl.BlockSpec((1, rows, half), lambda z: (z, 0, 0))
        x_shape = shape_of(4, rows, half)
        self.x_keep, x_send = pl.pallas_call(
            fold_kernel,
            grid=(4,),
            out_shape=(x_shape, x_shape),
            in_specs=[a_block, a_block],
            out_specs=(x_block, x_block),
            compiler_params=params(),
            cost_estimate=cost(4),
            name="fold",
        )(self.a_keep, self.a_arrived)
        self.x_arrived = flip(x_send)
        return x_send

    def join(self):
        shape = shape_of(self.rows, self.columns - self.wide // 2)
        parts = pl.pallas_call(
            join_kernel,
            out_shape=(shape,) * 4,
            in_specs=[vmem_spec()] * 4,
            out_specs=(vmem_spec(),) * 4,
            compiler_params=params(),
            cost_estimate=cost(3),
            name="join",
        )(self.x_keep, self.x_arrived, self.b_keep, self.b_arrived)
        self.turned = [parts[0]] + [turn(parts[step], -step) for step in (1, 2, 3)]
        return parts[1]

    def gather(self):
        self.own = pl.pallas_call(
            gather_sum_kernel,
            out_shape=shape_of(self.rows, self.columns - self.wide // 2),
            in_specs=[vmem_spec()] * 4,
            out_specs=vmem_spec(),
            compiler_params=params(),
            cost_estimate=cost(2),
            name="gather_sum",
        )(*self.turned)
        self.last = other(self.own)
        return self.own

    def final(self):
        return pl.pallas_call(
            functools.partial(final_kernel, self.wide, self.pieces),
            out_shape=tuple(shape_of(self.rows, size, dtype=F32) for _, size in self.pieces),
            in_specs=[smem_spec(), vmem_spec(), vmem_spec()],
            out_specs=(vmem_spec(),) * len(self.pieces),
            scratch_shapes=[pltpu.VMEM((self.rows, self.columns), F32)],
            compiler_params=params(),
            cost_estimate=cost(2),
            name="final",
        )(self.order, self.own, self.last)


def bulk_final_kernel(own, arrived, inner, outer, small):
    part, hidden = inner.shape
    width = own.shape[1]
    total = own[...].astype(F32) + arrived[...].astype(F32)
    folds = hidden // width
    for m in range(folds):
        inner[:, m * width : (m + 1) * width] = total[m * part : (m + 1) * part]
    outer[...] = total[folds * part : 2 * folds * part]
    small[...] = total[2 * folds * part :]


def plain_total(whole):
    return rep_total(lax.psum_scatter(whole, "shard", scatter_dimension=0, tiled=True))


def plain_scatter(blocks, parts):
    keep, give = blocks
    full = jnp.stack([keep, give]).transpose(2, 1, 0, 3, 4).reshape(SLOTS, keep.shape[2], keep.shape[3])
    width = SLOTS * keep.shape[2]
    return [plain_total(full[:, :, start:stop].reshape(width, -1)) for start, stop in parts]


def rep_total(piece):
    count = lax.axis_size("rep")
    total = piece.astype(F32)
    for step in range(1, count):
        route = [(i, (i + step) % count) for i in range(count)]
        total = total + lax.ppermute(piece, "rep", route).astype(F32)
    return total


def shift(block, distance):
    count = lax.axis_size("shard")
    return lax.ppermute(
        block, "shard", [(i, i + distance) for i in range(count) if 0 <= i + distance < count]
    )


def swap(block):
    return lax.ppermute(block, "shard", [(i, i ^ 1) for i in range(lax.axis_size("shard"))])


def hop(block, outer):
    count = lax.axis_size("shard")
    route = [(i, i + (2 if (i % 2 == 0) == outer else -2)) for i in range(count)]
    return lax.ppermute(block, "shard", [(i, j) for i, j in route if 0 <= j < count])


def shards(
    tokens,
    query_proj,
    key_proj,
    value_proj,
    pooled_query,
    output_proj,
    conv_taps,
    output_bias,
    first_gain,
    first_shift,
    inner_proj,
    inner_bias,
    outer_proj,
    outer_bias,
    second_gain,
    second_shift,
    block_ids,
    cotangent,
):
    seqs, tok_span, width = tokens.shape
    rows = seqs * tok_span
    hidden = inner_proj.shape[1]
    device_count = lax.axis_size("shard")
    device_index = lax.axis_index("shard")
    seq_length = tok_span * device_count
    pools = tok_span // STRIDE
    pool_reach = POOL_SPAN // (2 * STRIDE)
    n_pair = width // PAIR
    core = lax.rem(device_index, 2)

    tok = tokens.reshape(rows, width)
    cot = cotangent.reshape(rows, width)
    vectors = [output_bias, first_gain, first_shift, outer_bias, second_gain, second_shift]
    part = width // device_count
    block = width // SLOTS
    order = block_order()
    if direct():
        packed = pl.pallas_call(
            pack_kernel,
            out_shape=(
                shape_of(part, 3 * width // 2 + 128),
                shape_of(part, 3 * width // 2),
                shape_of(part, width),
                shape_of(part, width),
                shape_of(2 * hidden // width * part, width),
                shape_of(seqs, HALF, width),
                shape_of(seqs, HALF, width),
            ),
            in_specs=[smem_spec()] + [vmem_spec()] * 16,
            out_specs=(vmem_spec(),) * 7,
            scratch_shapes=[pltpu.VMEM((part, 3 * width), BF16), pltpu.VMEM((128, 128), F32)],
            compiler_params=params(),
            cost_estimate=cost(3),
            name="pack",
        )(
            order,
            query_proj,
            key_proj,
            value_proj,
            pooled_query,
            output_proj,
            inner_proj,
            outer_proj,
            tokens,
            conv_taps,
            *[vector.reshape(1, part) for vector in vectors],
            inner_bias.reshape(4, part),
        )
        lead, mid = (Gather(None, packed[k], packed[k + 1]) for k in (0, 2))
        tick = jnp.zeros((8, 128), F32)
        tick = anchor(after(tick, packed[0]))
        lead.turn()
        bulk = lax.all_gather(after(packed[4], lead.along), "shard", axis=0, tiled=True)
        tick = anchor(after(tick, lead.along))
        lead.cross(tick)
        tick = anchor(after(tick, lead.across))
        lead.rep()
        tok_low = shift(after(packed[5], tick), 1).reshape(seqs * HALF, width)
        tok_high = shift(after(packed[6], tick), -1).reshape(seqs * HALF, width)
        mid.turn(tick)
        tick = anchor(after(tick, lead.second, mid.along))
        lead, lead_table = lead.cores(tick)
        mid.cross(tick)
    else:
        tok_low = shift(tokens[:, tok_span - HALF :], 1).reshape(seqs * HALF, width)
        tok_high = shift(tokens[:, :HALF], -1).reshape(seqs * HALF, width)
        small = jnp.concatenate(vectors + [conv_taps.reshape(-1), inner_bias]).reshape(SMALL, part).T
        small = jnp.pad(small, ((0, 0), (0, 128 - SMALL)))
        lead, lead_table = plain_gather(jnp.concatenate([query_proj, key_proj, value_proj], axis=1), small)
        mid, mid_table = plain_gather(jnp.concatenate([pooled_query, output_proj], axis=1))
        full = lax.all_gather(inner_proj, "shard", axis=0, tiled=True)
        full = full.reshape(SLOTS, block, hidden // width, width).transpose(0, 2, 1, 3)
        full = full.reshape(SLOTS, hidden // SLOTS, width)
        down = lax.all_gather(outer_proj, "shard", axis=0, tiled=True)
        bulk = jnp.concatenate([full, down.reshape(SLOTS, hidden // SLOTS, width)], axis=1).reshape(-1, width)

    row = jnp.arange(tok_span, dtype=jnp.int32)[:, None]
    lane = jnp.arange(WINDOW, dtype=jnp.int32)[None, :]
    query_ids = lax.dynamic_slice_in_dim(block_ids, device_index * tok_span, tok_span, 1)[:, :, None]

    def bias_for(ids, start, length, step, reach):
        ids = lax.dynamic_slice_in_dim(jnp.pad(ids, ((0, 0), (reach, reach + WINDOW))), start, WIDE, 1)
        near = lane >= row // step
        place = start - reach + jnp.where(near, lane, lane + WINDOW)
        key_ids = jnp.where(near[None], ids[:, None, :WINDOW], ids[:, None, WINDOW:])
        allowed = ((place >= 0) & (place < length))[None] & (key_ids <= query_ids)
        return jnp.where(allowed, 0.0, neg_fill)

    bias_one = bias_for(block_ids, device_index * tok_span, seq_length, 1, HALF)
    bias_two = bias_for(
        block_ids[:, ::STRIDE], device_index * pools, seq_length // STRIDE, STRIDE, pool_reach
    )

    n_lead = len(lead)
    xext, queries, pairs, pooled, vecs = pl.pallas_call(
        functools.partial(project_kernel, lead_table),
        out_shape=(
            shape_of(seqs * WIDE, width),
            shape_of(rows, width),
            shape_of(seqs * WIDE, 2 * width),
            shape_of(seqs * pools, 2 * width),
            shape_of(24, width, dtype=F32),
        ),
        in_specs=[smem_spec()] + [vmem_spec()] * 3 + [any_spec()] * n_lead,
        out_specs=(vmem_spec(),) * 5,
        scratch_shapes=[
            pltpu.VMEM((width, 3 * width), BF16),
            pltpu.VMEM((width, 128), BF16),
            pltpu.SemaphoreType.DMA,
        ],
        compiler_params=params(),
        cost_estimate=cost(15),
        name="project",
    )(order, tok, tok_low, tok_high, *lead)
    bias_in = vecs[BIAS_ROW:SMALL].reshape(4, device_count, part).transpose(1, 0, 2).reshape(1, hidden)

    if direct():
        mid.rep(pooled)
        mid, mid_table = mid.cores()
    pool_away = swap(pooled)
    pool_far = hop(pooled, True)
    pool_near = hop(pooled, False)
    pool_cross = swap(pool_near)
    pool_blocks = (pooled, pool_away, pool_cross, pool_near, pool_far)
    places = jnp.where(
        core == 0, jnp.array([2, 3, 1, 4, 0], jnp.int32), jnp.array([2, 1, 3, 0, 4], jnp.int32)
    )

    seq_block = lambda r, c: pl.BlockSpec((r, c), lambda s: (s, 0))
    whole_block = lambda r, c: pl.BlockSpec((r, c), lambda s: (0, 0))
    bias_block = pl.BlockSpec((1, tok_span, WINDOW), lambda s: (s, 0, 0))
    prob_block = pl.BlockSpec((1, n_pair, 2 * tok_span, WINDOW), lambda s: (s, 0, 0, 0))
    prob_shape = shape_of(seqs, n_pair, 2 * tok_span, WINDOW)

    attended, probs_one = pl.pallas_call(
        window_kernel,
        grid=(seqs,),
        out_shape=(shape_of(rows, width), prob_shape),
        in_specs=[seq_block(tok_span, width), seq_block(WIDE, 2 * width), bias_block],
        out_specs=(seq_block(tok_span, width), prob_block),
        compiler_params=params(),
        cost_estimate=cost(10),
        name="window",
    )(queries, pairs, bias_one)

    n_mid = len(mid)
    pool_specs = [seq_block(pools, 2 * width)] * 5
    second, mixed, probs_two = pl.pallas_call(
        functools.partial(pooled_kernel, mid_table),
        grid=(seqs,),
        out_shape=(shape_of(rows, width), shape_of(rows, width), prob_shape),
        in_specs=[smem_spec(), smem_spec(), whole_block(rows, width), bias_block]
        + pool_specs
        + [any_spec()] * n_mid,
        out_specs=(whole_block(rows, width), seq_block(tok_span, width), prob_block),
        scratch_shapes=[
            pltpu.VMEM((WIDE, 2 * width), BF16),
            pltpu.VMEM((width, width), BF16),
            pltpu.SemaphoreType.DMA,
        ],
        compiler_params=params(),
        cost_estimate=cost(14),
        name="pooled",
    )(order, places, attended, bias_two, *pool_blocks, *mid)

    each = 2 * hidden // SLOTS + SMALL_ROWS
    result, grad_resid, grad_attn, grad_bulk, _ = pl.pallas_call(
        functools.partial(feed_kernel, mid_table),
        out_shape=(
            shape_of(rows, width),
            shape_of(rows, width, dtype=F32),
            shape_of(rows, width),
            shape_of(SLOTS * each, width),
            shape_of(8, width, dtype=F32),
        ),
        in_specs=[smem_spec()] + [vmem_spec()] * 5 + [any_spec()] * (1 + n_mid),
        out_specs=(vmem_spec(),) * 3 + (any_spec(), vmem_spec()),
        scratch_shapes=[
            pltpu.VMEM((width, width), BF16),
            pltpu.VMEM((width, hidden), BF16),
            pltpu.VMEM((hidden, width), BF16),
            pltpu.VMEM((rows, width), F32),
            pltpu.VMEM((rows, 128), F32),
            pltpu.VMEM((rows, width), BF16),
            pltpu.VMEM((width, rows), BF16),
            pltpu.VMEM((rows, hidden), BF16),
            pltpu.VMEM((rows, hidden), BF16),
            pltpu.VMEM((rows, width), F32),
            pltpu.VMEM((rows, width), BF16),
            pltpu.VMEM((width, hidden), BF16),
            pltpu.VMEM((hidden, width), BF16),
            pltpu.VMEM((1, hidden), F32),
            pltpu.VMEM((SLOTS, SMALL_ROWS, width), BF16),
            pltpu.SemaphoreType.DMA((4,)),
        ],
        compiler_params=params(),
        cost_estimate=cost(45),
        name="feed",
    )(order, tok, mixed, cot, vecs, bias_in, bulk, *mid)
    if direct():
        own_bulk = lax.psum_scatter(grad_bulk, "shard", scatter_dimension=0, tiled=True)

    back_shape = shape_of(seqs * pools, 2 * width)
    grad_mixed, grad_second, grad_out, pg_own, pg_away, pg_near, pg_far = pl.pallas_call(
        functools.partial(pooled_back_kernel, mid_table),
        grid=(seqs,),
        out_shape=(
            shape_of(rows, width, dtype=F32),
            shape_of(rows, width),
            shape_of(width, width),
            back_shape,
            shape_of(2, seqs * pools, 2 * width),
            back_shape,
            back_shape,
        ),
        in_specs=[
            smem_spec(),
            smem_spec(),
            whole_block(rows, width),
            whole_block(rows, width),
            seq_block(tok_span, width),
            prob_block,
        ]
        + pool_specs
        + [any_spec()] * n_mid,
        out_specs=(
            whole_block(rows, width),
            seq_block(tok_span, width),
            whole_block(width, width),
            seq_block(pools, 2 * width),
            pl.BlockSpec((2, pools, 2 * width), lambda s: (0, s, 0)),
            seq_block(pools, 2 * width),
            seq_block(pools, 2 * width),
        ),
        scratch_shapes=[
            pltpu.VMEM((WIDE, 2 * width), BF16),
            pltpu.VMEM((WIDE, 2 * width), F32),
            pltpu.VMEM((rows, width), BF16),
            pltpu.VMEM((width, width), BF16),
            pltpu.SemaphoreType.DMA,
        ],
        compiler_params=params(),
        cost_estimate=cost(22),
        name="pooled_back",
    )(order, places, grad_attn, mixed, second, probs_two, *pool_blocks, *mid)

    pg_cross = swap(pg_away)
    back_far = lax.ppermute(pg_far, "shard", back_route(device_count, True))
    pg_near = (pg_near.astype(F32) + pg_cross[1].astype(F32)).astype(BF16)
    back_near = lax.ppermute(pg_near, "shard", back_route(device_count, False))

    grad_queries, grad_pairs, grad_pooled = pl.pallas_call(
        functools.partial(window_back_kernel, mid_table),
        grid=(seqs,),
        out_shape=(shape_of(rows, width), shape_of(seqs * WIDE, 2 * width), shape_of(width, width)),
        in_specs=[
            smem_spec(),
            whole_block(rows, width),
            whole_block(rows, width),
            whole_block(rows, width),
            seq_block(tok_span, width),
            seq_block(WIDE, 2 * width),
            prob_block,
        ]
        + [any_spec()] * n_mid,
        out_specs=(seq_block(tok_span, width), seq_block(WIDE, 2 * width), whole_block(width, width)),
        scratch_shapes=[
            pltpu.VMEM((rows, width), BF16),
            pltpu.VMEM((width, width), BF16),
            pltpu.SemaphoreType.DMA,
        ],
        compiler_params=params(),
        cost_estimate=cost(22),
        name="window_back",
    )(order, grad_mixed, grad_second, attended, queries, pairs, probs_one, *mid)

    pair_total, tap_grads, edges = pl.pallas_call(
        functools.partial(conv_back_kernel, lead_table),
        out_shape=(
            shape_of(seqs * WIDE, 2 * width),
            shape_of(16, width, dtype=F32),
            shape_of(2 * seqs * HALF, width),
        ),
        in_specs=[smem_spec()] + [vmem_spec()] * 7 + [any_spec()] * n_lead,
        out_specs=(vmem_spec(),) * 3,
        scratch_shapes=[
            pltpu.VMEM((width, 3 * width), BF16),
            pltpu.VMEM((2 * seqs * HALF, 2 * width), BF16),
            pltpu.SemaphoreType.DMA,
        ],
        compiler_params=params(),
        cost_estimate=cost(12),
        name="conv_back",
    )(order, pg_own, pg_cross[0], back_near, back_far, vecs, pairs, grad_pairs, *lead)

    edge_high = shift(edges[: seqs * HALF], -1)
    edge_low = shift(edges[seqs * HALF :], 1)

    lead_shape = shape_of(2, 4, block, 5 * width + 128)
    lead_keep, lead_give = pl.pallas_call(
        weight_grad_kernel,
        out_shape=(lead_shape, lead_shape),
        in_specs=[smem_spec()] + [vmem_spec()] * 7,
        out_specs=(any_spec(),) * 2,
        scratch_shapes=[
            pltpu.VMEM((width, rows), BF16),
            pltpu.VMEM((width, seqs * WIDE), BF16),
            pltpu.VMEM((width, 3 * width), BF16),
            pltpu.VMEM((width, 128), BF16),
            pltpu.SemaphoreType.DMA,
        ],
        compiler_params=params(),
        cost_estimate=cost(14),
        name="weight_grad",
    )(order, tok, xext, grad_queries, pair_total, tap_grads, grad_pooled, grad_out)
    pieces = tuple((k * width, width) for k in range(5)) + ((5 * width, 128),)
    lead_sum = Scatter(lead_keep, lead_give, order, 14 * 128, pieces)
    if direct():
        grad_resid = after(grad_resid, lead_sum.split())

    tokens_grad = pl.pallas_call(
        functools.partial(token_grad_kernel, lead_table),
        out_shape=shape_of(rows, width, dtype=F32),
        in_specs=[smem_spec()] + [vmem_spec()] * 5 + [any_spec()] * n_lead,
        out_specs=vmem_spec(),
        scratch_shapes=[
            pltpu.VMEM((width, 3 * width), BF16),
            pltpu.VMEM((rows, 3 * width), BF16),
            pltpu.SemaphoreType.DMA,
        ],
        compiler_params=params(),
        cost_estimate=cost(11),
        name="token_grad",
    )(order, grad_resid, grad_queries, pair_total, edge_low, edge_high, *lead)

    folds = hidden // width
    if direct():
        lead_sum.fold()
        lead_sum.join()
        lead_sum.gather()
        own_in, own_down, small_own = pl.pallas_call(
            bulk_final_kernel,
            out_shape=(
                shape_of(part, hidden, dtype=F32),
                shape_of(folds * part, width, dtype=F32),
                shape_of(SMALL_ROWS, width, dtype=F32),
            ),
            in_specs=[vmem_spec()] * 2,
            out_specs=(vmem_spec(),) * 3,
            compiler_params=params(),
            cost_estimate=cost(2),
            name="bulk_final",
        )(own_bulk, other(own_bulk))
        vec_own = [small_own[k, :part] for k in range(6)]
        bias_own = small_own[8, : folds * part]
        own_query, own_keys, own_values, own_pooled, own_out, taps_own = lead_sum.final()
    else:
        whole = grad_bulk.reshape(SLOTS, each, width)
        inner_part = whole[:, : folds * block].reshape(SLOTS, folds, block, width).transpose(0, 2, 1, 3)
        own_in = plain_total(inner_part.reshape(width, hidden))
        own_down = plain_total(whole[:, folds * block : 2 * folds * block].reshape(hidden, width))
        small = whole[:, 2 * folds * block :]
        vec_own = [plain_total(small[:, k, :block].reshape(width)) for k in range(6)]
        bias_own = plain_total(small[:, 8, : folds * block].reshape(hidden))
        parts = [(k * width, (k + 1) * width) for k in range(5)] + [(5 * width, None)]
        own_query, own_keys, own_values, own_pooled, own_out, taps_own = plain_scatter(
            (lead_keep, lead_give), parts
        )
    taps_own = taps_own.T[: 2 * KERNEL].reshape(KERNEL, 2, part)
    return (
        result.reshape(tokens.shape),
        tokens_grad.reshape(tokens.shape),
        own_query,
        own_keys,
        own_values,
        own_pooled,
        own_out,
        taps_own,
        vec_own[0],
        vec_own[1],
        vec_own[2],
        own_in,
        bias_own,
        own_down,
        vec_own[3],
        vec_own[4],
        vec_own[5],
    )


def back_route(count, outer):
    route = [(i, i + (2 if (i % 2 == 0) == outer else -2)) for i in range(count)]
    return [(j, i) for i, j in route if 0 <= j < count]


def solution(mesh):
    in_specs = (
        P("rep", "shard", None),
        P("shard", None),
        P("shard", None),
        P("shard", None),
        P("shard", None),
        P("shard", None),
        P(None, None, "shard"),
        P("shard"),
        P("shard"),
        P("shard"),
        P("shard", None),
        P("shard"),
        P("shard", None),
        P("shard"),
        P("shard"),
        P("shard"),
        P("rep", None),
        P("rep", "shard", None),
    )
    out_specs = (
        P("rep", "shard", None),
        P("rep", "shard", None),
        P("shard", None),
        P("shard", None),
        P("shard", None),
        P("shard", None),
        P("shard", None),
        P(None, None, "shard"),
        P("shard"),
        P("shard"),
        P("shard"),
        P("shard", None),
        P("shard"),
        P("shard", None),
        P("shard"),
        P("shard"),
        P("shard"),
    )
    return jax.shard_map(shards, mesh=mesh, in_specs=in_specs, out_specs=out_specs, check_vma=False)
```

```python
import functools

import jax
import jax.numpy as jnp
from jax import lax
from jax.experimental import pallas as pl
from jax.experimental.pallas import tpu as pltpu
from jax.sharding import PartitionSpec as P

HEAD_DIM = 64
WINDOW = 128
POOL_SPAN = 512
STRIDE = 4
KERNEL = 5

neg_fill = -1e30
norm_eps = 1e-05
F32 = jnp.float32
BF16 = jnp.bfloat16
ROOT_HALF = 0.7071067811865476
ROOT_TWO_PI = 0.3989422804014327

HALF = WINDOW // 2
WIDE = 2 * WINDOW
PAIR = 2 * HEAD_DIM
TILE = 256
SLOTS = 16
VMEM_LIMIT = 58
SCALE = 0.05


def product(former, latter):
    return jnp.dot(former, latter, preferred_element_type=F32)


def product_back(former, latter):
    return lax.dot_general(former, latter, (((1,), (1,)), ((), ())), preferred_element_type=F32)


def outer_sum(former, latter):
    return lax.dot_general(former, latter, (((0,), (0,)), ((), ())), preferred_element_type=F32)


def span(index, size):
    return pl.ds(pl.multiple_of(index * size, size), size)


def any_spec():
    return pl.BlockSpec(memory_space=pl.ANY)


def hbm_spec():
    return pl.BlockSpec(memory_space=pltpu.HBM)


def vmem_spec():
    return pl.BlockSpec(memory_space=pltpu.VMEM)


def smem_spec():
    return pl.BlockSpec(memory_space=pltpu.SMEM)


def params(mebibytes=VMEM_LIMIT):
    return pltpu.CompilerParams(vmem_limit_bytes=mebibytes * 1024 * 1024)


def cost(microseconds):
    return pl.CostEstimate(
        flops=int(microseconds * 1.1e9 * SCALE), bytes_accessed=int(microseconds * 3.5e6 * SCALE), transcendentals=0
    )


def fetch(order, stacks, table, half, columns, target, sem):
    rows = stacks[0].shape[1]
    pairs = []
    for k, places in enumerate(table):
        goal = target.at[span(order[k], rows), :]
        pairs.append(
            [
                pltpu.make_async_copy(
                    stacks[stack].at[part, :, pl.ds(start + columns[0], columns[1])], goal, sem
                )
                for stack, part, start in places
            ]
        )

    @pl.when(order[SLOTS] == half)
    def _():
        for pair in pairs:
            pair[0].start()

    @pl.when(order[SLOTS] != half)
    def _():
        for pair in pairs:
            pair[1].start()

    return [pair[0] for pair in pairs]


def fetch_all(order, stacks, table, half_width, target, sem):
    copies = []
    for half in range(2):
        view = target.at[:, pl.ds(half * half_width, half_width)]
        copies = copies + fetch(order, stacks, table, half, (0, half_width), view, sem)
    return copies


def bulk_rows(width, hidden):
    return (2 * width + 2 * hidden) // SLOTS


def fetch_square(bulk, which, target, sem):
    width = bulk.shape[1]
    block = width // SLOTS
    each = bulk.shape[0] // SLOTS
    copies = []
    for j in range(SLOTS):
        source = bulk.at[pl.ds(j * each + which * block, block), :]
        copies.append(pltpu.make_async_copy(source, target.at[pl.ds(j * block, block), :], sem))
        copies[-1].start()
    return copies


def fetch_bulk(bulk, w_in, w_down, sems):
    width = bulk.shape[1]
    block = width // SLOTS
    each = bulk.shape[0] // SLOTS
    folds = w_in.shape[1] // width
    first, second = [], []
    for j in range(SLOTS):
        start = j * each + 2 * block
        for m in range(folds):
            source = bulk.at[pl.ds(start + m * block, block), :]
            target = w_in.at[pl.ds(j * block, block), pl.ds(m * width, width)]
            first.append(pltpu.make_async_copy(source, target, sems[0]))
        source = bulk.at[pl.ds(start + folds * block, folds * block), :]
        target = w_down.at[pl.ds(j * folds * block, folds * block), :]
        second.append(pltpu.make_async_copy(source, target, sems[1]))
    for copy in first + second:
        copy.start()
    return first, second


def settle(copies):
    for copy in copies:
        copy.wait()


def emit(order, source, columns, rows, targets, start, sem):
    copies = []
    for k in range(SLOTS):
        copies.append(
            pltpu.make_async_copy(
                source.at[span(order[k], rows), columns],
                targets[k % 2].at[k // 2 % 2, k // 4, :, pl.ds(start, columns.size)],
                sem,
            )
        )
    for copy in copies:
        copy.start()
    return copies


def tap_matrix(pools):
    rows = lax.broadcasted_iota(jnp.int32, (KERNEL * pools, WIDE), 0)
    cols = lax.broadcasted_iota(jnp.int32, (KERNEL * pools, WIDE), 1)
    tap = rows // pools
    wanted = HALF - KERNEL // 2 + STRIDE * (rows - tap * pools) + tap
    return jnp.where(cols == wanted, 1.0, 0.0).astype(BF16)


def tap_matrix_back(pools):
    rows = lax.broadcasted_iota(jnp.int32, (WIDE, KERNEL * pools), 0)
    cols = lax.broadcasted_iota(jnp.int32, (WIDE, KERNEL * pools), 1)
    tap = cols // pools
    wanted = HALF - KERNEL // 2 + STRIDE * (cols - tap * pools) + tap
    return jnp.where(rows == wanted, 1.0, 0.0).astype(BF16)


TAP_ROW = 6
BIAS_ROW = TAP_ROW + 2 * KERNEL
SMALL = BIAS_ROW + 4
SMALL_ROWS = 16


def tap_row(tap, kind):
    return TAP_ROW + 2 * tap + kind


def project_kernel(table, order, tok, low, high, *refs):
    queries, pairs, pooled, vecs, xext, weights, narrow, sem = refs[-8:]
    stacks = refs[:-8]
    width = tok.shape[1]
    copies = fetch_all(order, stacks, table, 3 * width // 2, weights, sem)
    rows = stacks[0].shape[1]
    for k, places in enumerate(table):
        stack, part, start = places[0]
        copies.append(
            pltpu.make_async_copy(
                stacks[stack].at[part, :, pl.ds(start + 3 * width // 2, 128)],
                narrow.at[span(order[k], rows), :],
                sem,
            )
        )
        copies[-1].start()
    seqs = low.shape[0] // HALF
    for s in range(seqs):
        xext[s * WIDE : s * WIDE + HALF, :] = low[s * HALF : (s + 1) * HALF, :]
        xext[s * WIDE + HALF : s * WIDE + HALF + WINDOW, :] = tok[s * WINDOW : (s + 1) * WINDOW, :]
        xext[s * WIDE + HALF + WINDOW : (s + 1) * WIDE, :] = high[s * HALF : (s + 1) * HALF, :]
    settle(copies)

    @pl.loop(0, 2 * width // TILE)
    def _(n):
        cols = span(n + width // TILE, TILE)
        pairs[:, span(n, TILE)] = product(xext[...], weights[:, cols]).astype(BF16)

    vecs[...] = narrow[...].astype(F32).T[: vecs.shape[0]]
    pools = WINDOW // STRIDE
    matrix = tap_matrix(pools)

    @pl.loop(0, seqs)
    def _(s):
        for n in range(2 * width // TILE):
            cols = slice(n * TILE, (n + 1) * TILE)
            kind, own = divmod(n * TILE, width)
            slab = product(matrix, pairs[span(s, WIDE), cols])
            total = 0.0
            for t in range(KERNEL):
                row = tap_row(t, kind)
                total = total + vecs[row : row + 1, own : own + TILE] * slab[t * pools : (t + 1) * pools]
            pooled[span(s, pools), cols] = total.astype(BF16)

    @pl.loop(0, width // TILE)
    def _(n):
        cols = span(n, TILE)
        queries[:, cols] = product(tok[...], weights[:, cols]).astype(BF16) * HEAD_DIM**-0.5


def lane_masks():
    lane = lax.broadcasted_iota(jnp.int32, (WINDOW, PAIR), 1)
    first = lane < HEAD_DIM
    return first, jnp.where(first, 1.0, 0.0).astype(BF16), jnp.where(first, 0.0, 1.0).astype(BF16)


def side_masks(step):
    slot = lax.broadcasted_iota(jnp.int32, (WINDOW, 2 * WINDOW), 0)
    query = lax.broadcasted_iota(jnp.int32, (WINDOW, 2 * WINDOW), 1)
    near = slot >= lax.bitwise_and(query, WINDOW - 1) // step
    return near, jnp.where(near, 1.0, 0.0).astype(BF16), jnp.where(near, 0.0, 1.0).astype(BF16)


def stack_heads(block, lanes):
    return jnp.concatenate([block * lanes[1], block * lanes[2]], axis=0)


def merge_heads(block, lanes):
    return jnp.where(lanes[0], block[:WINDOW], block[WINDOW:])


def spread_sides(block, sides):
    return jnp.concatenate([block * sides[1], block * sides[2]], axis=0)


def attend(queries, keys, values, bias, lanes, sides):
    scores = product_back(keys, stack_heads(queries, lanes))
    scores = jnp.where(sides[0], scores[:WINDOW], scores[WINDOW:]) + bias
    weights = jnp.exp(scores - jnp.max(scores, axis=0, keepdims=True))
    probs = (weights * (1.0 / jnp.sum(weights, axis=0, keepdims=True))).astype(BF16)
    mixed = outer_sum(spread_sides(probs, sides), values)
    return probs, merge_heads(mixed, lanes)


def attend_back(queries, keys, values, probs, grad_out, lanes, sides):
    grad_stack = stack_heads(grad_out, lanes)
    grad_probs = product_back(values, grad_stack)
    grad_probs = jnp.where(sides[0], grad_probs[:WINDOW], grad_probs[WINDOW:])
    probs_full = probs.astype(F32)
    centre = jnp.sum(probs_full * grad_probs, axis=0, keepdims=True)
    grad_scores = spread_sides((probs_full * (grad_probs - centre)).astype(BF16), sides)
    grad_values = product(spread_sides(probs, sides), grad_stack)
    grad_keys = product(grad_scores, stack_heads(queries, lanes))
    grad_queries = merge_heads(outer_sum(grad_scores, keys), lanes) * HEAD_DIM**-0.5
    return grad_queries, grad_keys, grad_values


def window_kernel(queries, pairs, bias, attended, probs):
    width = queries.shape[1]
    lanes = lane_masks()
    sides = side_masks(1)
    both = jnp.concatenate([bias[0], bias[0]], axis=1)
    for n in range(width // PAIR):
        cols = slice(n * PAIR, (n + 1) * PAIR)
        held, out = attend(
            queries[:, cols],
            pairs[:, cols],
            pairs[:, width + n * PAIR : width + (n + 1) * PAIR],
            both,
            lanes,
            sides,
        )
        probs[0, n] = held
        attended[:, cols] = out.astype(BF16)


def lay_pooled(places, blocks, field):
    pools = blocks[0].shape[0]
    for k, block in enumerate(blocks):
        field[span(places[k], pools), :] = block[...]


def pooled_kernel(places, attended, bias, bulk, *refs):
    blocks = refs[:5]
    queries, mixed, probs, weights, field, sem = refs[-6:]
    width = attended.shape[1]
    s = pl.program_id(0)

    @pl.when(s == 0)
    def _():
        copies = fetch_square(bulk, 0, weights, sem)
        field[...] = jnp.zeros_like(field)
        settle(copies)

        @pl.loop(0, width // TILE)
        def _(n):
            cols = span(n, TILE)
            queries[:, cols] = product(attended[...], weights[:, cols]).astype(BF16) * HEAD_DIM**-0.5

    lay_pooled(places, blocks, field)
    lanes = lane_masks()
    sides = side_masks(STRIDE)
    both = jnp.concatenate([bias[0], bias[0]], axis=1)
    rows = span(s, WINDOW)
    for n in range(width // PAIR):
        cols = slice(n * PAIR, (n + 1) * PAIR)
        held, out = attend(
            queries[rows, cols],
            field[:, cols],
            field[:, width + n * PAIR : width + (n + 1) * PAIR],
            both,
            lanes,
            sides,
        )
        probs[0, n] = held
        first = attended[rows, cols].astype(F32)
        mixed[:, cols] = (first + out.astype(BF16).astype(F32)).astype(BF16)


def feed_kernel(tok, mixed, cot, vecs, bias_in, bulk, *refs):
    (
        result,
        grad_resid,
        grad_attn,
        gone,
        w_out,
        vec_grads,
        w_in,
        w_down,
        centred,
        rstd,
        normed,
        normed_t,
        active,
        slope,
        field,
        grad_outer,
        grad_in,
        grad_down,
        bias_grad,
        narrow,
        sems,
    ) = refs
    rows, width = tok.shape
    hidden = w_in.shape[1]
    first = fetch_square(bulk, 1, w_out, sems.at[0])
    second, third = fetch_bulk(bulk, w_in, w_down, (sems.at[1], sems.at[2]))
    settle(first)

    @pl.loop(0, width // TILE)
    def _(n):
        cols = span(n, TILE)
        field[:, cols] = tok[:, cols].astype(F32) + product(mixed[...], w_out[:, cols]) + vecs[0:1, cols]

    blocks = rows // WINDOW

    @pl.loop(0, blocks)
    def _(b):
        part = span(b, WINDOW)
        resid = field[part, :]
        middle = resid - jnp.mean(resid, axis=-1, keepdims=True)
        scale = lax.rsqrt(jnp.mean(middle * middle, axis=-1, keepdims=True) + norm_eps)
        unit = middle * scale
        centred[part, :] = unit
        rstd[part, :] = jnp.broadcast_to(scale, (WINDOW, 128))
        low = (unit * vecs[1:2, :] + vecs[2:3, :]).astype(BF16)
        normed[part, :] = low
        normed_t[:, part] = low.T

    settle(second)

    @pl.loop(0, hidden // TILE)
    def _(n):
        cols = span(n, TILE)
        inner = product(normed[...], w_in[:, cols]) + bias_in[0:1, cols]
        cdf = 0.5 + 0.5 * lax.erf(inner * ROOT_HALF)
        active[:, cols] = (inner * cdf).astype(BF16)
        slope[:, cols] = (cdf + inner * (jnp.exp(-0.5 * inner * inner) * ROOT_TWO_PI)).astype(BF16)

    settle(third)

    @pl.loop(0, width // TILE)
    def _(n):
        cols = span(n, TILE)
        unit = centred[:, cols] * vecs[1:2, cols] + vecs[2:3, cols]
        field[:, cols] = unit + product(active[...], w_down[:, cols]) + vecs[3:4, cols]

    vec_grads[...] = jnp.zeros_like(vec_grads)

    def add_row(k, value):
        vec_grads[k : k + 1, :] += jnp.sum(value, axis=0, keepdims=True)

    @pl.loop(0, blocks)
    def _(b):
        part = span(b, WINDOW)
        summed = field[part, :]
        middle = summed - jnp.mean(summed, axis=-1, keepdims=True)
        scale = lax.rsqrt(jnp.mean(middle * middle, axis=-1, keepdims=True) + norm_eps)
        unit = middle * scale
        result[part, :] = (unit * vecs[4:5, :] + vecs[5:6, :]).astype(BF16)
        grad = cot[part, :].astype(F32)
        add_row(4, grad * unit)
        add_row(5, grad)
        u = grad * vecs[4:5, :]
        lean = jnp.mean(u * unit, axis=-1, keepdims=True)
        grad = scale * (u - jnp.mean(u, axis=-1, keepdims=True) - unit * lean)
        field[part, :] = grad
        low = grad.astype(BF16)
        grad_outer[part, :] = low
        add_row(3, low.astype(F32))

    @pl.loop(0, hidden // TILE)
    def _(n):
        cols = span(n, TILE)
        grad = product_back(grad_outer[...], w_down[cols, :]).astype(BF16).astype(F32)
        low = (grad * slope[:, cols].astype(F32)).astype(BF16)
        slope[:, cols] = low
        bias_grad[:, cols] = jnp.sum(low.astype(F32), axis=0, keepdims=True)
        grad_down[cols, :] = outer_sum(active[:, cols], grad_outer[...]).astype(BF16)
        grad_in[:, cols] = product(normed_t[...], low).astype(BF16)

    block = width // SLOTS
    folds = hidden // width
    each = gone.shape[0] // SLOTS
    emits = []
    for j in range(SLOTS):
        for m in range(folds):
            source = grad_in.at[pl.ds(j * block, block), pl.ds(m * width, width)]
            target = gone.at[pl.ds(j * each + m * block, block), :]
            emits.append(pltpu.make_async_copy(source, target, sems.at[3]))
        source = grad_down.at[pl.ds(j * folds * block, folds * block), :]
        target = gone.at[pl.ds(j * each + folds * block, folds * block), :]
        emits.append(pltpu.make_async_copy(source, target, sems.at[3]))
    for copy in emits:
        copy.start()

    @pl.loop(0, width // TILE)
    def _(n):
        cols = span(n, TILE)
        field[:, cols] += product_back(slope[...], w_in[cols, :])

    @pl.loop(0, blocks)
    def _(b):
        part = span(b, WINDOW)
        grad = field[part, :]
        unit = centred[part, :]
        add_row(1, grad * unit)
        add_row(2, grad)
        u = grad * vecs[1:2, :]
        lean = jnp.mean(u * unit, axis=-1, keepdims=True)
        grad = rstd[part, 0:1] * (u - jnp.mean(u, axis=-1, keepdims=True) - unit * lean)
        grad_resid[part, :] = grad
        low = grad.astype(BF16)
        grad_attn[part, :] = low
        add_row(0, low.astype(F32))

    narrow[...] = jnp.zeros_like(narrow)
    small = narrow.shape[1]
    for j in range(SLOTS):
        narrow[j, :8, :block] = vec_grads[:, j * block : (j + 1) * block].astype(BF16)
        part = bias_grad[:, j * folds * block : (j + 1) * folds * block]
        narrow[j, 8:9, : folds * block] = part.astype(BF16)
        emits.append(
            pltpu.make_async_copy(
                narrow.at[j], gone.at[pl.ds(j * each + each - small, small), :], sems.at[3]
            )
        )
        emits[-1].start()
    settle(emits)


def pooled_back_kernel(places, grad_attn, mixed, queries, probs, weights, *refs):
    blocks = refs[:5]
    grad_mixed, grad_queries, grad_out, grad_own, grad_away, grad_near, grad_far = refs[-10:-3]
    field, total, grad_low = refs[-3:]
    width = grad_attn.shape[1]
    pools = blocks[0].shape[0]
    s = pl.program_id(0)

    @pl.when(s == 0)
    def _():
        field[...] = jnp.zeros_like(field)

        @pl.loop(0, width // TILE)
        def _(n):
            cols = span(n, TILE)
            grad = product_back(grad_attn[...], weights[cols, :])
            grad_mixed[:, cols] = grad
            grad_low[:, cols] = grad.astype(BF16)
            grad_out[cols, :] = outer_sum(mixed[:, cols], grad_attn[...]).astype(BF16)

    lay_pooled(places, blocks, field)
    lanes = lane_masks()
    sides = side_masks(STRIDE)
    rows = span(s, WINDOW)
    for n in range(width // PAIR):
        cols = slice(n * PAIR, (n + 1) * PAIR)
        others = slice(width + n * PAIR, width + (n + 1) * PAIR)
        grad_q, grad_k, grad_v = attend_back(
            queries[:, cols], field[:, cols], field[:, others], probs[0, n], grad_low[rows, cols], lanes, sides
        )
        grad_queries[:, cols] = grad_q.astype(BF16)
        total[:, cols] = grad_k
        total[:, others] = grad_v
    for k, target in enumerate((grad_own, grad_away.at[0], grad_away.at[1], grad_near, grad_far)):
        target[...] = total[span(places[k], pools), :].astype(BF16)


def window_back_kernel(grad_mixed, grad_second, first, queries, pairs, probs, weights, *refs):
    grad_queries, grad_pairs, grad_pooled, grad_low = refs
    width = first.shape[1]
    s = pl.program_id(0)

    @pl.when(s == 0)
    def _():
        @pl.loop(0, width // TILE)
        def _(n):
            cols = span(n, TILE)
            grad = grad_mixed[:, cols] + product_back(grad_second[...], weights[cols, :])
            grad_low[:, cols] = grad.astype(BF16)
            grad_pooled[cols, :] = outer_sum(first[:, cols], grad_second[...]).astype(BF16)

    lanes = lane_masks()
    sides = side_masks(1)
    rows = span(s, WINDOW)
    for n in range(width // PAIR):
        cols = slice(n * PAIR, (n + 1) * PAIR)
        others = slice(width + n * PAIR, width + (n + 1) * PAIR)
        grad_q, grad_k, grad_v = attend_back(
            queries[:, cols], pairs[:, cols], pairs[:, others], probs[0, n], grad_low[rows, cols], lanes, sides
        )
        grad_queries[:, cols] = grad_q.astype(BF16)
        grad_pairs[:, cols] = grad_k.astype(BF16)
        grad_pairs[:, others] = grad_v.astype(BF16)


def conv_back_kernel(table, order, own, away, near, far, vecs, pairs, grad_pairs, *refs):
    stacks = refs[:-6]
    total, tap_grads, edges, weights, rim, sem = refs[-6:]
    width = pairs.shape[1] // 2
    seqs = pairs.shape[0] // WIDE
    pools = WINDOW // STRIDE
    copies = fetch_all(order, stacks, table, 3 * width // 2, weights, sem)
    matrix = tap_matrix(pools)
    back = tap_matrix_back(pools)
    tap_grads[...] = jnp.zeros_like(tap_grads)

    @pl.loop(0, seqs)
    def _(s):
        for n in range(2 * width // TILE):
            cols = slice(n * TILE, (n + 1) * TILE)
            kind, start = divmod(n * TILE, width)
            taps = [vecs[tap_row(t, kind) : tap_row(t, kind) + 1, start : start + TILE] for t in range(KERNEL)]
            part = span(s, pools)
            grad = own[part, cols].astype(F32) + away[part, cols].astype(F32)
            grad = grad + near[part, cols].astype(F32) + far[part, cols].astype(F32)
            grad = grad.astype(BF16).astype(F32)
            spread = [(taps[t] * grad).astype(BF16) for t in range(KERNEL)]
            whole = grad_pairs[span(s, WIDE), cols].astype(F32) + product(back, jnp.concatenate(spread, axis=0))
            total[span(s, WIDE), cols] = whole.astype(BF16)
            slab = product(matrix, pairs[span(s, WIDE), cols])
            for t in range(KERNEL):
                row = 2 * t + kind
                tap_grads[row : row + 1, start : start + TILE] += jnp.sum(
                    grad * slab[t * pools : (t + 1) * pools], axis=0, keepdims=True
                )

    for s in range(seqs):
        rim[s * HALF : (s + 1) * HALF, :] = total[s * WIDE : s * WIDE + HALF, :]
        rim[(seqs + s) * HALF : (seqs + s + 1) * HALF, :] = total[s * WIDE + HALF + WINDOW : (s + 1) * WIDE, :]
    settle(copies)

    @pl.loop(0, width // TILE)
    def _(n):
        cols = span(n, TILE)
        edges[:, cols] = product_back(rim[...], weights[cols, width:]).astype(BF16)


def query_grad_kernel(order, tok, grad_queries, grad_pooled, grad_out, keep, give, tok_t, total, sem):
    width = tok.shape[1]
    block = width // SLOTS
    targets = (keep, give)
    copies = emit(order, grad_pooled, pl.ds(0, width), block, targets, 3 * width, sem)
    copies += emit(order, grad_out, pl.ds(0, width), block, targets, 4 * width, sem)
    tok_t[...] = tok[...].T

    @pl.loop(0, width // TILE)
    def _(n):
        cols = span(n, TILE)
        total[:, cols] = product(tok_t[...], grad_queries[:, cols]).astype(BF16)

    copies += emit(order, total, pl.ds(0, width), block, targets, 0, sem)
    settle(copies)


def weight_grad_kernel(order, tok, low, high, grad_pairs, tap_grads, *refs):
    keep, give, xext_t, total, narrow, sem = refs[2:]
    width = tok.shape[1]
    block = width // SLOTS
    targets = (keep, give)
    taps = jnp.concatenate([tap_grads[...], jnp.zeros((112, width), F32)], axis=0).T
    narrow[...] = taps.astype(BF16)
    copies = emit(order, narrow, pl.ds(0, 128), block, targets, 5 * width, sem)
    for s in range(low.shape[0] // HALF):
        parts = (
            low[s * HALF : (s + 1) * HALF, :],
            tok[s * WINDOW : (s + 1) * WINDOW, :],
            high[s * HALF : (s + 1) * HALF, :],
        )
        xext_t[:, s * WIDE : (s + 1) * WIDE] = jnp.concatenate(parts, axis=0).T

    @pl.loop(0, 2 * width // TILE)
    def _(n):
        cols = span(n, TILE)
        total[:, cols] = product(xext_t[...], grad_pairs[:, cols]).astype(BF16)

    copies += emit(order, total, pl.ds(0, 2 * width), block, targets, width, sem)
    settle(copies)


def token_grad_kernel(table, order, grad_resid, grad_queries, grad_pairs, low, high, *refs):
    stacks = refs[:-4]
    out, weights, own, sem = refs[-4:]
    width = grad_resid.shape[1]
    seqs = grad_resid.shape[0] // WINDOW
    copies = fetch_all(order, stacks, table, 3 * width // 2, weights, sem)
    for s in range(seqs):
        own[s * WINDOW : (s + 1) * WINDOW, :width] = grad_queries[s * WINDOW : (s + 1) * WINDOW, :]
        own[s * WINDOW : (s + 1) * WINDOW, width:] = grad_pairs[s * WIDE + HALF : s * WIDE + HALF + WINDOW, :]
    settle(copies)

    @pl.loop(0, width // TILE)
    def _(n):
        cols = span(n, TILE)
        out[:, cols] = grad_resid[:, cols] + product_back(own[...], weights[cols, :])
        for s in range(seqs):
            part = slice(s * HALF, (s + 1) * HALF)
            out[s * WINDOW : s * WINDOW + HALF, cols] += low[part, cols].astype(F32)
            out[s * WINDOW + HALF : (s + 1) * WINDOW, cols] += high[part, cols].astype(F32)


def shape_of(*dims, dtype=BF16):
    return jax.ShapeDtypeStruct(dims, dtype)


def turn(block, step):
    return lax.ppermute(block, "shard", [(i, (i - 4 * step) % SLOTS) for i in range(SLOTS)])


def flip(block):
    return lax.ppermute(block, "shard", [(i, i ^ 2) for i in range(SLOTS)])


def other(block):
    return lax.ppermute(block, "rep", [(0, 1), (1, 0)])


def gate_kernel(*refs):
    del refs


def after(value, *others):
    if not direct() or not others:
        return value
    return pl.pallas_call(
        gate_kernel,
        out_shape=jax.ShapeDtypeStruct(value.shape, value.dtype),
        in_specs=[any_spec()] * (1 + len(others)),
        out_specs=any_spec(),
        input_output_aliases={0: 0},
        compiler_params=params(2),
        cost_estimate=cost(0),
        name="gate",
    )(value, *others)


def direct():
    return lax.axis_size("shard") == SLOTS and lax.axis_size("rep") == 2


def block_order():
    if not direct():
        return jnp.arange(SLOTS + 1, dtype=jnp.int32) % SLOTS
    me = lax.axis_index("shard")
    k = jnp.arange(SLOTS, dtype=jnp.int32)
    places = ((me // 4 + k // 4) % 4) * 4 + jnp.bitwise_xor(me % 4, k % 4)
    return jnp.concatenate([places, lax.axis_index("rep")[None]]).astype(jnp.int32)


class Gather:
    def __init__(self, block):
        self.block = block

    def turn(self, *gate):
        own = after(self.block, *gate)
        self.along = jnp.stack([own] + [turn(own, step) for step in (1, 2, 3)])

    def cross(self, *gate):
        self.along = after(self.along, *gate)
        self.across = flip(self.along)

    def rep(self, *gate):
        self.across = after(self.across, *gate)
        self.first = jnp.concatenate([self.along, self.across], axis=0)
        self.second = other(self.first)

    def cores(self, *gate):
        stacks = [self.first, after(self.second, *gate)]
        stacks = stacks + [swap(stack) for stack in stacks]
        table = []
        for k in range(SLOTS):
            part = k // 2 % 2 * 4 + k // 4
            table.append(((2 * (k % 2), part, 0), (2 * (k % 2) + 1, part, 0)))
        return stacks, tuple(table)


def plain_gather(block, extra=None):
    rows, width = block.shape
    half = width // 2
    rows = rows * lax.axis_size("shard") // SLOTS
    mine, rest = block[:, :half], block[:, half:]
    both = jnp.concatenate([mine] + ([] if extra is None else [extra]) + [rest], axis=1)
    full = lax.all_gather(both, "shard", axis=0, tiled=True)
    table = tuple(((0, k, 0), (0, k, both.shape[1] - half)) for k in range(SLOTS))
    return [full.reshape(SLOTS, rows, both.shape[1])], table


def pack_kernel(order, query, key, value, pooled, out, inner, outer, tokens, taps, *refs):
    vectors, bias = refs[:6], refs[6]
    lead, bulk, low, high, joined, small = refs[7:]
    part, width = query.shape
    half = 3 * width // 2
    for k, source in enumerate((query, key, value)):
        joined[:, k * width : (k + 1) * width] = source[...]
    mine = order[SLOTS]
    small[...] = jnp.zeros_like(small)
    for k, source in enumerate(vectors):
        small[k : k + 1, :part] = source[...].astype(F32)
    for t in range(KERNEL):
        small[tap_row(t, 0) : tap_row(t, 0) + 2, :part] = taps[t].astype(F32)
    small[BIAS_ROW:SMALL, :part] = bias[...].astype(F32)
    lead[:, :half] = joined[:, span(mine, half)]
    lead[:, half:] = small[...].T[:part].astype(BF16)
    bulk[:part, :] = pooled[...]
    bulk[part : 2 * part, :] = out[...]
    folds = inner.shape[1] // width
    for m in range(folds):
        bulk[(2 + m) * part : (3 + m) * part, :] = inner[:, m * width : (m + 1) * width]
    bulk[(2 + folds) * part :, :] = outer[...]
    high[...] = tokens[:, :HALF, :]
    low[...] = tokens[:, tokens.shape[1] - HALF :, :]


def split_kernel(wide, order, keep, arrived, a_keep, a_send, b_keep, b_send):
    half = wide // 2
    mine = span(order[SLOTS], half)
    rest = span(1 - order[SLOTS], half)
    for across in range(2):
        a_keep[across, 0] = keep[across, 0, :, mine] + arrived[across, 0, :, mine]
        a_send[across, 0] = keep[across, 0, :, rest] + arrived[across, 0, :, rest]
        target = b_send if across else b_keep
        target[0] = keep[across, 0, :, wide:] + arrived[across, 0, :, wide:]


def fold_kernel(keep, arrived, x_keep, x_send):
    x_keep[0] = keep[0, 0] + arrived[0, 0]
    x_send[0] = keep[1, 0] + arrived[1, 0]


def join_kernel(x_keep, x_arrived, b_keep, b_arrived, *parts):
    half = x_keep.shape[2]
    for k, part in enumerate(parts):
        part[:, :half] = x_keep[k] + x_arrived[k]
        part[:, half:] = b_keep[k] + b_arrived[k]


def gather_sum_kernel(own, first, second, third, out):
    total = own[...].astype(F32) + first[...].astype(F32) + second[...].astype(F32) + third[...].astype(F32)
    out[...] = total.astype(BF16)


def final_kernel(wide, pieces, order, own, arrived, *refs):
    outs, total = refs[:-1], refs[-1]
    half = wide // 2
    total[:, span(order[SLOTS], half)] = own[:, :half].astype(F32)
    total[:, span(1 - order[SLOTS], half)] = arrived[:, :half].astype(F32)
    total[:, wide:] = own[:, half:].astype(F32) + arrived[:, half:].astype(F32)
    for (start, size), out in zip(pieces, outs):
        out[...] = total[:, start : start + size]


class Scatter:
    def __init__(self, keep, give, order, wide, pieces):
        self.order, self.wide, self.pieces = order, wide, pieces
        self.rows, self.columns = keep.shape[2:]
        self.keep, self.give = keep, give
        if direct():
            self.arrived = swap(give)

    def split(self):
        rows, half, rest = self.rows, self.wide // 2, self.columns - self.wide
        four = pl.BlockSpec((2, 1, rows, self.columns), lambda z: (0, z, 0, 0))
        a_block = pl.BlockSpec((2, 1, rows, half), lambda z: (0, z, 0, 0))
        b_block = pl.BlockSpec((1, rows, rest), lambda z: (z, 0, 0))
        a_shape, b_shape = shape_of(2, 4, rows, half), shape_of(4, rows, rest)
        self.a_keep, a_send, self.b_keep, b_send = pl.pallas_call(
            functools.partial(split_kernel, self.wide),
            grid=(4,),
            out_shape=(a_shape, a_shape, b_shape, b_shape),
            in_specs=[smem_spec(), four, four],
            out_specs=(a_block, a_block, b_block, b_block),
            compiler_params=params(14),
            cost_estimate=cost(5),
            name="split",
        )(self.order, self.keep, self.arrived)
        self.a_arrived = other(a_send)
        self.b_arrived = flip(b_send)
        return a_send

    def fold(self):
        rows, half = self.rows, self.wide // 2
        a_block = pl.BlockSpec((2, 1, rows, half), lambda z: (0, z, 0, 0))
        x_block = pl.BlockSpec((1, rows, half), lambda z: (z, 0, 0))
        x_shape = shape_of(4, rows, half)
        self.x_keep, x_send = pl.pallas_call(
            fold_kernel,
            grid=(4,),
            out_shape=(x_shape, x_shape),
            in_specs=[a_block, a_block],
            out_specs=(x_block, x_block),
            compiler_params=params(10),
            cost_estimate=cost(4),
            name="fold",
        )(self.a_keep, self.a_arrived)
        self.x_arrived = flip(x_send)
        return x_send

    def join(self):
        shape = shape_of(self.rows, self.columns - self.wide // 2)
        parts = pl.pallas_call(
            join_kernel,
            out_shape=(shape,) * 4,
            in_specs=[vmem_spec()] * 4,
            out_specs=(vmem_spec(),) * 4,
            compiler_params=params(14),
            cost_estimate=cost(3),
            name="join",
        )(self.x_keep, self.x_arrived, self.b_keep, self.b_arrived)
        self.turned = [parts[0]] + [turn(parts[step], -step) for step in (1, 2, 3)]
        return parts[1]

    def gather(self):
        self.own = pl.pallas_call(
            gather_sum_kernel,
            out_shape=shape_of(self.rows, self.columns - self.wide // 2),
            in_specs=[vmem_spec()] * 4,
            out_specs=vmem_spec(),
            compiler_params=params(10),
            cost_estimate=cost(2),
            name="gather_sum",
        )(*self.turned)
        self.last = other(self.own)
        return self.own

    def final(self):
        return pl.pallas_call(
            functools.partial(final_kernel, self.wide, self.pieces),
            out_shape=tuple(shape_of(self.rows, size, dtype=F32) for _, size in self.pieces),
            in_specs=[smem_spec(), vmem_spec(), vmem_spec()],
            out_specs=(vmem_spec(),) * len(self.pieces),
            scratch_shapes=[pltpu.VMEM((self.rows, self.columns), F32)],
            compiler_params=params(12),
            cost_estimate=cost(2),
            name="final",
        )(self.order, self.own, self.last)


def bulk_final_kernel(own, arrived, inner, outer, small):
    part, hidden = inner.shape
    width = own.shape[1]
    total = own[...].astype(F32) + arrived[...].astype(F32)
    folds = hidden // width
    for m in range(folds):
        inner[:, m * width : (m + 1) * width] = total[m * part : (m + 1) * part]
    outer[...] = total[folds * part : 2 * folds * part]
    small[...] = total[2 * folds * part :]


def plain_total(whole):
    return rep_total(lax.psum_scatter(whole, "shard", scatter_dimension=0, tiled=True))


def plain_scatter(blocks, parts):
    keep, give = blocks
    full = jnp.stack([keep, give]).transpose(2, 1, 0, 3, 4).reshape(SLOTS, keep.shape[2], keep.shape[3])
    width = SLOTS * keep.shape[2]
    return [plain_total(full[:, :, start:stop].reshape(width, -1)) for start, stop in parts]


def rep_total(piece):
    count = lax.axis_size("rep")
    total = piece.astype(F32)
    for step in range(1, count):
        route = [(i, (i + step) % count) for i in range(count)]
        total = total + lax.ppermute(piece, "rep", route).astype(F32)
    return total


def shift(block, distance):
    count = lax.axis_size("shard")
    return lax.ppermute(
        block, "shard", [(i, i + distance) for i in range(count) if 0 <= i + distance < count]
    )


def swap(block):
    return lax.ppermute(block, "shard", [(i, i ^ 1) for i in range(lax.axis_size("shard"))])


def hop(block, outer):
    count = lax.axis_size("shard")
    route = [(i, i + (2 if (i % 2 == 0) == outer else -2)) for i in range(count)]
    return lax.ppermute(block, "shard", [(i, j) for i, j in route if 0 <= j < count])


def shards(
    tokens,
    query_proj,
    key_proj,
    value_proj,
    pooled_query,
    output_proj,
    conv_taps,
    output_bias,
    first_gain,
    first_shift,
    inner_proj,
    inner_bias,
    outer_proj,
    outer_bias,
    second_gain,
    second_shift,
    block_ids,
    cotangent,
):
    seqs, tok_span, width = tokens.shape
    rows = seqs * tok_span
    hidden = inner_proj.shape[1]
    device_count = lax.axis_size("shard")
    device_index = lax.axis_index("shard")
    seq_length = tok_span * device_count
    pools = tok_span // STRIDE
    pool_reach = POOL_SPAN // (2 * STRIDE)
    n_pair = width // PAIR
    core = lax.rem(device_index, 2)

    tok = tokens.reshape(rows, width)
    cot = cotangent.reshape(rows, width)
    vectors = [output_bias, first_gain, first_shift, outer_bias, second_gain, second_shift]
    part = width // device_count
    block = width // SLOTS
    order = block_order()
    if direct():
        packed = pl.pallas_call(
            pack_kernel,
            out_shape=(
                shape_of(part, 3 * width // 2 + 128),
                shape_of(bulk_rows(width, hidden), width),
                shape_of(seqs, HALF, width),
                shape_of(seqs, HALF, width),
            ),
            in_specs=[smem_spec()] + [vmem_spec()] * 16,
            out_specs=(vmem_spec(),) * 4,
            scratch_shapes=[pltpu.VMEM((part, 3 * width), BF16), pltpu.VMEM((128, 128), F32)],
            compiler_params=params(),
            cost_estimate=cost(3),
            name="pack",
        )(
            order,
            query_proj,
            key_proj,
            value_proj,
            pooled_query,
            output_proj,
            inner_proj,
            outer_proj,
            tokens,
            conv_taps,
            *[vector.reshape(1, part) for vector in vectors],
            inner_bias.reshape(4, part),
        )
        lead = Gather(packed[0])
        bulk = lax.all_gather(packed[1], "shard", axis=0, tiled=True)
        lead.turn()
        lead.cross()
        tick = after(jnp.zeros((8, 128), F32), lead.across)
        lead.rep()
        tok_low = shift(after(packed[2], tick), 1).reshape(seqs * HALF, width)
        tok_high = shift(after(packed[3], tick), -1).reshape(seqs * HALF, width)
        lead, lead_table = lead.cores(tok_low, tok_high)
    else:
        tok_low = shift(tokens[:, tok_span - HALF :], 1).reshape(seqs * HALF, width)
        tok_high = shift(tokens[:, :HALF], -1).reshape(seqs * HALF, width)
        small = jnp.concatenate(vectors + [conv_taps.reshape(-1), inner_bias]).reshape(SMALL, part).T
        small = jnp.pad(small, ((0, 0), (0, 128 - SMALL)))
        lead, lead_table = plain_gather(jnp.concatenate([query_proj, key_proj, value_proj], axis=1), small)
        square = [
            lax.all_gather(block_rows, "shard", axis=0, tiled=True).reshape(SLOTS, block, width)
            for block_rows in (pooled_query, output_proj)
        ]
        full = lax.all_gather(inner_proj, "shard", axis=0, tiled=True)
        full = full.reshape(SLOTS, block, hidden // width, width).transpose(0, 2, 1, 3)
        full = full.reshape(SLOTS, hidden // SLOTS, width)
        down = lax.all_gather(outer_proj, "shard", axis=0, tiled=True)
        down = down.reshape(SLOTS, hidden // SLOTS, width)
        bulk = jnp.concatenate(square + [full, down], axis=1).reshape(-1, width)

    query = jnp.arange(tok_span, dtype=jnp.int32)[None, :]
    slot = jnp.arange(WINDOW, dtype=jnp.int32)[:, None]
    query_ids = lax.dynamic_slice_in_dim(block_ids, device_index * tok_span, tok_span, 1)[:, None, :]

    def bias_for(ids, start, length, step, reach):
        ids = lax.dynamic_slice_in_dim(jnp.pad(ids, ((0, 0), (reach, reach + WINDOW))), start, WIDE, 1)
        near = slot >= query // step
        place = start - reach + jnp.where(near, slot, slot + WINDOW)
        key_ids = jnp.where(near[None], ids[:, :WINDOW, None], ids[:, WINDOW:, None])
        allowed = ((place >= 0) & (place < length))[None] & (key_ids <= query_ids)
        return jnp.where(allowed, 0.0, neg_fill)

    bias_one = bias_for(block_ids, device_index * tok_span, seq_length, 1, HALF)
    bias_two = bias_for(
        block_ids[:, ::STRIDE], device_index * pools, seq_length // STRIDE, STRIDE, pool_reach
    )

    n_lead = len(lead)
    queries, pairs, pooled, vecs = pl.pallas_call(
        functools.partial(project_kernel, lead_table),
        out_shape=(
            shape_of(rows, width),
            shape_of(seqs * WIDE, 2 * width),
            shape_of(seqs * pools, 2 * width),
            shape_of(24, width, dtype=F32),
        ),
        in_specs=[smem_spec()] + [vmem_spec()] * 3 + [hbm_spec()] * n_lead,
        out_specs=(vmem_spec(),) * 4,
        scratch_shapes=[
            pltpu.VMEM((seqs * WIDE, width), BF16),
            pltpu.VMEM((width, 3 * width), BF16),
            pltpu.VMEM((width, 128), BF16),
            pltpu.SemaphoreType.DMA,
        ],
        compiler_params=params(54),
        cost_estimate=cost(15),
        name="project",
    )(order, tok, tok_low, tok_high, *lead)
    bias_in = vecs[BIAS_ROW:SMALL].reshape(4, device_count, part).transpose(1, 0, 2).reshape(1, hidden)

    pool_away = swap(pooled)
    pool_far = hop(pooled, True)
    pool_near = hop(pooled, False)
    places = jnp.where(
        core == 0, jnp.array([2, 3, 1, 4, 0], jnp.int32), jnp.array([2, 1, 3, 0, 4], jnp.int32)
    )

    seq_block = lambda r, c: pl.BlockSpec((r, c), lambda s: (s, 0))
    whole_block = lambda r, c: pl.BlockSpec((r, c), lambda s: (0, 0))
    bias_block = pl.BlockSpec((1, WINDOW, tok_span), lambda s: (s, 0, 0))
    prob_block = pl.BlockSpec((1, n_pair, WINDOW, 2 * tok_span), lambda s: (s, 0, 0, 0))
    prob_shape = shape_of(seqs, n_pair, WINDOW, 2 * tok_span)

    attended, probs_one = pl.pallas_call(
        window_kernel,
        grid=(seqs,),
        out_shape=(shape_of(rows, width), prob_shape),
        in_specs=[seq_block(tok_span, width), seq_block(WIDE, 2 * width), bias_block],
        out_specs=(seq_block(tok_span, width), prob_block),
        compiler_params=params(12),
        cost_estimate=cost(10),
        name="window",
    )(queries, pairs, bias_one)

    pool_near = after(pool_near, attended)
    pool_blocks = (pooled, pool_away, swap(pool_near), pool_near, pool_far)
    pool_specs = [seq_block(pools, 2 * width)] * 5
    second, mixed, probs_two, pooled_weights = pl.pallas_call(
        pooled_kernel,
        grid=(seqs,),
        out_shape=(shape_of(rows, width), shape_of(rows, width), prob_shape, shape_of(width, width)),
        in_specs=[smem_spec(), whole_block(rows, width), bias_block, hbm_spec()] + pool_specs,
        out_specs=(
            whole_block(rows, width),
            seq_block(tok_span, width),
            prob_block,
            whole_block(width, width),
        ),
        scratch_shapes=[pltpu.VMEM((WIDE, 2 * width), BF16), pltpu.SemaphoreType.DMA],
        compiler_params=params(54),
        cost_estimate=cost(14),
        name="pooled",
    )(places, attended, bias_two, bulk, *pool_blocks)

    each = 2 * hidden // SLOTS + SMALL_ROWS
    result, grad_resid, grad_attn, grad_bulk, out_weights, _ = pl.pallas_call(
        feed_kernel,
        out_shape=(
            shape_of(rows, width),
            shape_of(rows, width, dtype=F32),
            shape_of(rows, width),
            shape_of(SLOTS * each, width),
            shape_of(width, width),
            shape_of(8, width, dtype=F32),
        ),
        in_specs=[vmem_spec()] * 5 + [hbm_spec()],
        out_specs=(vmem_spec(),) * 3 + (any_spec(), vmem_spec(), vmem_spec()),
        scratch_shapes=[
            pltpu.VMEM((width, hidden), BF16),
            pltpu.VMEM((hidden, width), BF16),
            pltpu.VMEM((rows, width), F32),
            pltpu.VMEM((rows, 128), F32),
            pltpu.VMEM((rows, width), BF16),
            pltpu.VMEM((width, rows), BF16),
            pltpu.VMEM((rows, hidden), BF16),
            pltpu.VMEM((rows, hidden), BF16),
            pltpu.VMEM((rows, width), F32),
            pltpu.VMEM((rows, width), BF16),
            pltpu.VMEM((width, hidden), BF16),
            pltpu.VMEM((hidden, width), BF16),
            pltpu.VMEM((1, hidden), F32),
            pltpu.VMEM((SLOTS, SMALL_ROWS, width), BF16),
            pltpu.SemaphoreType.DMA((4,)),
        ],
        compiler_params=params(58),
        cost_estimate=cost(45),
        name="feed",
    )(tok, mixed, cot, vecs, bias_in, bulk)
    if direct():
        own_bulk = lax.psum_scatter(grad_bulk, "shard", scatter_dimension=0, tiled=True)

    back_shape = shape_of(seqs * pools, 2 * width)
    grad_mixed, grad_second, grad_out, pg_own, pg_away, pg_near, pg_far = pl.pallas_call(
        pooled_back_kernel,
        grid=(seqs,),
        out_shape=(
            shape_of(rows, width, dtype=F32),
            shape_of(rows, width),
            shape_of(width, width),
            back_shape,
            shape_of(2, seqs * pools, 2 * width),
            back_shape,
            back_shape,
        ),
        in_specs=[
            smem_spec(),
            whole_block(rows, width),
            whole_block(rows, width),
            seq_block(tok_span, width),
            prob_block,
            whole_block(width, width),
        ]
        + pool_specs,
        out_specs=(
            whole_block(rows, width),
            seq_block(tok_span, width),
            whole_block(width, width),
            seq_block(pools, 2 * width),
            pl.BlockSpec((2, pools, 2 * width), lambda s: (0, s, 0)),
            seq_block(pools, 2 * width),
            seq_block(pools, 2 * width),
        ),
        scratch_shapes=[
            pltpu.VMEM((WIDE, 2 * width), BF16),
            pltpu.VMEM((WIDE, 2 * width), F32),
            pltpu.VMEM((rows, width), BF16),
        ],
        compiler_params=params(24),
        cost_estimate=cost(22),
        name="pooled_back",
    )(places, grad_attn, mixed, second, probs_two, out_weights, *pool_blocks)

    pg_cross = swap(pg_away)
    pg_near = (pg_near.astype(F32) + pg_cross[1].astype(F32)).astype(BF16)
    back_near = lax.ppermute(pg_near, "shard", back_route(device_count, False))
    back_far = lax.ppermute(pg_far, "shard", back_route(device_count, True))
    grad_second = after(grad_second, pg_near)

    grad_queries, grad_pairs, grad_pooled = pl.pallas_call(
        window_back_kernel,
        grid=(seqs,),
        out_shape=(shape_of(rows, width), shape_of(seqs * WIDE, 2 * width), shape_of(width, width)),
        in_specs=[
            whole_block(rows, width),
            whole_block(rows, width),
            whole_block(rows, width),
            seq_block(tok_span, width),
            seq_block(WIDE, 2 * width),
            prob_block,
            whole_block(width, width),
        ],
        out_specs=(seq_block(tok_span, width), seq_block(WIDE, 2 * width), whole_block(width, width)),
        scratch_shapes=[pltpu.VMEM((rows, width), BF16)],
        compiler_params=params(24),
        cost_estimate=cost(22),
        name="window_back",
    )(grad_mixed, grad_second, attended, queries, pairs, probs_one, pooled_weights)

    lead_shape = shape_of(2, 4, block, 5 * width + 128)
    lead_keep, lead_give = pl.pallas_call(
        query_grad_kernel,
        out_shape=(lead_shape, lead_shape),
        in_specs=[smem_spec()] + [vmem_spec()] * 4,
        out_specs=(any_spec(),) * 2,
        scratch_shapes=[
            pltpu.VMEM((width, rows), BF16),
            pltpu.VMEM((width, width), BF16),
            pltpu.SemaphoreType.DMA,
        ],
        compiler_params=params(16),
        cost_estimate=cost(5),
        name="query_grad",
    )(order, tok, grad_queries, grad_pooled, grad_out)
    vecs = after(vecs, lead_keep)

    pair_total, tap_grads, edges = pl.pallas_call(
        functools.partial(conv_back_kernel, lead_table),
        out_shape=(
            shape_of(seqs * WIDE, 2 * width),
            shape_of(16, width, dtype=F32),
            shape_of(2 * seqs * HALF, width),
        ),
        in_specs=[smem_spec()] + [vmem_spec()] * 7 + [hbm_spec()] * n_lead,
        out_specs=(vmem_spec(),) * 3,
        scratch_shapes=[
            pltpu.VMEM((width, 3 * width), BF16),
            pltpu.VMEM((2 * seqs * HALF, 2 * width), BF16),
            pltpu.SemaphoreType.DMA,
        ],
        compiler_params=params(34),
        cost_estimate=cost(12),
        name="conv_back",
    )(order, pg_own, pg_cross[0], back_near, back_far, vecs, pairs, grad_pairs, *lead)

    edge_high = shift(edges[: seqs * HALF], -1)
    edge_low = shift(edges[seqs * HALF :], 1)

    lead_keep, lead_give = pl.pallas_call(
        weight_grad_kernel,
        out_shape=(lead_shape, lead_shape),
        in_specs=[smem_spec()] + [vmem_spec()] * 5 + [any_spec()] * 2,
        out_specs=(any_spec(),) * 2,
        input_output_aliases={6: 0, 7: 1},
        scratch_shapes=[
            pltpu.VMEM((width, seqs * WIDE), BF16),
            pltpu.VMEM((width, 2 * width), BF16),
            pltpu.VMEM((width, 128), BF16),
            pltpu.SemaphoreType.DMA,
        ],
        compiler_params=params(32),
        cost_estimate=cost(10),
        name="weight_grad",
    )(order, tok, tok_low, tok_high, pair_total, tap_grads, lead_keep, lead_give)
    lead_give = after(lead_give, edge_low, edge_high)
    pieces = tuple((k * width, width) for k in range(5)) + ((5 * width, 128),)
    lead_sum = Scatter(lead_keep, lead_give, order, 14 * 128, pieces)
    if direct():
        lead_sum.split()
        edge_low = after(edge_low, lead_sum.b_keep)

    tokens_grad = pl.pallas_call(
        functools.partial(token_grad_kernel, lead_table),
        out_shape=shape_of(rows, width, dtype=F32),
        in_specs=[smem_spec()] + [vmem_spec()] * 5 + [hbm_spec()] * n_lead,
        out_specs=vmem_spec(),
        scratch_shapes=[
            pltpu.VMEM((width, 3 * width), BF16),
            pltpu.VMEM((rows, 3 * width), BF16),
            pltpu.SemaphoreType.DMA,
        ],
        compiler_params=params(30),
        cost_estimate=cost(11),
        name="token_grad",
    )(order, grad_resid, grad_queries, pair_total, edge_low, edge_high, *lead)

    folds = hidden // width
    if direct():
        lead_sum.a_keep = after(lead_sum.a_keep, tokens_grad)
        lead_sum.fold()
        lead_sum.join()
        lead_sum.gather()
        own_in, own_down, small_own = pl.pallas_call(
            bulk_final_kernel,
            out_shape=(
                shape_of(part, hidden, dtype=F32),
                shape_of(folds * part, width, dtype=F32),
                shape_of(SMALL_ROWS, width, dtype=F32),
            ),
            in_specs=[vmem_spec()] * 2,
            out_specs=(vmem_spec(),) * 3,
            compiler_params=params(10),
            cost_estimate=cost(2),
            name="bulk_final",
        )(own_bulk, other(own_bulk))
        vec_own = [small_own[k, :part] for k in range(6)]
        bias_own = small_own[8, : folds * part]
        own_query, own_keys, own_values, own_pooled, own_out, taps_own = lead_sum.final()
    else:
        whole = grad_bulk.reshape(SLOTS, each, width)
        inner_part = whole[:, : folds * block].reshape(SLOTS, folds, block, width).transpose(0, 2, 1, 3)
        own_in = plain_total(inner_part.reshape(width, hidden))
        own_down = plain_total(whole[:, folds * block : 2 * folds * block].reshape(hidden, width))
        small = whole[:, 2 * folds * block :]
        vec_own = [plain_total(small[:, k, :block].reshape(width)) for k in range(6)]
        bias_own = plain_total(small[:, 8, : folds * block].reshape(hidden))
        parts = [(k * width, (k + 1) * width) for k in range(5)] + [(5 * width, None)]
        own_query, own_keys, own_values, own_pooled, own_out, taps_own = plain_scatter(
            (lead_keep, lead_give), parts
        )
    taps_own = taps_own.T[: 2 * KERNEL].reshape(KERNEL, 2, part)
    return (
        result.reshape(tokens.shape),
        tokens_grad.reshape(tokens.shape),
        own_query,
        own_keys,
        own_values,
        own_pooled,
        own_out,
        taps_own,
        vec_own[0],
        vec_own[1],
        vec_own[2],
        own_in,
        bias_own,
        own_down,
        vec_own[3],
        vec_own[4],
        vec_own[5],
    )


def back_route(count, outer):
    route = [(i, i + (2 if (i % 2 == 0) == outer else -2)) for i in range(count)]
    return [(j, i) for i, j in route if 0 <= j < count]


def solution(mesh):
    in_specs = (
        P("rep", "shard", None),
        P("shard", None),
        P("shard", None),
        P("shard", None),
        P("shard", None),
        P("shard", None),
        P(None, None, "shard"),
        P("shard"),
        P("shard"),
        P("shard"),
        P("shard", None),
        P("shard"),
        P("shard", None),
        P("shard"),
        P("shard"),
        P("shard"),
        P("rep", None),
        P("rep", "shard", None),
    )
    out_specs = (
        P("rep", "shard", None),
        P("rep", "shard", None),
        P("shard", None),
        P("shard", None),
        P("shard", None),
        P("shard", None),
        P("shard", None),
        P(None, None, "shard"),
        P("shard"),
        P("shard"),
        P("shard"),
        P("shard", None),
        P("shard"),
        P("shard", None),
        P("shard"),
        P("shard"),
        P("shard"),
    )
    return jax.shard_map(shards, mesh=mesh, in_specs=in_specs, out_specs=out_specs, check_vma=False)
```

```python
import functools

import jax
import jax.numpy as jnp
from jax import lax
from jax.experimental import pallas as pl
from jax.experimental.pallas import tpu as pltpu
from jax.sharding import PartitionSpec as P

HEAD_DIM = 64
WINDOW = 128
POOL_SPAN = 512
STRIDE = 4
KERNEL = 5

neg_fill = -1e30
norm_eps = 1e-05
F32 = jnp.float32
BF16 = jnp.bfloat16
ROOT_HALF = 0.7071067811865476
ROOT_TWO_PI = 0.3989422804014327

HALF = WINDOW // 2
WIDE = 2 * WINDOW
PAIR = 2 * HEAD_DIM
TILE = 256
SLOTS = 16
VMEM_LIMIT = 58
SCALE = 0.05


def product(former, latter):
    return jnp.dot(former, latter, preferred_element_type=F32)


def product_back(former, latter):
    return lax.dot_general(former, latter, (((1,), (1,)), ((), ())), preferred_element_type=F32)


def outer_sum(former, latter):
    return lax.dot_general(former, latter, (((0,), (0,)), ((), ())), preferred_element_type=F32)


def span(index, size):
    return pl.ds(pl.multiple_of(index * size, size), size)


def any_spec():
    return pl.BlockSpec(memory_space=pl.ANY)


def hbm_spec():
    return pl.BlockSpec(memory_space=pltpu.HBM)


def vmem_spec():
    return pl.BlockSpec(memory_space=pltpu.VMEM)


def smem_spec():
    return pl.BlockSpec(memory_space=pltpu.SMEM)


def params(mebibytes=VMEM_LIMIT):
    return pltpu.CompilerParams(vmem_limit_bytes=mebibytes * 1024 * 1024)


def cost(microseconds):
    return pl.CostEstimate(
        flops=int(microseconds * 1.1e9 * SCALE), bytes_accessed=int(microseconds * 3.5e6 * SCALE), transcendentals=0
    )


def fetch(order, stacks, table, half, columns, target, sem):
    rows = stacks[0].shape[1]
    pairs = []
    for k, places in enumerate(table):
        goal = target.at[span(order[k], rows), :]
        pairs.append(
            [
                pltpu.make_async_copy(
                    stacks[stack].at[part, :, pl.ds(start + columns[0], columns[1])], goal, sem
                )
                for stack, part, start in places
            ]
        )

    @pl.when(order[SLOTS] == half)
    def _():
        for pair in pairs:
            pair[0].start()

    @pl.when(order[SLOTS] != half)
    def _():
        for pair in pairs:
            pair[1].start()

    return [pair[0] for pair in pairs]


def fetch_all(order, stacks, table, half_width, target, sem):
    copies = []
    for half in range(2):
        view = target.at[:, pl.ds(half * half_width, half_width)]
        copies = copies + fetch(order, stacks, table, half, (0, half_width), view, sem)
    return copies


def bulk_rows(width, hidden):
    return (2 * width + 2 * hidden) // SLOTS


def fetch_square(bulk, which, target, sem):
    width = bulk.shape[1]
    block = width // SLOTS
    each = bulk.shape[0] // SLOTS
    copies = []
    for j in range(SLOTS):
        source = bulk.at[pl.ds(j * each + which * block, block), :]
        copies.append(pltpu.make_async_copy(source, target.at[pl.ds(j * block, block), :], sem))
        copies[-1].start()
    return copies


def fetch_bulk(bulk, w_in, w_down, sems):
    width = bulk.shape[1]
    block = width // SLOTS
    each = bulk.shape[0] // SLOTS
    folds = w_in.shape[1] // width
    first, second = [], []
    for j in range(SLOTS):
        start = j * each + 2 * block
        for m in range(folds):
            source = bulk.at[pl.ds(start + m * block, block), :]
            target = w_in.at[pl.ds(j * block, block), pl.ds(m * width, width)]
            first.append(pltpu.make_async_copy(source, target, sems[0]))
        source = bulk.at[pl.ds(start + folds * block, folds * block), :]
        target = w_down.at[pl.ds(j * folds * block, folds * block), :]
        second.append(pltpu.make_async_copy(source, target, sems[1]))
    for copy in first + second:
        copy.start()
    return first, second


def settle(copies):
    for copy in copies:
        copy.wait()


def emit(order, source, columns, rows, targets, start, sem):
    copies = []
    for k in range(SLOTS):
        copies.append(
            pltpu.make_async_copy(
                source.at[span(order[k], rows), columns],
                targets[k % 2].at[k // 2 % 2, k // 4, :, pl.ds(start, columns.size)],
                sem,
            )
        )
    for copy in copies:
        copy.start()
    return copies


def tap_matrix(pools):
    rows = lax.broadcasted_iota(jnp.int32, (KERNEL * pools, WIDE), 0)
    cols = lax.broadcasted_iota(jnp.int32, (KERNEL * pools, WIDE), 1)
    tap = rows // pools
    wanted = HALF - KERNEL // 2 + STRIDE * (rows - tap * pools) + tap
    return jnp.where(cols == wanted, 1.0, 0.0).astype(BF16)


def tap_matrix_back(pools):
    rows = lax.broadcasted_iota(jnp.int32, (WIDE, KERNEL * pools), 0)
    cols = lax.broadcasted_iota(jnp.int32, (WIDE, KERNEL * pools), 1)
    tap = cols // pools
    wanted = HALF - KERNEL // 2 + STRIDE * (cols - tap * pools) + tap
    return jnp.where(rows == wanted, 1.0, 0.0).astype(BF16)


TAP_ROW = 6
BIAS_ROW = TAP_ROW + 2 * KERNEL
SMALL = BIAS_ROW + 4
SMALL_ROWS = 16


def tap_row(tap, kind):
    return TAP_ROW + 2 * tap + kind


def project_kernel(table, order, tok, low, high, *refs):
    queries, pairs, pooled, vecs, xext, weights, narrow, sem = refs[-8:]
    stacks = refs[:-8]
    width = tok.shape[1]
    copies = fetch_all(order, stacks, table, 3 * width // 2, weights, sem)
    rows = stacks[0].shape[1]
    for k, places in enumerate(table):
        stack, part, start = places[0]
        copies.append(
            pltpu.make_async_copy(
                stacks[stack].at[part, :, pl.ds(start + 3 * width // 2, 128)],
                narrow.at[span(order[k], rows), :],
                sem,
            )
        )
        copies[-1].start()
    seqs = low.shape[0] // HALF
    for s in range(seqs):
        xext[s * WIDE : s * WIDE + HALF, :] = low[s * HALF : (s + 1) * HALF, :]
        xext[s * WIDE + HALF : s * WIDE + HALF + WINDOW, :] = tok[s * WINDOW : (s + 1) * WINDOW, :]
        xext[s * WIDE + HALF + WINDOW : (s + 1) * WIDE, :] = high[s * HALF : (s + 1) * HALF, :]
    settle(copies)

    @pl.loop(0, 2 * width // TILE)
    def _(n):
        cols = span(n + width // TILE, TILE)
        pairs[:, span(n, TILE)] = product(xext[...], weights[:, cols]).astype(BF16)

    vecs[...] = narrow[...].astype(F32).T[: vecs.shape[0]]
    pools = WINDOW // STRIDE
    matrix = tap_matrix(pools)

    @pl.loop(0, seqs)
    def _(s):
        for n in range(2 * width // TILE):
            cols = slice(n * TILE, (n + 1) * TILE)
            kind, own = divmod(n * TILE, width)
            slab = product(matrix, pairs[span(s, WIDE), cols])
            total = 0.0
            for t in range(KERNEL):
                row = tap_row(t, kind)
                total = total + vecs[row : row + 1, own : own + TILE] * slab[t * pools : (t + 1) * pools]
            pooled[span(s, pools), cols] = total.astype(BF16)

    @pl.loop(0, width // TILE)
    def _(n):
        cols = span(n, TILE)
        queries[:, cols] = product(tok[...], weights[:, cols]).astype(BF16) * HEAD_DIM**-0.5


def lane_masks():
    lane = lax.broadcasted_iota(jnp.int32, (WINDOW, PAIR), 1)
    first = lane < HEAD_DIM
    return first, jnp.where(first, 1.0, 0.0).astype(BF16), jnp.where(first, 0.0, 1.0).astype(BF16)


def side_masks(step):
    slot = lax.broadcasted_iota(jnp.int32, (WINDOW, 2 * WINDOW), 0)
    query = lax.broadcasted_iota(jnp.int32, (WINDOW, 2 * WINDOW), 1)
    near = slot >= lax.bitwise_and(query, WINDOW - 1) // step
    return near, jnp.where(near, 1.0, 0.0).astype(BF16), jnp.where(near, 0.0, 1.0).astype(BF16)


def stack_heads(block, lanes):
    return jnp.concatenate([block * lanes[1], block * lanes[2]], axis=0)


def merge_heads(block, lanes):
    return jnp.where(lanes[0], block[:WINDOW], block[WINDOW:])


def spread_sides(block, sides):
    return jnp.concatenate([block * sides[1], block * sides[2]], axis=0)


def attend(queries, keys, values, bias, lanes, sides):
    scores = product_back(keys, stack_heads(queries, lanes))
    scores = jnp.where(sides[0], scores[:WINDOW], scores[WINDOW:]) + bias
    weights = jnp.exp(scores - jnp.max(scores, axis=0, keepdims=True))
    probs = (weights * (1.0 / jnp.sum(weights, axis=0, keepdims=True))).astype(BF16)
    mixed = outer_sum(spread_sides(probs, sides), values)
    return probs, merge_heads(mixed, lanes)


def attend_back(queries, keys, values, probs, grad_out, lanes, sides):
    grad_stack = stack_heads(grad_out, lanes)
    grad_probs = product_back(values, grad_stack)
    grad_probs = jnp.where(sides[0], grad_probs[:WINDOW], grad_probs[WINDOW:])
    probs_full = probs.astype(F32)
    centre = jnp.sum(probs_full * grad_probs, axis=0, keepdims=True)
    grad_scores = spread_sides((probs_full * (grad_probs - centre)).astype(BF16), sides)
    grad_values = product(spread_sides(probs, sides), grad_stack)
    grad_keys = product(grad_scores, stack_heads(queries, lanes))
    grad_queries = merge_heads(outer_sum(grad_scores, keys), lanes) * HEAD_DIM**-0.5
    return grad_queries, grad_keys, grad_values


def window_kernel(queries, pairs, bias, attended, probs):
    width = queries.shape[1]
    lanes = lane_masks()
    sides = side_masks(1)
    both = jnp.concatenate([bias[0], bias[0]], axis=1)
    for n in range(width // PAIR):
        cols = slice(n * PAIR, (n + 1) * PAIR)
        held, out = attend(
            queries[:, cols],
            pairs[:, cols],
            pairs[:, width + n * PAIR : width + (n + 1) * PAIR],
            both,
            lanes,
            sides,
        )
        probs[0, n] = held
        attended[:, cols] = out.astype(BF16)


def lay_pooled(places, blocks, field):
    pools = blocks[0].shape[0]
    for k, block in enumerate(blocks):
        field[span(places[k], pools), :] = block[...]


def pooled_kernel(places, attended, bias, bulk, *refs):
    blocks = refs[:5]
    queries, mixed, probs, weights, field, sem = refs[-6:]
    width = attended.shape[1]
    s = pl.program_id(0)

    @pl.when(s == 0)
    def _():
        copies = fetch_square(bulk, 0, weights, sem)
        field[...] = jnp.zeros_like(field)
        settle(copies)

        @pl.loop(0, width // TILE)
        def _(n):
            cols = span(n, TILE)
            queries[:, cols] = product(attended[...], weights[:, cols]).astype(BF16) * HEAD_DIM**-0.5

    lay_pooled(places, blocks, field)
    lanes = lane_masks()
    sides = side_masks(STRIDE)
    both = jnp.concatenate([bias[0], bias[0]], axis=1)
    rows = span(s, WINDOW)
    for n in range(width // PAIR):
        cols = slice(n * PAIR, (n + 1) * PAIR)
        held, out = attend(
            queries[rows, cols],
            field[:, cols],
            field[:, width + n * PAIR : width + (n + 1) * PAIR],
            both,
            lanes,
            sides,
        )
        probs[0, n] = held
        first = attended[rows, cols].astype(F32)
        mixed[:, cols] = (first + out.astype(BF16).astype(F32)).astype(BF16)


def feed_kernel(tok, mixed, cot, vecs, bias_in, bulk, *refs):
    (
        result,
        grad_resid,
        grad_attn,
        gone,
        w_out,
        vec_grads,
        w_in,
        w_down,
        centred,
        rstd,
        normed,
        normed_t,
        active,
        slope,
        field,
        grad_outer,
        grad_in,
        grad_down,
        bias_grad,
        narrow,
        sems,
    ) = refs
    rows, width = tok.shape
    hidden = w_in.shape[1]
    first = fetch_square(bulk, 1, w_out, sems.at[0])
    second, third = fetch_bulk(bulk, w_in, w_down, (sems.at[1], sems.at[2]))
    settle(first)

    @pl.loop(0, width // TILE)
    def _(n):
        cols = span(n, TILE)
        field[:, cols] = tok[:, cols].astype(F32) + product(mixed[...], w_out[:, cols]) + vecs[0:1, cols]

    blocks = rows // WINDOW

    @pl.loop(0, blocks)
    def _(b):
        part = span(b, WINDOW)
        resid = field[part, :]
        middle = resid - jnp.mean(resid, axis=-1, keepdims=True)
        scale = lax.rsqrt(jnp.mean(middle * middle, axis=-1, keepdims=True) + norm_eps)
        unit = middle * scale
        centred[part, :] = unit
        rstd[part, :] = jnp.broadcast_to(scale, (WINDOW, 128))
        low = (unit * vecs[1:2, :] + vecs[2:3, :]).astype(BF16)
        normed[part, :] = low
        normed_t[:, part] = low.T

    settle(second)

    @pl.loop(0, hidden // TILE)
    def _(n):
        cols = span(n, TILE)
        inner = product(normed[...], w_in[:, cols]) + bias_in[0:1, cols]
        cdf = 0.5 + 0.5 * lax.erf(inner * ROOT_HALF)
        active[:, cols] = (inner * cdf).astype(BF16)
        slope[:, cols] = (cdf + inner * (jnp.exp(-0.5 * inner * inner) * ROOT_TWO_PI)).astype(BF16)

    settle(third)

    @pl.loop(0, width // TILE)
    def _(n):
        cols = span(n, TILE)
        unit = centred[:, cols] * vecs[1:2, cols] + vecs[2:3, cols]
        field[:, cols] = unit + product(active[...], w_down[:, cols]) + vecs[3:4, cols]

    vec_grads[...] = jnp.zeros_like(vec_grads)

    def add_row(k, value):
        vec_grads[k : k + 1, :] += jnp.sum(value, axis=0, keepdims=True)

    @pl.loop(0, blocks)
    def _(b):
        part = span(b, WINDOW)
        summed = field[part, :]
        middle = summed - jnp.mean(summed, axis=-1, keepdims=True)
        scale = lax.rsqrt(jnp.mean(middle * middle, axis=-1, keepdims=True) + norm_eps)
        unit = middle * scale
        result[part, :] = (unit * vecs[4:5, :] + vecs[5:6, :]).astype(BF16)
        grad = cot[part, :].astype(F32)
        add_row(4, grad * unit)
        add_row(5, grad)
        u = grad * vecs[4:5, :]
        lean = jnp.mean(u * unit, axis=-1, keepdims=True)
        grad = scale * (u - jnp.mean(u, axis=-1, keepdims=True) - unit * lean)
        field[part, :] = grad
        low = grad.astype(BF16)
        grad_outer[part, :] = low
        add_row(3, low.astype(F32))

    @pl.loop(0, hidden // TILE)
    def _(n):
        cols = span(n, TILE)
        grad = product_back(grad_outer[...], w_down[cols, :]).astype(BF16).astype(F32)
        low = (grad * slope[:, cols].astype(F32)).astype(BF16)
        slope[:, cols] = low
        bias_grad[:, cols] = jnp.sum(low.astype(F32), axis=0, keepdims=True)
        grad_down[cols, :] = outer_sum(active[:, cols], grad_outer[...]).astype(BF16)
        grad_in[:, cols] = product(normed_t[...], low).astype(BF16)

    block = width // SLOTS
    folds = hidden // width
    each = gone.shape[0] // SLOTS
    emits = []
    for j in range(SLOTS):
        for m in range(folds):
            source = grad_in.at[pl.ds(j * block, block), pl.ds(m * width, width)]
            target = gone.at[pl.ds(j * each + m * block, block), :]
            emits.append(pltpu.make_async_copy(source, target, sems.at[3]))
        source = grad_down.at[pl.ds(j * folds * block, folds * block), :]
        target = gone.at[pl.ds(j * each + folds * block, folds * block), :]
        emits.append(pltpu.make_async_copy(source, target, sems.at[3]))
    for copy in emits:
        copy.start()

    @pl.loop(0, width // TILE)
    def _(n):
        cols = span(n, TILE)
        field[:, cols] += product_back(slope[...], w_in[cols, :])

    @pl.loop(0, blocks)
    def _(b):
        part = span(b, WINDOW)
        grad = field[part, :]
        unit = centred[part, :]
        add_row(1, grad * unit)
        add_row(2, grad)
        u = grad * vecs[1:2, :]
        lean = jnp.mean(u * unit, axis=-1, keepdims=True)
        grad = rstd[part, 0:1] * (u - jnp.mean(u, axis=-1, keepdims=True) - unit * lean)
        grad_resid[part, :] = grad
        low = grad.astype(BF16)
        grad_attn[part, :] = low
        add_row(0, low.astype(F32))

    narrow[...] = jnp.zeros_like(narrow)
    small = narrow.shape[1]
    for j in range(SLOTS):
        narrow[j, :8, :block] = vec_grads[:, j * block : (j + 1) * block].astype(BF16)
        part = bias_grad[:, j * folds * block : (j + 1) * folds * block]
        narrow[j, 8:9, : folds * block] = part.astype(BF16)
        emits.append(
            pltpu.make_async_copy(
                narrow.at[j], gone.at[pl.ds(j * each + each - small, small), :], sems.at[3]
            )
        )
        emits[-1].start()
    settle(emits)


def pooled_back_kernel(places, grad_attn, mixed, queries, probs, weights, *refs):
    blocks = refs[:5]
    grad_mixed, grad_queries, grad_out, grad_own, grad_away, grad_near, grad_far = refs[-10:-3]
    field, total, grad_low = refs[-3:]
    width = grad_attn.shape[1]
    pools = blocks[0].shape[0]
    s = pl.program_id(0)

    @pl.when(s == 0)
    def _():
        field[...] = jnp.zeros_like(field)

        @pl.loop(0, width // TILE)
        def _(n):
            cols = span(n, TILE)
            grad = product_back(grad_attn[...], weights[cols, :])
            grad_mixed[:, cols] = grad
            grad_low[:, cols] = grad.astype(BF16)
            grad_out[cols, :] = outer_sum(mixed[:, cols], grad_attn[...]).astype(BF16)

    lay_pooled(places, blocks, field)
    lanes = lane_masks()
    sides = side_masks(STRIDE)
    rows = span(s, WINDOW)
    for n in range(width // PAIR):
        cols = slice(n * PAIR, (n + 1) * PAIR)
        others = slice(width + n * PAIR, width + (n + 1) * PAIR)
        grad_q, grad_k, grad_v = attend_back(
            queries[:, cols], field[:, cols], field[:, others], probs[0, n], grad_low[rows, cols], lanes, sides
        )
        grad_queries[:, cols] = grad_q.astype(BF16)
        total[:, cols] = grad_k
        total[:, others] = grad_v
    for k, target in enumerate((grad_own, grad_away.at[0], grad_away.at[1], grad_near, grad_far)):
        target[...] = total[span(places[k], pools), :].astype(BF16)


def window_back_kernel(grad_mixed, grad_second, first, queries, pairs, probs, weights, *refs):
    grad_queries, grad_pairs, grad_pooled, grad_low = refs
    width = first.shape[1]
    s = pl.program_id(0)

    @pl.when(s == 0)
    def _():
        @pl.loop(0, width // TILE)
        def _(n):
            cols = span(n, TILE)
            grad = grad_mixed[:, cols] + product_back(grad_second[...], weights[cols, :])
            grad_low[:, cols] = grad.astype(BF16)
            grad_pooled[cols, :] = outer_sum(first[:, cols], grad_second[...]).astype(BF16)

    lanes = lane_masks()
    sides = side_masks(1)
    rows = span(s, WINDOW)
    for n in range(width // PAIR):
        cols = slice(n * PAIR, (n + 1) * PAIR)
        others = slice(width + n * PAIR, width + (n + 1) * PAIR)
        grad_q, grad_k, grad_v = attend_back(
            queries[:, cols], pairs[:, cols], pairs[:, others], probs[0, n], grad_low[rows, cols], lanes, sides
        )
        grad_queries[:, cols] = grad_q.astype(BF16)
        grad_pairs[:, cols] = grad_k.astype(BF16)
        grad_pairs[:, others] = grad_v.astype(BF16)


def conv_back_kernel(table, order, own, away, near, far, vecs, pairs, grad_pairs, *refs):
    stacks = refs[:-6]
    total, tap_grads, edges, weights, rim, sem = refs[-6:]
    width = pairs.shape[1] // 2
    seqs = pairs.shape[0] // WIDE
    pools = WINDOW // STRIDE
    copies = fetch_all(order, stacks, table, 3 * width // 2, weights, sem)
    matrix = tap_matrix(pools)
    back = tap_matrix_back(pools)
    tap_grads[...] = jnp.zeros_like(tap_grads)

    @pl.loop(0, seqs)
    def _(s):
        for n in range(2 * width // TILE):
            cols = slice(n * TILE, (n + 1) * TILE)
            kind, start = divmod(n * TILE, width)
            taps = [vecs[tap_row(t, kind) : tap_row(t, kind) + 1, start : start + TILE] for t in range(KERNEL)]
            part = span(s, pools)
            grad = own[part, cols].astype(F32) + away[part, cols].astype(F32)
            grad = grad + near[part, cols].astype(F32) + far[part, cols].astype(F32)
            grad = grad.astype(BF16).astype(F32)
            spread = [(taps[t] * grad).astype(BF16) for t in range(KERNEL)]
            whole = grad_pairs[span(s, WIDE), cols].astype(F32) + product(back, jnp.concatenate(spread, axis=0))
            total[span(s, WIDE), cols] = whole.astype(BF16)
            slab = product(matrix, pairs[span(s, WIDE), cols])
            for t in range(KERNEL):
                row = 2 * t + kind
                tap_grads[row : row + 1, start : start + TILE] += jnp.sum(
                    grad * slab[t * pools : (t + 1) * pools], axis=0, keepdims=True
                )

    for s in range(seqs):
        rim[s * HALF : (s + 1) * HALF, :] = total[s * WIDE : s * WIDE + HALF, :]
        rim[(seqs + s) * HALF : (seqs + s + 1) * HALF, :] = total[s * WIDE + HALF + WINDOW : (s + 1) * WIDE, :]
    settle(copies)

    @pl.loop(0, width // TILE)
    def _(n):
        cols = span(n, TILE)
        edges[:, cols] = product_back(rim[...], weights[cols, width:]).astype(BF16)


def query_grad_kernel(order, tok, grad_queries, grad_pooled, grad_out, keep, give, tok_t, total, sem):
    width = tok.shape[1]
    block = width // SLOTS
    targets = (keep, give)
    copies = emit(order, grad_pooled, pl.ds(0, width), block, targets, 3 * width, sem)
    copies += emit(order, grad_out, pl.ds(0, width), block, targets, 4 * width, sem)
    tok_t[...] = tok[...].T

    @pl.loop(0, width // TILE)
    def _(n):
        cols = span(n, TILE)
        total[:, cols] = product(tok_t[...], grad_queries[:, cols]).astype(BF16)

    copies += emit(order, total, pl.ds(0, width), block, targets, 0, sem)
    settle(copies)


def weight_grad_kernel(order, tok, low, high, grad_pairs, tap_grads, *refs):
    keep, give, xext_t, total, narrow, sem = refs[2:]
    width = tok.shape[1]
    block = width // SLOTS
    targets = (keep, give)
    taps = jnp.concatenate([tap_grads[...], jnp.zeros((112, width), F32)], axis=0).T
    narrow[...] = taps.astype(BF16)
    copies = emit(order, narrow, pl.ds(0, 128), block, targets, 5 * width, sem)
    for s in range(low.shape[0] // HALF):
        parts = (
            low[s * HALF : (s + 1) * HALF, :],
            tok[s * WINDOW : (s + 1) * WINDOW, :],
            high[s * HALF : (s + 1) * HALF, :],
        )
        xext_t[:, s * WIDE : (s + 1) * WIDE] = jnp.concatenate(parts, axis=0).T

    @pl.loop(0, 2 * width // TILE)
    def _(n):
        cols = span(n, TILE)
        total[:, cols] = product(xext_t[...], grad_pairs[:, cols]).astype(BF16)

    copies += emit(order, total, pl.ds(0, 2 * width), block, targets, width, sem)
    settle(copies)


def token_grad_kernel(table, order, grad_resid, grad_queries, grad_pairs, low, high, *refs):
    stacks = refs[:-4]
    out, weights, own, sem = refs[-4:]
    width = grad_resid.shape[1]
    seqs = grad_resid.shape[0] // WINDOW
    copies = fetch_all(order, stacks, table, 3 * width // 2, weights, sem)
    for s in range(seqs):
        own[s * WINDOW : (s + 1) * WINDOW, :width] = grad_queries[s * WINDOW : (s + 1) * WINDOW, :]
        own[s * WINDOW : (s + 1) * WINDOW, width:] = grad_pairs[s * WIDE + HALF : s * WIDE + HALF + WINDOW, :]
    settle(copies)

    @pl.loop(0, width // TILE)
    def _(n):
        cols = span(n, TILE)
        out[:, cols] = grad_resid[:, cols] + product_back(own[...], weights[cols, :])
        for s in range(seqs):
            part = slice(s * HALF, (s + 1) * HALF)
            out[s * WINDOW : s * WINDOW + HALF, cols] += low[part, cols].astype(F32)
            out[s * WINDOW + HALF : (s + 1) * WINDOW, cols] += high[part, cols].astype(F32)


def shape_of(*dims, dtype=BF16):
    return jax.ShapeDtypeStruct(dims, dtype)


def turn(block, step):
    return lax.ppermute(block, "shard", [(i, (i - 4 * step) % SLOTS) for i in range(SLOTS)])


def flip(block):
    return lax.ppermute(block, "shard", [(i, i ^ 2) for i in range(SLOTS)])


def other(block):
    return lax.ppermute(block, "rep", [(0, 1), (1, 0)])


def gate_kernel(*refs):
    del refs


def after(value, *others):
    if not direct() or not others:
        return value
    return pl.pallas_call(
        gate_kernel,
        out_shape=jax.ShapeDtypeStruct(value.shape, value.dtype),
        in_specs=[any_spec()] * (1 + len(others)),
        out_specs=any_spec(),
        input_output_aliases={0: 0},
        compiler_params=params(2),
        cost_estimate=cost(0),
        name="gate",
    )(value, *others)


def direct():
    return lax.axis_size("shard") == SLOTS and lax.axis_size("rep") == 2


def block_order():
    if not direct():
        return jnp.arange(SLOTS + 1, dtype=jnp.int32) % SLOTS
    me = lax.axis_index("shard")
    k = jnp.arange(SLOTS, dtype=jnp.int32)
    places = ((me // 4 + k // 4) % 4) * 4 + jnp.bitwise_xor(me % 4, k % 4)
    return jnp.concatenate([places, lax.axis_index("rep")[None]]).astype(jnp.int32)


class Gather:
    def __init__(self, block):
        self.block = block

    def turn(self, *gate):
        own = after(self.block, *gate)
        self.along = jnp.stack([own] + [turn(own, step) for step in (1, 2, 3)])

    def cross(self, *gate):
        self.along = after(self.along, *gate)
        self.across = flip(self.along)

    def rep(self, *gate):
        self.across = after(self.across, *gate)
        self.first = jnp.concatenate([self.along, self.across], axis=0)
        self.second = other(self.first)

    def cores(self, *gate):
        stacks = [self.first, after(self.second, *gate)]
        stacks = stacks + [swap(stack) for stack in stacks]
        table = []
        for k in range(SLOTS):
            part = k // 2 % 2 * 4 + k // 4
            table.append(((2 * (k % 2), part, 0), (2 * (k % 2) + 1, part, 0)))
        return stacks, tuple(table)


def plain_gather(block, extra=None):
    rows, width = block.shape
    half = width // 2
    rows = rows * lax.axis_size("shard") // SLOTS
    mine, rest = block[:, :half], block[:, half:]
    both = jnp.concatenate([mine] + ([] if extra is None else [extra]) + [rest], axis=1)
    full = lax.all_gather(both, "shard", axis=0, tiled=True)
    table = tuple(((0, k, 0), (0, k, both.shape[1] - half)) for k in range(SLOTS))
    return [full.reshape(SLOTS, rows, both.shape[1])], table


def pack_kernel(order, query, key, value, pooled, out, inner, outer, tokens, taps, *refs):
    vectors, bias = refs[:6], refs[6]
    lead, bulk, low, high, joined, small = refs[7:]
    part, width = query.shape
    half = 3 * width // 2
    for k, source in enumerate((query, key, value)):
        joined[:, k * width : (k + 1) * width] = source[...]
    mine = order[SLOTS]
    small[...] = jnp.zeros_like(small)
    for k, source in enumerate(vectors):
        small[k : k + 1, :part] = source[...].astype(F32)
    for t in range(KERNEL):
        small[tap_row(t, 0) : tap_row(t, 0) + 2, :part] = taps[t].astype(F32)
    small[BIAS_ROW:SMALL, :part] = bias[...].astype(F32)
    lead[:, :half] = joined[:, span(mine, half)]
    lead[:, half:] = small[...].T[:part].astype(BF16)
    bulk[:part, :] = pooled[...]
    bulk[part : 2 * part, :] = out[...]
    folds = inner.shape[1] // width
    for m in range(folds):
        bulk[(2 + m) * part : (3 + m) * part, :] = inner[:, m * width : (m + 1) * width]
    bulk[(2 + folds) * part :, :] = outer[...]
    high[...] = tokens[:, :HALF, :]
    low[...] = tokens[:, tokens.shape[1] - HALF :, :]


def split_kernel(wide, order, keep, arrived, a_keep, a_send, b_keep, b_send):
    half = wide // 2
    mine = span(order[SLOTS], half)
    rest = span(1 - order[SLOTS], half)
    for across in range(2):
        a_keep[across, 0] = keep[across, 0, :, mine] + arrived[across, 0, :, mine]
        a_send[across, 0] = keep[across, 0, :, rest] + arrived[across, 0, :, rest]
        target = b_send if across else b_keep
        target[0] = keep[across, 0, :, wide:] + arrived[across, 0, :, wide:]


def fold_kernel(keep, arrived, x_keep, x_send):
    x_keep[0] = keep[0, 0] + arrived[0, 0]
    x_send[0] = keep[1, 0] + arrived[1, 0]


def join_kernel(x_keep, x_arrived, b_keep, b_arrived, *parts):
    half = x_keep.shape[2]
    for k, part in enumerate(parts):
        part[:, :half] = x_keep[k] + x_arrived[k]
        part[:, half:] = b_keep[k] + b_arrived[k]


def gather_sum_kernel(own, first, second, third, out):
    total = own[...].astype(F32) + first[...].astype(F32) + second[...].astype(F32) + third[...].astype(F32)
    out[...] = total.astype(BF16)


def final_kernel(wide, pieces, order, own, arrived, *refs):
    outs, total = refs[:-1], refs[-1]
    half = wide // 2
    total[:, span(order[SLOTS], half)] = own[:, :half].astype(F32)
    total[:, span(1 - order[SLOTS], half)] = arrived[:, :half].astype(F32)
    total[:, wide:] = own[:, half:].astype(F32) + arrived[:, half:].astype(F32)
    for (start, size), out in zip(pieces, outs):
        out[...] = total[:, start : start + size]


class Scatter:
    def __init__(self, keep, give, order, wide, pieces):
        self.order, self.wide, self.pieces = order, wide, pieces
        self.rows, self.columns = keep.shape[2:]
        self.keep, self.give = keep, give
        if direct():
            self.arrived = swap(give)

    def split(self):
        rows, half, rest = self.rows, self.wide // 2, self.columns - self.wide
        four = pl.BlockSpec((2, 1, rows, self.columns), lambda z: (0, z, 0, 0))
        a_block = pl.BlockSpec((2, 1, rows, half), lambda z: (0, z, 0, 0))
        b_block = pl.BlockSpec((1, rows, rest), lambda z: (z, 0, 0))
        a_shape, b_shape = shape_of(2, 4, rows, half), shape_of(4, rows, rest)
        self.a_keep, a_send, self.b_keep, b_send = pl.pallas_call(
            functools.partial(split_kernel, self.wide),
            grid=(4,),
            out_shape=(a_shape, a_shape, b_shape, b_shape),
            in_specs=[smem_spec(), four, four],
            out_specs=(a_block, a_block, b_block, b_block),
            compiler_params=params(14),
            cost_estimate=cost(5),
            name="split",
        )(self.order, self.keep, self.arrived)
        self.a_arrived = other(a_send)
        self.b_arrived = flip(b_send)
        return a_send

    def fold(self):
        rows, half = self.rows, self.wide // 2
        a_block = pl.BlockSpec((2, 1, rows, half), lambda z: (0, z, 0, 0))
        x_block = pl.BlockSpec((1, rows, half), lambda z: (z, 0, 0))
        x_shape = shape_of(4, rows, half)
        self.x_keep, x_send = pl.pallas_call(
            fold_kernel,
            grid=(4,),
            out_shape=(x_shape, x_shape),
            in_specs=[a_block, a_block],
            out_specs=(x_block, x_block),
            compiler_params=params(10),
            cost_estimate=cost(4),
            name="fold",
        )(self.a_keep, self.a_arrived)
        self.x_arrived = flip(x_send)
        return x_send

    def join(self):
        shape = shape_of(self.rows, self.columns - self.wide // 2)
        parts = pl.pallas_call(
            join_kernel,
            out_shape=(shape,) * 4,
            in_specs=[vmem_spec()] * 4,
            out_specs=(vmem_spec(),) * 4,
            compiler_params=params(14),
            cost_estimate=cost(3),
            name="join",
        )(self.x_keep, self.x_arrived, self.b_keep, self.b_arrived)
        self.turned = [parts[0]] + [turn(parts[step], -step) for step in (1, 2, 3)]
        return parts[1]

    def gather(self):
        self.own = pl.pallas_call(
            gather_sum_kernel,
            out_shape=shape_of(self.rows, self.columns - self.wide // 2),
            in_specs=[vmem_spec()] * 4,
            out_specs=vmem_spec(),
            compiler_params=params(10),
            cost_estimate=cost(2),
            name="gather_sum",
        )(*self.turned)
        self.last = other(self.own)
        return self.own

    def final(self):
        return pl.pallas_call(
            functools.partial(final_kernel, self.wide, self.pieces),
            out_shape=tuple(shape_of(self.rows, size, dtype=F32) for _, size in self.pieces),
            in_specs=[smem_spec(), vmem_spec(), vmem_spec()],
            out_specs=(vmem_spec(),) * len(self.pieces),
            scratch_shapes=[pltpu.VMEM((self.rows, self.columns), F32)],
            compiler_params=params(12),
            cost_estimate=cost(2),
            name="final",
        )(self.order, self.own, self.last)


def bulk_final_kernel(own, arrived, inner, outer, small):
    part, hidden = inner.shape
    width = own.shape[1]
    total = own[...].astype(F32) + arrived[...].astype(F32)
    folds = hidden // width
    for m in range(folds):
        inner[:, m * width : (m + 1) * width] = total[m * part : (m + 1) * part]
    outer[...] = total[folds * part : 2 * folds * part]
    small[...] = total[2 * folds * part :]


def plain_total(whole):
    return rep_total(lax.psum_scatter(whole, "shard", scatter_dimension=0, tiled=True))


def plain_scatter(blocks, parts):
    keep, give = blocks
    full = jnp.stack([keep, give]).transpose(2, 1, 0, 3, 4).reshape(SLOTS, keep.shape[2], keep.shape[3])
    width = SLOTS * keep.shape[2]
    return [plain_total(full[:, :, start:stop].reshape(width, -1)) for start, stop in parts]


def rep_total(piece):
    count = lax.axis_size("rep")
    total = piece.astype(F32)
    for step in range(1, count):
        route = [(i, (i + step) % count) for i in range(count)]
        total = total + lax.ppermute(piece, "rep", route).astype(F32)
    return total


def shift(block, distance):
    count = lax.axis_size("shard")
    return lax.ppermute(
        block, "shard", [(i, i + distance) for i in range(count) if 0 <= i + distance < count]
    )


def swap(block):
    return lax.ppermute(block, "shard", [(i, i ^ 1) for i in range(lax.axis_size("shard"))])


def hop(block, outer):
    count = lax.axis_size("shard")
    route = [(i, i + (2 if (i % 2 == 0) == outer else -2)) for i in range(count)]
    return lax.ppermute(block, "shard", [(i, j) for i, j in route if 0 <= j < count])


def shards(
    tokens,
    query_proj,
    key_proj,
    value_proj,
    pooled_query,
    output_proj,
    conv_taps,
    output_bias,
    first_gain,
    first_shift,
    inner_proj,
    inner_bias,
    outer_proj,
    outer_bias,
    second_gain,
    second_shift,
    block_ids,
    cotangent,
):
    seqs, tok_span, width = tokens.shape
    rows = seqs * tok_span
    hidden = inner_proj.shape[1]
    device_count = lax.axis_size("shard")
    device_index = lax.axis_index("shard")
    seq_length = tok_span * device_count
    pools = tok_span // STRIDE
    pool_reach = POOL_SPAN // (2 * STRIDE)
    n_pair = width // PAIR
    core = lax.rem(device_index, 2)

    tok = tokens.reshape(rows, width)
    cot = cotangent.reshape(rows, width)
    vectors = [output_bias, first_gain, first_shift, outer_bias, second_gain, second_shift]
    part = width // device_count
    block = width // SLOTS
    order = block_order()
    if direct():
        packed = pl.pallas_call(
            pack_kernel,
            out_shape=(
                shape_of(part, 3 * width // 2 + 128),
                shape_of(bulk_rows(width, hidden), width),
                shape_of(seqs, HALF, width),
                shape_of(seqs, HALF, width),
            ),
            in_specs=[smem_spec()] + [vmem_spec()] * 16,
            out_specs=(vmem_spec(),) * 4,
            scratch_shapes=[pltpu.VMEM((part, 3 * width), BF16), pltpu.VMEM((128, 128), F32)],
            compiler_params=params(),
            cost_estimate=cost(3),
            name="pack",
        )(
            order,
            query_proj,
            key_proj,
            value_proj,
            pooled_query,
            output_proj,
            inner_proj,
            outer_proj,
            tokens,
            conv_taps,
            *[vector.reshape(1, part) for vector in vectors],
            inner_bias.reshape(4, part),
        )
        lead = Gather(packed[0])
        bulk = lax.all_gather(packed[1], "shard", axis=0, tiled=True)
        lead.turn()
        lead.cross()
        tick = after(jnp.zeros((8, 128), F32), lead.across)
        lead.rep()
        tok_low = shift(after(packed[2], tick), 1).reshape(seqs * HALF, width)
        tok_high = shift(after(packed[3], tick), -1).reshape(seqs * HALF, width)
        lead, lead_table = lead.cores(tok_low, tok_high)
    else:
        tok_low = shift(tokens[:, tok_span - HALF :], 1).reshape(seqs * HALF, width)
        tok_high = shift(tokens[:, :HALF], -1).reshape(seqs * HALF, width)
        small = jnp.concatenate(vectors + [conv_taps.reshape(-1), inner_bias]).reshape(SMALL, part).T
        small = jnp.pad(small, ((0, 0), (0, 128 - SMALL)))
        lead, lead_table = plain_gather(jnp.concatenate([query_proj, key_proj, value_proj], axis=1), small)
        square = [
            lax.all_gather(block_rows, "shard", axis=0, tiled=True).reshape(SLOTS, block, width)
            for block_rows in (pooled_query, output_proj)
        ]
        full = lax.all_gather(inner_proj, "shard", axis=0, tiled=True)
        full = full.reshape(SLOTS, block, hidden // width, width).transpose(0, 2, 1, 3)
        full = full.reshape(SLOTS, hidden // SLOTS, width)
        down = lax.all_gather(outer_proj, "shard", axis=0, tiled=True)
        down = down.reshape(SLOTS, hidden // SLOTS, width)
        bulk = jnp.concatenate(square + [full, down], axis=1).reshape(-1, width)

    query = jnp.arange(tok_span, dtype=jnp.int32)[None, :]
    slot = jnp.arange(WINDOW, dtype=jnp.int32)[:, None]
    query_ids = lax.dynamic_slice_in_dim(block_ids, device_index * tok_span, tok_span, 1)[:, None, :]

    def bias_for(ids, start, length, step, reach):
        ids = lax.dynamic_slice_in_dim(jnp.pad(ids, ((0, 0), (reach, reach + WINDOW))), start, WIDE, 1)
        near = slot >= query // step
        place = start - reach + jnp.where(near, slot, slot + WINDOW)
        key_ids = jnp.where(near[None], ids[:, :WINDOW, None], ids[:, WINDOW:, None])
        allowed = ((place >= 0) & (place < length))[None] & (key_ids <= query_ids)
        return jnp.where(allowed, 0.0, neg_fill)

    bias_one = bias_for(block_ids, device_index * tok_span, seq_length, 1, HALF)
    bias_two = bias_for(
        block_ids[:, ::STRIDE], device_index * pools, seq_length // STRIDE, STRIDE, pool_reach
    )

    n_lead = len(lead)
    queries, pairs, pooled, vecs = pl.pallas_call(
        functools.partial(project_kernel, lead_table),
        out_shape=(
            shape_of(rows, width),
            shape_of(seqs * WIDE, 2 * width),
            shape_of(seqs * pools, 2 * width),
            shape_of(24, width, dtype=F32),
        ),
        in_specs=[smem_spec()] + [vmem_spec()] * 3 + [hbm_spec()] * n_lead,
        out_specs=(vmem_spec(),) * 4,
        scratch_shapes=[
            pltpu.VMEM((seqs * WIDE, width), BF16),
            pltpu.VMEM((width, 3 * width), BF16),
            pltpu.VMEM((width, 128), BF16),
            pltpu.SemaphoreType.DMA,
        ],
        compiler_params=params(54),
        cost_estimate=cost(15),
        name="project",
    )(order, tok, tok_low, tok_high, *lead)
    bias_in = vecs[BIAS_ROW:SMALL].reshape(4, device_count, part).transpose(1, 0, 2).reshape(1, hidden)

    pool_away = swap(pooled)
    pool_far = hop(pooled, True)
    pool_near = hop(pooled, False)
    places = jnp.where(
        core == 0, jnp.array([2, 3, 1, 4, 0], jnp.int32), jnp.array([2, 1, 3, 0, 4], jnp.int32)
    )

    seq_block = lambda r, c: pl.BlockSpec((r, c), lambda s: (s, 0))
    whole_block = lambda r, c: pl.BlockSpec((r, c), lambda s: (0, 0))
    bias_block = pl.BlockSpec((1, WINDOW, tok_span), lambda s: (s, 0, 0))
    prob_block = pl.BlockSpec((1, n_pair, WINDOW, 2 * tok_span), lambda s: (s, 0, 0, 0))
    prob_shape = shape_of(seqs, n_pair, WINDOW, 2 * tok_span)

    attended, probs_one = pl.pallas_call(
        window_kernel,
        grid=(seqs,),
        out_shape=(shape_of(rows, width), prob_shape),
        in_specs=[seq_block(tok_span, width), seq_block(WIDE, 2 * width), bias_block],
        out_specs=(seq_block(tok_span, width), prob_block),
        compiler_params=params(12),
        cost_estimate=cost(10),
        name="window",
    )(queries, pairs, bias_one)

    pool_near = after(pool_near, attended)
    pool_blocks = (pooled, pool_away, swap(pool_near), pool_near, pool_far)
    pool_specs = [seq_block(pools, 2 * width)] * 5
    second, mixed, probs_two, pooled_weights = pl.pallas_call(
        pooled_kernel,
        grid=(seqs,),
        out_shape=(shape_of(rows, width), shape_of(rows, width), prob_shape, shape_of(width, width)),
        in_specs=[smem_spec(), whole_block(rows, width), bias_block, hbm_spec()] + pool_specs,
        out_specs=(
            whole_block(rows, width),
            seq_block(tok_span, width),
            prob_block,
            whole_block(width, width),
        ),
        scratch_shapes=[pltpu.VMEM((WIDE, 2 * width), BF16), pltpu.SemaphoreType.DMA],
        compiler_params=params(54),
        cost_estimate=cost(14),
        name="pooled",
    )(places, attended, bias_two, bulk, *pool_blocks)

    each = 2 * hidden // SLOTS + SMALL_ROWS
    result, grad_resid, grad_attn, grad_bulk, out_weights, _ = pl.pallas_call(
        feed_kernel,
        out_shape=(
            shape_of(rows, width),
            shape_of(rows, width, dtype=F32),
            shape_of(rows, width),
            shape_of(SLOTS * each, width),
            shape_of(width, width),
            shape_of(8, width, dtype=F32),
        ),
        in_specs=[vmem_spec()] * 5 + [hbm_spec()],
        out_specs=(vmem_spec(),) * 3 + (any_spec(), vmem_spec(), vmem_spec()),
        scratch_shapes=[
            pltpu.VMEM((width, hidden), BF16),
            pltpu.VMEM((hidden, width), BF16),
            pltpu.VMEM((rows, width), F32),
            pltpu.VMEM((rows, 128), F32),
            pltpu.VMEM((rows, width), BF16),
            pltpu.VMEM((width, rows), BF16),
            pltpu.VMEM((rows, hidden), BF16),
            pltpu.VMEM((rows, hidden), BF16),
            pltpu.VMEM((rows, width), F32),
            pltpu.VMEM((rows, width), BF16),
            pltpu.VMEM((width, hidden), BF16),
            pltpu.VMEM((hidden, width), BF16),
            pltpu.VMEM((1, hidden), F32),
            pltpu.VMEM((SLOTS, SMALL_ROWS, width), BF16),
            pltpu.SemaphoreType.DMA((4,)),
        ],
        compiler_params=params(58),
        cost_estimate=cost(45),
        name="feed",
    )(tok, mixed, cot, vecs, bias_in, bulk)
    if direct():
        own_bulk = lax.psum_scatter(grad_bulk, "shard", scatter_dimension=0, tiled=True)

    back_shape = shape_of(seqs * pools, 2 * width)
    grad_mixed, grad_second, grad_out, pg_own, pg_away, pg_near, pg_far = pl.pallas_call(
        pooled_back_kernel,
        grid=(seqs,),
        out_shape=(
            shape_of(rows, width, dtype=F32),
            shape_of(rows, width),
            shape_of(width, width),
            back_shape,
            shape_of(2, seqs * pools, 2 * width),
            back_shape,
            back_shape,
        ),
        in_specs=[
            smem_spec(),
            whole_block(rows, width),
            whole_block(rows, width),
            seq_block(tok_span, width),
            prob_block,
            whole_block(width, width),
        ]
        + pool_specs,
        out_specs=(
            whole_block(rows, width),
            seq_block(tok_span, width),
            whole_block(width, width),
            seq_block(pools, 2 * width),
            pl.BlockSpec((2, pools, 2 * width), lambda s: (0, s, 0)),
            seq_block(pools, 2 * width),
            seq_block(pools, 2 * width),
        ),
        scratch_shapes=[
            pltpu.VMEM((WIDE, 2 * width), BF16),
            pltpu.VMEM((WIDE, 2 * width), F32),
            pltpu.VMEM((rows, width), BF16),
        ],
        compiler_params=params(20),
        cost_estimate=cost(22),
        name="pooled_back",
    )(places, grad_attn, mixed, second, probs_two, out_weights, *pool_blocks)

    pg_cross = swap(pg_away)
    pg_near = (pg_near.astype(F32) + pg_cross[1].astype(F32)).astype(BF16)
    back_near = lax.ppermute(pg_near, "shard", back_route(device_count, False))
    back_far = lax.ppermute(pg_far, "shard", back_route(device_count, True))
    grad_second = after(grad_second, pg_near)

    grad_queries, grad_pairs, grad_pooled = pl.pallas_call(
        window_back_kernel,
        grid=(seqs,),
        out_shape=(shape_of(rows, width), shape_of(seqs * WIDE, 2 * width), shape_of(width, width)),
        in_specs=[
            whole_block(rows, width),
            whole_block(rows, width),
            whole_block(rows, width),
            seq_block(tok_span, width),
            seq_block(WIDE, 2 * width),
            prob_block,
            whole_block(width, width),
        ],
        out_specs=(seq_block(tok_span, width), seq_block(WIDE, 2 * width), whole_block(width, width)),
        scratch_shapes=[pltpu.VMEM((rows, width), BF16)],
        compiler_params=params(20),
        cost_estimate=cost(22),
        name="window_back",
    )(grad_mixed, grad_second, attended, queries, pairs, probs_one, pooled_weights)

    lead_shape = shape_of(2, 4, block, 5 * width + 128)
    lead_keep, lead_give = pl.pallas_call(
        query_grad_kernel,
        out_shape=(lead_shape, lead_shape),
        in_specs=[smem_spec()] + [vmem_spec()] * 4,
        out_specs=(any_spec(),) * 2,
        scratch_shapes=[
            pltpu.VMEM((width, rows), BF16),
            pltpu.VMEM((width, width), BF16),
            pltpu.SemaphoreType.DMA,
        ],
        compiler_params=params(12),
        cost_estimate=cost(5),
        name="query_grad",
    )(order, tok, grad_queries, grad_pooled, grad_out)
    vecs = after(vecs, lead_keep)

    pair_total, tap_grads, edges = pl.pallas_call(
        functools.partial(conv_back_kernel, lead_table),
        out_shape=(
            shape_of(seqs * WIDE, 2 * width),
            shape_of(16, width, dtype=F32),
            shape_of(2 * seqs * HALF, width),
        ),
        in_specs=[smem_spec()] + [vmem_spec()] * 7 + [hbm_spec()] * n_lead,
        out_specs=(vmem_spec(),) * 3,
        scratch_shapes=[
            pltpu.VMEM((width, 3 * width), BF16),
            pltpu.VMEM((2 * seqs * HALF, 2 * width), BF16),
            pltpu.SemaphoreType.DMA,
        ],
        compiler_params=params(28),
        cost_estimate=cost(12),
        name="conv_back",
    )(order, pg_own, pg_cross[0], back_near, back_far, vecs, pairs, grad_pairs, *lead)

    lead_keep, lead_give = pl.pallas_call(
        weight_grad_kernel,
        out_shape=(lead_shape, lead_shape),
        in_specs=[smem_spec()] + [vmem_spec()] * 5 + [any_spec()] * 2,
        out_specs=(any_spec(),) * 2,
        input_output_aliases={6: 0, 7: 1},
        scratch_shapes=[
            pltpu.VMEM((width, seqs * WIDE), BF16),
            pltpu.VMEM((width, 2 * width), BF16),
            pltpu.VMEM((width, 128), BF16),
            pltpu.SemaphoreType.DMA,
        ],
        compiler_params=params(18),
        cost_estimate=cost(10),
        name="weight_grad",
    )(order, tok, tok_low, tok_high, pair_total, tap_grads, lead_keep, lead_give)
    pieces = tuple((k * width, width) for k in range(5)) + ((5 * width, 128),)
    lead_sum = Scatter(lead_keep, lead_give, order, 24 * 128, pieces)
    if direct():
        lead_sum.split()
        edges = after(edges, lead_sum.b_keep)
    edge_high = shift(edges[: seqs * HALF], -1)
    edge_low = shift(edges[seqs * HALF :], 1)

    tokens_grad = pl.pallas_call(
        functools.partial(token_grad_kernel, lead_table),
        out_shape=shape_of(rows, width, dtype=F32),
        in_specs=[smem_spec()] + [vmem_spec()] * 5 + [hbm_spec()] * n_lead,
        out_specs=vmem_spec(),
        scratch_shapes=[
            pltpu.VMEM((width, 3 * width), BF16),
            pltpu.VMEM((rows, 3 * width), BF16),
            pltpu.SemaphoreType.DMA,
        ],
        compiler_params=params(22),
        cost_estimate=cost(11),
        name="token_grad",
    )(order, grad_resid, grad_queries, pair_total, edge_low, edge_high, *lead)

    folds = hidden // width
    if direct():
        lead_sum.a_keep = after(lead_sum.a_keep, tokens_grad, lead_sum.b_arrived)
        lead_sum.fold()
        lead_sum.join()
        own_bulk = after(own_bulk, lead_sum.turned[0])
        lead_sum.gather()
        own_in, own_down, small_own = pl.pallas_call(
            bulk_final_kernel,
            out_shape=(
                shape_of(part, hidden, dtype=F32),
                shape_of(folds * part, width, dtype=F32),
                shape_of(SMALL_ROWS, width, dtype=F32),
            ),
            in_specs=[vmem_spec()] * 2,
            out_specs=(vmem_spec(),) * 3,
            compiler_params=params(10),
            cost_estimate=cost(2),
            name="bulk_final",
        )(own_bulk, other(own_bulk))
        vec_own = [small_own[k, :part] for k in range(6)]
        bias_own = small_own[8, : folds * part]
        own_query, own_keys, own_values, own_pooled, own_out, taps_own = lead_sum.final()
    else:
        whole = grad_bulk.reshape(SLOTS, each, width)
        inner_part = whole[:, : folds * block].reshape(SLOTS, folds, block, width).transpose(0, 2, 1, 3)
        own_in = plain_total(inner_part.reshape(width, hidden))
        own_down = plain_total(whole[:, folds * block : 2 * folds * block].reshape(hidden, width))
        small = whole[:, 2 * folds * block :]
        vec_own = [plain_total(small[:, k, :block].reshape(width)) for k in range(6)]
        bias_own = plain_total(small[:, 8, : folds * block].reshape(hidden))
        parts = [(k * width, (k + 1) * width) for k in range(5)] + [(5 * width, None)]
        own_query, own_keys, own_values, own_pooled, own_out, taps_own = plain_scatter(
            (lead_keep, lead_give), parts
        )
    taps_own = taps_own.T[: 2 * KERNEL].reshape(KERNEL, 2, part)
    return (
        result.reshape(tokens.shape),
        tokens_grad.reshape(tokens.shape),
        own_query,
        own_keys,
        own_values,
        own_pooled,
        own_out,
        taps_own,
        vec_own[0],
        vec_own[1],
        vec_own[2],
        own_in,
        bias_own,
        own_down,
        vec_own[3],
        vec_own[4],
        vec_own[5],
    )


def back_route(count, outer):
    route = [(i, i + (2 if (i % 2 == 0) == outer else -2)) for i in range(count)]
    return [(j, i) for i, j in route if 0 <= j < count]


def solution(mesh):
    in_specs = (
        P("rep", "shard", None),
        P("shard", None),
        P("shard", None),
        P("shard", None),
        P("shard", None),
        P("shard", None),
        P(None, None, "shard"),
        P("shard"),
        P("shard"),
        P("shard"),
        P("shard", None),
        P("shard"),
        P("shard", None),
        P("shard"),
        P("shard"),
        P("shard"),
        P("rep", None),
        P("rep", "shard", None),
    )
    out_specs = (
        P("rep", "shard", None),
        P("rep", "shard", None),
        P("shard", None),
        P("shard", None),
        P("shard", None),
        P("shard", None),
        P("shard", None),
        P(None, None, "shard"),
        P("shard"),
        P("shard"),
        P("shard"),
        P("shard", None),
        P("shard"),
        P("shard", None),
        P("shard"),
        P("shard"),
        P("shard"),
    )
    return jax.shard_map(shards, mesh=mesh, in_specs=in_specs, out_specs=out_specs, check_vma=False)
```

```python
import functools

import jax
import jax.numpy as jnp
from jax import lax
from jax.experimental import pallas as pl
from jax.experimental.pallas import tpu as pltpu
from jax.sharding import PartitionSpec as P

HEAD_DIM = 64
WINDOW = 128
POOL_SPAN = 512
STRIDE = 4
KERNEL = 5

neg_fill = -1e30
norm_eps = 1e-05
F32 = jnp.float32
BF16 = jnp.bfloat16
ROOT_HALF = 0.7071067811865476
ROOT_TWO_PI = 0.3989422804014327

HALF = WINDOW // 2
WIDE = 2 * WINDOW
PAIR = 2 * HEAD_DIM
TILE = 256
SLOTS = 16
VMEM_LIMIT = 58
SCALE = 0.05


def product(former, latter):
    return jnp.dot(former, latter, preferred_element_type=F32)


def product_back(former, latter):
    return lax.dot_general(former, latter, (((1,), (1,)), ((), ())), preferred_element_type=F32)


def outer_sum(former, latter):
    return lax.dot_general(former, latter, (((0,), (0,)), ((), ())), preferred_element_type=F32)


def span(index, size):
    return pl.ds(pl.multiple_of(index * size, size), size)


def any_spec():
    return pl.BlockSpec(memory_space=pl.ANY)


def hbm_spec():
    return pl.BlockSpec(memory_space=pltpu.HBM)


def vmem_spec():
    return pl.BlockSpec(memory_space=pltpu.VMEM)


def smem_spec():
    return pl.BlockSpec(memory_space=pltpu.SMEM)


def params(mebibytes=VMEM_LIMIT):
    return pltpu.CompilerParams(vmem_limit_bytes=mebibytes * 1024 * 1024)


def cost(microseconds):
    return pl.CostEstimate(
        flops=int(microseconds * 1.1e9 * SCALE), bytes_accessed=int(microseconds * 3.5e6 * SCALE), transcendentals=0
    )


def fetch(order, stacks, table, half, columns, target, sem):
    rows = stacks[0].shape[1]
    pairs = []
    for k, places in enumerate(table):
        goal = target.at[span(order[k], rows), :]
        pairs.append(
            [
                pltpu.make_async_copy(
                    stacks[stack].at[part, :, pl.ds(start + columns[0], columns[1])], goal, sem
                )
                for stack, part, start in places
            ]
        )

    @pl.when(order[SLOTS] == half)
    def _():
        for pair in pairs:
            pair[0].start()

    @pl.when(order[SLOTS] != half)
    def _():
        for pair in pairs:
            pair[1].start()

    return [pair[0] for pair in pairs]


def fetch_all(order, stacks, table, half_width, target, sem):
    copies = []
    for half in range(2):
        view = target.at[:, pl.ds(half * half_width, half_width)]
        copies = copies + fetch(order, stacks, table, half, (0, half_width), view, sem)
    return copies


def bulk_rows(width, hidden):
    return (2 * width + 2 * hidden) // SLOTS


def fetch_square(bulk, which, target, sem):
    width = bulk.shape[1]
    block = width // SLOTS
    each = bulk.shape[0] // SLOTS
    copies = []
    for j in range(SLOTS):
        source = bulk.at[pl.ds(j * each + which * block, block), :]
        copies.append(pltpu.make_async_copy(source, target.at[pl.ds(j * block, block), :], sem))
        copies[-1].start()
    return copies


def fetch_bulk(bulk, w_in, w_down, sems):
    width = bulk.shape[1]
    block = width // SLOTS
    each = bulk.shape[0] // SLOTS
    folds = w_in.shape[1] // width
    first, second = [], []
    for j in range(SLOTS):
        start = j * each + 2 * block
        for m in range(folds):
            source = bulk.at[pl.ds(start + m * block, block), :]
            target = w_in.at[pl.ds(j * block, block), pl.ds(m * width, width)]
            first.append(pltpu.make_async_copy(source, target, sems[0]))
        source = bulk.at[pl.ds(start + folds * block, folds * block), :]
        target = w_down.at[pl.ds(j * folds * block, folds * block), :]
        second.append(pltpu.make_async_copy(source, target, sems[1]))
    for copy in first + second:
        copy.start()
    return first, second


def settle(copies):
    for copy in copies:
        copy.wait()


def emit(order, source, columns, rows, targets, start, sem):
    copies = []
    for k in range(SLOTS):
        copies.append(
            pltpu.make_async_copy(
                source.at[span(order[k], rows), columns],
                targets[k % 2].at[k // 2 % 2, k // 4, :, pl.ds(start, columns.size)],
                sem,
            )
        )
    for copy in copies:
        copy.start()
    return copies


def tap_matrix(pools):
    rows = lax.broadcasted_iota(jnp.int32, (KERNEL * pools, WIDE), 0)
    cols = lax.broadcasted_iota(jnp.int32, (KERNEL * pools, WIDE), 1)
    tap = rows // pools
    wanted = HALF - KERNEL // 2 + STRIDE * (rows - tap * pools) + tap
    return jnp.where(cols == wanted, 1.0, 0.0).astype(BF16)


def tap_matrix_back(pools):
    rows = lax.broadcasted_iota(jnp.int32, (WIDE, KERNEL * pools), 0)
    cols = lax.broadcasted_iota(jnp.int32, (WIDE, KERNEL * pools), 1)
    tap = cols // pools
    wanted = HALF - KERNEL // 2 + STRIDE * (cols - tap * pools) + tap
    return jnp.where(rows == wanted, 1.0, 0.0).astype(BF16)


TAP_ROW = 6
BIAS_ROW = TAP_ROW + 2 * KERNEL
SMALL = BIAS_ROW + 4
SMALL_ROWS = 16


def tap_row(tap, kind):
    return TAP_ROW + 2 * tap + kind


def project_kernel(table, order, tok, low, high, *refs):
    queries, pairs, pooled, vecs, xext, weights, narrow, sem = refs[-8:]
    stacks = refs[:-8]
    width = tok.shape[1]
    copies = fetch_all(order, stacks, table, 3 * width // 2, weights, sem)
    rows = stacks[0].shape[1]
    for k, places in enumerate(table):
        stack, part, start = places[0]
        copies.append(
            pltpu.make_async_copy(
                stacks[stack].at[part, :, pl.ds(start + 3 * width // 2, 128)],
                narrow.at[span(order[k], rows), :],
                sem,
            )
        )
        copies[-1].start()
    seqs = low.shape[0] // HALF
    for s in range(seqs):
        xext[s * WIDE : s * WIDE + HALF, :] = low[s * HALF : (s + 1) * HALF, :]
        xext[s * WIDE + HALF : s * WIDE + HALF + WINDOW, :] = tok[s * WINDOW : (s + 1) * WINDOW, :]
        xext[s * WIDE + HALF + WINDOW : (s + 1) * WIDE, :] = high[s * HALF : (s + 1) * HALF, :]
    settle(copies)

    @pl.loop(0, 2 * width // TILE)
    def _(n):
        cols = span(n + width // TILE, TILE)
        pairs[:, span(n, TILE)] = product(xext[...], weights[:, cols]).astype(BF16)

    vecs[...] = narrow[...].astype(F32).T[: vecs.shape[0]]
    pools = WINDOW // STRIDE
    matrix = tap_matrix(pools)

    @pl.loop(0, seqs)
    def _(s):
        for n in range(2 * width // TILE):
            cols = slice(n * TILE, (n + 1) * TILE)
            kind, own = divmod(n * TILE, width)
            slab = product(matrix, pairs[span(s, WIDE), cols])
            total = 0.0
            for t in range(KERNEL):
                row = tap_row(t, kind)
                total = total + vecs[row : row + 1, own : own + TILE] * slab[t * pools : (t + 1) * pools]
            pooled[span(s, pools), cols] = total.astype(BF16)

    @pl.loop(0, width // TILE)
    def _(n):
        cols = span(n, TILE)
        queries[:, cols] = product(tok[...], weights[:, cols]).astype(BF16) * HEAD_DIM**-0.5


def lane_masks():
    lane = lax.broadcasted_iota(jnp.int32, (WINDOW, PAIR), 1)
    first = lane < HEAD_DIM
    return first, jnp.where(first, 1.0, 0.0).astype(BF16), jnp.where(first, 0.0, 1.0).astype(BF16)


def side_masks(step):
    slot = lax.broadcasted_iota(jnp.int32, (WINDOW, 2 * WINDOW), 0)
    query = lax.broadcasted_iota(jnp.int32, (WINDOW, 2 * WINDOW), 1)
    near = slot >= lax.bitwise_and(query, WINDOW - 1) // step
    return near, jnp.where(near, 1.0, 0.0).astype(BF16), jnp.where(near, 0.0, 1.0).astype(BF16)


def stack_heads(block, lanes):
    return jnp.concatenate([block * lanes[1], block * lanes[2]], axis=0)


def merge_heads(block, lanes):
    return jnp.where(lanes[0], block[:WINDOW], block[WINDOW:])


def spread_sides(block, sides):
    return jnp.concatenate([block * sides[1], block * sides[2]], axis=0)


def attend(queries, keys, values, bias, lanes, sides):
    scores = product_back(keys, stack_heads(queries, lanes))
    scores = jnp.where(sides[0], scores[:WINDOW], scores[WINDOW:]) + bias
    weights = jnp.exp(scores - jnp.max(scores, axis=0, keepdims=True))
    probs = (weights * (1.0 / jnp.sum(weights, axis=0, keepdims=True))).astype(BF16)
    mixed = outer_sum(spread_sides(probs, sides), values)
    return probs, merge_heads(mixed, lanes)


def attend_back(queries, keys, values, probs, grad_out, lanes, sides):
    grad_stack = stack_heads(grad_out, lanes)
    grad_probs = product_back(values, grad_stack)
    grad_probs = jnp.where(sides[0], grad_probs[:WINDOW], grad_probs[WINDOW:])
    probs_full = probs.astype(F32)
    centre = jnp.sum(probs_full * grad_probs, axis=0, keepdims=True)
    grad_scores = spread_sides((probs_full * (grad_probs - centre)).astype(BF16), sides)
    grad_values = product(spread_sides(probs, sides), grad_stack)
    grad_keys = product(grad_scores, stack_heads(queries, lanes))
    grad_queries = merge_heads(outer_sum(grad_scores, keys), lanes) * HEAD_DIM**-0.5
    return grad_queries, grad_keys, grad_values


def window_kernel(queries, pairs, bias, attended, probs):
    width = queries.shape[1]
    lanes = lane_masks()
    sides = side_masks(1)
    both = jnp.concatenate([bias[0], bias[0]], axis=1)
    for n in range(width // PAIR):
        cols = slice(n * PAIR, (n + 1) * PAIR)
        held, out = attend(
            queries[:, cols],
            pairs[:, cols],
            pairs[:, width + n * PAIR : width + (n + 1) * PAIR],
            both,
            lanes,
            sides,
        )
        probs[0, n] = held
        attended[:, cols] = out.astype(BF16)


def lay_pooled(places, blocks, field):
    pools = blocks[0].shape[0]
    for k, block in enumerate(blocks):
        field[span(places[k], pools), :] = block[...]


def pooled_kernel(places, attended, bias, bulk, *refs):
    blocks = refs[:5]
    queries, mixed, probs, weights, field, sem = refs[-6:]
    width = attended.shape[1]
    s = pl.program_id(0)

    @pl.when(s == 0)
    def _():
        copies = fetch_square(bulk, 0, weights, sem)
        field[...] = jnp.zeros_like(field)
        settle(copies)

        @pl.loop(0, width // TILE)
        def _(n):
            cols = span(n, TILE)
            queries[:, cols] = product(attended[...], weights[:, cols]).astype(BF16) * HEAD_DIM**-0.5

    lay_pooled(places, blocks, field)
    lanes = lane_masks()
    sides = side_masks(STRIDE)
    both = jnp.concatenate([bias[0], bias[0]], axis=1)
    rows = span(s, WINDOW)
    for n in range(width // PAIR):
        cols = slice(n * PAIR, (n + 1) * PAIR)
        held, out = attend(
            queries[rows, cols],
            field[:, cols],
            field[:, width + n * PAIR : width + (n + 1) * PAIR],
            both,
            lanes,
            sides,
        )
        probs[0, n] = held
        first = attended[rows, cols].astype(F32)
        mixed[:, cols] = (first + out.astype(BF16).astype(F32)).astype(BF16)


def feed_kernel(tok, mixed, cot, vecs, bias_in, bulk, *refs):
    (
        result,
        grad_resid,
        grad_mixed,
        gone,
        vec_grads,
        w_out,
        w_in,
        w_down,
        centred,
        rstd,
        normed,
        normed_t,
        active,
        slope,
        field,
        grad_outer,
        grad_in,
        grad_down,
        grad_out,
        bias_grad,
        narrow,
        sems,
    ) = refs
    rows, width = tok.shape
    hidden = w_in.shape[1]
    first = fetch_square(bulk, 1, w_out, sems.at[0])
    second, third = fetch_bulk(bulk, w_in, w_down, (sems.at[1], sems.at[2]))
    settle(first)

    @pl.loop(0, width // TILE, unroll=3)
    def _(n):
        cols = span(n, TILE)
        field[:, cols] = tok[:, cols].astype(F32) + product(mixed[...], w_out[:, cols]) + vecs[0:1, cols]

    blocks = rows // WINDOW

    @pl.loop(0, blocks, unroll=2)
    def _(b):
        part = span(b, WINDOW)
        resid = field[part, :]
        middle = resid - jnp.mean(resid, axis=-1, keepdims=True)
        scale = lax.rsqrt(jnp.mean(middle * middle, axis=-1, keepdims=True) + norm_eps)
        unit = middle * scale
        centred[part, :] = unit
        rstd[part, :] = jnp.broadcast_to(scale, (WINDOW, 128))
        low = (unit * vecs[1:2, :] + vecs[2:3, :]).astype(BF16)
        normed[part, :] = low
        normed_t[:, part] = low.T

    settle(second)

    @pl.loop(0, hidden // TILE, unroll=3)
    def _(n):
        cols = span(n, TILE)
        inner = product(normed[...], w_in[:, cols]) + bias_in[0:1, cols]
        cdf = 0.5 + 0.5 * lax.erf(inner * ROOT_HALF)
        active[:, cols] = (inner * cdf).astype(BF16)
        slope[:, cols] = (cdf + inner * (jnp.exp(-0.5 * inner * inner) * ROOT_TWO_PI)).astype(BF16)

    settle(third)

    @pl.loop(0, width // TILE, unroll=3)
    def _(n):
        cols = span(n, TILE)
        unit = centred[:, cols] * vecs[1:2, cols] + vecs[2:3, cols]
        field[:, cols] = unit + product(active[...], w_down[:, cols]) + vecs[3:4, cols]

    vec_grads[...] = jnp.zeros_like(vec_grads)

    def add_row(k, value):
        vec_grads[k : k + 1, :] += jnp.sum(value, axis=0, keepdims=True)

    @pl.loop(0, blocks, unroll=2)
    def _(b):
        part = span(b, WINDOW)
        summed = field[part, :]
        middle = summed - jnp.mean(summed, axis=-1, keepdims=True)
        scale = lax.rsqrt(jnp.mean(middle * middle, axis=-1, keepdims=True) + norm_eps)
        unit = middle * scale
        result[part, :] = (unit * vecs[4:5, :] + vecs[5:6, :]).astype(BF16)
        grad = cot[part, :].astype(F32)
        add_row(4, grad * unit)
        add_row(5, grad)
        u = grad * vecs[4:5, :]
        lean = jnp.mean(u * unit, axis=-1, keepdims=True)
        grad = scale * (u - jnp.mean(u, axis=-1, keepdims=True) - unit * lean)
        field[part, :] = grad
        low = grad.astype(BF16)
        grad_outer[part, :] = low
        add_row(3, low.astype(F32))

    @pl.loop(0, hidden // TILE, unroll=3)
    def _(n):
        cols = span(n, TILE)
        grad = product_back(grad_outer[...], w_down[cols, :]).astype(BF16).astype(F32)
        low = (grad * slope[:, cols].astype(F32)).astype(BF16)
        slope[:, cols] = low
        bias_grad[:, cols] = jnp.sum(low.astype(F32), axis=0, keepdims=True)
        grad_down[cols, :] = outer_sum(active[:, cols], grad_outer[...]).astype(BF16)
        grad_in[:, cols] = product(normed_t[...], low).astype(BF16)

    block = width // SLOTS
    folds = hidden // width
    each = gone.shape[0] // SLOTS
    emits = []
    for j in range(SLOTS):
        for m in range(folds):
            source = grad_in.at[pl.ds(j * block, block), pl.ds(m * width, width)]
            target = gone.at[pl.ds(j * each + m * block, block), :]
            emits.append(pltpu.make_async_copy(source, target, sems.at[3]))
        source = grad_down.at[pl.ds(j * folds * block, folds * block), :]
        target = gone.at[pl.ds(j * each + folds * block, folds * block), :]
        emits.append(pltpu.make_async_copy(source, target, sems.at[3]))
    for copy in emits:
        copy.start()

    @pl.loop(0, width // TILE, unroll=3)
    def _(n):
        cols = span(n, TILE)
        field[:, cols] += product_back(slope[...], w_in[cols, :])

    @pl.loop(0, blocks, unroll=2)
    def _(b):
        part = span(b, WINDOW)
        grad = field[part, :]
        unit = centred[part, :]
        add_row(1, grad * unit)
        add_row(2, grad)
        u = grad * vecs[1:2, :]
        lean = jnp.mean(u * unit, axis=-1, keepdims=True)
        grad = rstd[part, 0:1] * (u - jnp.mean(u, axis=-1, keepdims=True) - unit * lean)
        grad_resid[part, :] = grad
        low = grad.astype(BF16)
        grad_outer[part, :] = low
        add_row(0, low.astype(F32))

    @pl.loop(0, width // TILE, unroll=3)
    def _(n):
        cols = span(n, TILE)
        grad_out[cols, :] = outer_sum(mixed[:, cols], grad_outer[...]).astype(BF16)

    for j in range(SLOTS):
        source = grad_out.at[pl.ds(j * block, block), :]
        target = gone.at[pl.ds(j * each + 2 * folds * block, block), :]
        emits.append(pltpu.make_async_copy(source, target, sems.at[3]))
        emits[-1].start()

    @pl.loop(0, width // TILE, unroll=3)
    def _(n):
        cols = span(n, TILE)
        grad_mixed[:, cols] = product_back(grad_outer[...], w_out[cols, :]).astype(BF16)

    narrow[...] = jnp.zeros_like(narrow)
    small = narrow.shape[1]
    for j in range(SLOTS):
        narrow[j, :8, :block] = vec_grads[:, j * block : (j + 1) * block].astype(BF16)
        part = bias_grad[:, j * folds * block : (j + 1) * folds * block]
        narrow[j, 8:9, : folds * block] = part.astype(BF16)
        emits.append(
            pltpu.make_async_copy(
                narrow.at[j], gone.at[pl.ds(j * each + each - small, small), :], sems.at[3]
            )
        )
        emits[-1].start()
    settle(emits)


def pooled_back_kernel(places, grad_mixed, queries, probs, *refs):
    blocks = refs[:5]
    grad_queries, grad_own, grad_away, grad_near, grad_far = refs[5:10]
    field, total = refs[10:]
    width = grad_mixed.shape[1]
    pools = blocks[0].shape[0]

    @pl.when(pl.program_id(0) == 0)
    def _():
        field[...] = jnp.zeros_like(field)

    lay_pooled(places, blocks, field)
    lanes = lane_masks()
    sides = side_masks(STRIDE)
    for n in range(width // PAIR):
        cols = slice(n * PAIR, (n + 1) * PAIR)
        others = slice(width + n * PAIR, width + (n + 1) * PAIR)
        grad_q, grad_k, grad_v = attend_back(
            queries[:, cols], field[:, cols], field[:, others], probs[0, n], grad_mixed[:, cols], lanes, sides
        )
        grad_queries[:, cols] = grad_q.astype(BF16)
        total[:, cols] = grad_k
        total[:, others] = grad_v
    for k, target in enumerate((grad_own, grad_away.at[0], grad_away.at[1], grad_near, grad_far)):
        target[...] = total[span(places[k], pools), :].astype(BF16)


def window_back_kernel(grad_mixed, grad_second, first, queries, pairs, probs, weights, *refs):
    grad_queries, grad_pairs, grad_pooled, grad_low = refs
    width = first.shape[1]
    s = pl.program_id(0)

    @pl.when(s == 0)
    def _():
        @pl.loop(0, width // TILE)
        def _(n):
            cols = span(n, TILE)
            grad = grad_mixed[:, cols].astype(F32) + product_back(grad_second[...], weights[cols, :])
            grad_low[:, cols] = grad.astype(BF16)
            grad_pooled[cols, :] = outer_sum(first[:, cols], grad_second[...]).astype(BF16)

    lanes = lane_masks()
    sides = side_masks(1)
    rows = span(s, WINDOW)
    for n in range(width // PAIR):
        cols = slice(n * PAIR, (n + 1) * PAIR)
        others = slice(width + n * PAIR, width + (n + 1) * PAIR)
        grad_q, grad_k, grad_v = attend_back(
            queries[:, cols], pairs[:, cols], pairs[:, others], probs[0, n], grad_low[rows, cols], lanes, sides
        )
        grad_queries[:, cols] = grad_q.astype(BF16)
        grad_pairs[:, cols] = grad_k.astype(BF16)
        grad_pairs[:, others] = grad_v.astype(BF16)


def conv_back_kernel(table, order, own, away, near, far, vecs, pairs, grad_pairs, *refs):
    stacks = refs[:-6]
    total, tap_grads, edges, weights, rim, sem = refs[-6:]
    width = pairs.shape[1] // 2
    seqs = pairs.shape[0] // WIDE
    pools = WINDOW // STRIDE
    copies = fetch_all(order, stacks, table, 3 * width // 2, weights, sem)
    matrix = tap_matrix(pools)
    back = tap_matrix_back(pools)
    tap_grads[...] = jnp.zeros_like(tap_grads)

    @pl.loop(0, seqs)
    def _(s):
        for n in range(2 * width // TILE):
            cols = slice(n * TILE, (n + 1) * TILE)
            kind, start = divmod(n * TILE, width)
            taps = [vecs[tap_row(t, kind) : tap_row(t, kind) + 1, start : start + TILE] for t in range(KERNEL)]
            part = span(s, pools)
            grad = own[part, cols].astype(F32) + away[part, cols].astype(F32)
            grad = grad + near[part, cols].astype(F32) + far[part, cols].astype(F32)
            grad = grad.astype(BF16).astype(F32)
            spread = [(taps[t] * grad).astype(BF16) for t in range(KERNEL)]
            whole = grad_pairs[span(s, WIDE), cols].astype(F32) + product(back, jnp.concatenate(spread, axis=0))
            total[span(s, WIDE), cols] = whole.astype(BF16)
            slab = product(matrix, pairs[span(s, WIDE), cols])
            for t in range(KERNEL):
                row = 2 * t + kind
                tap_grads[row : row + 1, start : start + TILE] += jnp.sum(
                    grad * slab[t * pools : (t + 1) * pools], axis=0, keepdims=True
                )

    for s in range(seqs):
        rim[s * HALF : (s + 1) * HALF, :] = total[s * WIDE : s * WIDE + HALF, :]
        rim[(seqs + s) * HALF : (seqs + s + 1) * HALF, :] = total[s * WIDE + HALF + WINDOW : (s + 1) * WIDE, :]
    settle(copies)

    @pl.loop(0, width // TILE)
    def _(n):
        cols = span(n, TILE)
        edges[:, cols] = product_back(rim[...], weights[cols, width:]).astype(BF16)


def query_grad_kernel(order, tok, grad_queries, grad_pooled, keep, give, tok_t, total, sem):
    width = tok.shape[1]
    block = width // SLOTS
    targets = (keep, give)
    copies = emit(order, grad_pooled, pl.ds(0, width), block, targets, 3 * width, sem)
    tok_t[...] = tok[...].T

    @pl.loop(0, width // TILE)
    def _(n):
        cols = span(n, TILE)
        total[:, cols] = product(tok_t[...], grad_queries[:, cols]).astype(BF16)

    copies += emit(order, total, pl.ds(0, width), block, targets, 0, sem)
    settle(copies)


def weight_grad_kernel(order, tok, low, high, grad_pairs, tap_grads, *refs):
    keep, give, xext_t, total, narrow, sem = refs[2:]
    width = tok.shape[1]
    block = width // SLOTS
    targets = (keep, give)
    taps = jnp.concatenate([tap_grads[...], jnp.zeros((112, width), F32)], axis=0).T
    narrow[...] = taps.astype(BF16)
    copies = emit(order, narrow, pl.ds(0, 128), block, targets, 4 * width, sem)
    for s in range(low.shape[0] // HALF):
        parts = (
            low[s * HALF : (s + 1) * HALF, :],
            tok[s * WINDOW : (s + 1) * WINDOW, :],
            high[s * HALF : (s + 1) * HALF, :],
        )
        xext_t[:, s * WIDE : (s + 1) * WIDE] = jnp.concatenate(parts, axis=0).T

    @pl.loop(0, 2 * width // TILE)
    def _(n):
        cols = span(n, TILE)
        total[:, cols] = product(xext_t[...], grad_pairs[:, cols]).astype(BF16)

    copies += emit(order, total, pl.ds(0, 2 * width), block, targets, width, sem)
    settle(copies)


def token_grad_kernel(table, order, grad_resid, grad_queries, grad_pairs, low, high, *refs):
    stacks = refs[:-4]
    out, weights, own, sem = refs[-4:]
    width = grad_resid.shape[1]
    seqs = grad_resid.shape[0] // WINDOW
    copies = fetch_all(order, stacks, table, 3 * width // 2, weights, sem)
    for s in range(seqs):
        own[s * WINDOW : (s + 1) * WINDOW, :width] = grad_queries[s * WINDOW : (s + 1) * WINDOW, :]
        own[s * WINDOW : (s + 1) * WINDOW, width:] = grad_pairs[s * WIDE + HALF : s * WIDE + HALF + WINDOW, :]
    settle(copies)

    @pl.loop(0, width // TILE)
    def _(n):
        cols = span(n, TILE)
        out[:, cols] = grad_resid[:, cols] + product_back(own[...], weights[cols, :])
        for s in range(seqs):
            part = slice(s * HALF, (s + 1) * HALF)
            out[s * WINDOW : s * WINDOW + HALF, cols] += low[part, cols].astype(F32)
            out[s * WINDOW + HALF : (s + 1) * WINDOW, cols] += high[part, cols].astype(F32)


def shape_of(*dims, dtype=BF16):
    return jax.ShapeDtypeStruct(dims, dtype)


def turn(block, step):
    return lax.ppermute(block, "shard", [(i, (i - 4 * step) % SLOTS) for i in range(SLOTS)])


def flip(block):
    return lax.ppermute(block, "shard", [(i, i ^ 2) for i in range(SLOTS)])


def other(block):
    return lax.ppermute(block, "rep", [(0, 1), (1, 0)])


def gate_kernel(*refs):
    del refs


def after(value, *others):
    if not direct() or not others:
        return value
    return pl.pallas_call(
        gate_kernel,
        out_shape=jax.ShapeDtypeStruct(value.shape, value.dtype),
        in_specs=[any_spec()] * (1 + len(others)),
        out_specs=any_spec(),
        input_output_aliases={0: 0},
        compiler_params=params(2),
        cost_estimate=cost(0),
        name="gate",
    )(value, *others)


def direct():
    return lax.axis_size("shard") == SLOTS and lax.axis_size("rep") == 2


def block_order():
    if not direct():
        return jnp.arange(SLOTS + 1, dtype=jnp.int32) % SLOTS
    me = lax.axis_index("shard")
    k = jnp.arange(SLOTS, dtype=jnp.int32)
    places = ((me // 4 + k // 4) % 4) * 4 + jnp.bitwise_xor(me % 4, k % 4)
    return jnp.concatenate([places, lax.axis_index("rep")[None]]).astype(jnp.int32)


class Gather:
    def __init__(self, block):
        self.block = block

    def turn(self, *gate):
        own = after(self.block, *gate)
        self.along = jnp.stack([own] + [turn(own, step) for step in (1, 2, 3)])

    def cross(self, *gate):
        self.along = after(self.along, *gate)
        self.across = flip(self.along)

    def rep(self, *gate):
        self.across = after(self.across, *gate)
        self.first = jnp.concatenate([self.along, self.across], axis=0)
        self.second = other(self.first)

    def cores(self, *gate):
        stacks = [self.first, after(self.second, *gate)]
        stacks = stacks + [swap(stack) for stack in stacks]
        table = []
        for k in range(SLOTS):
            part = k // 2 % 2 * 4 + k // 4
            table.append(((2 * (k % 2), part, 0), (2 * (k % 2) + 1, part, 0)))
        return stacks, tuple(table)


def plain_gather(block, extra=None):
    rows, width = block.shape
    half = width // 2
    rows = rows * lax.axis_size("shard") // SLOTS
    mine, rest = block[:, :half], block[:, half:]
    both = jnp.concatenate([mine] + ([] if extra is None else [extra]) + [rest], axis=1)
    full = lax.all_gather(both, "shard", axis=0, tiled=True)
    table = tuple(((0, k, 0), (0, k, both.shape[1] - half)) for k in range(SLOTS))
    return [full.reshape(SLOTS, rows, both.shape[1])], table


def pack_kernel(order, query, key, value, pooled, out, inner, outer, tokens, taps, *refs):
    vectors, bias = refs[:6], refs[6]
    lead, bulk, low, high, joined, small = refs[7:]
    part, width = query.shape
    half = 3 * width // 2
    for k, source in enumerate((query, key, value)):
        joined[:, k * width : (k + 1) * width] = source[...]
    mine = order[SLOTS]
    small[...] = jnp.zeros_like(small)
    for k, source in enumerate(vectors):
        small[k : k + 1, :part] = source[...].astype(F32)
    for t in range(KERNEL):
        small[tap_row(t, 0) : tap_row(t, 0) + 2, :part] = taps[t].astype(F32)
    small[BIAS_ROW:SMALL, :part] = bias[...].astype(F32)
    lead[:, :half] = joined[:, span(mine, half)]
    lead[:, half:] = small[...].T[:part].astype(BF16)
    bulk[:part, :] = pooled[...]
    bulk[part : 2 * part, :] = out[...]
    folds = inner.shape[1] // width
    for m in range(folds):
        bulk[(2 + m) * part : (3 + m) * part, :] = inner[:, m * width : (m + 1) * width]
    bulk[(2 + folds) * part :, :] = outer[...]
    high[...] = tokens[:, :HALF, :]
    low[...] = tokens[:, tokens.shape[1] - HALF :, :]


def split_kernel(wide, order, keep, arrived, a_keep, a_send, b_keep, b_send):
    half = wide // 2
    mine = span(order[SLOTS], half)
    rest = span(1 - order[SLOTS], half)
    for across in range(2):
        a_keep[across, 0] = keep[across, 0, :, mine] + arrived[across, 0, :, mine]
        a_send[across, 0] = keep[across, 0, :, rest] + arrived[across, 0, :, rest]
        target = b_send if across else b_keep
        target[0] = keep[across, 0, :, wide:] + arrived[across, 0, :, wide:]


def fold_kernel(keep, arrived, x_keep, x_send):
    x_keep[0] = keep[0, 0] + arrived[0, 0]
    x_send[0] = keep[1, 0] + arrived[1, 0]


def join_kernel(x_keep, x_arrived, b_keep, b_arrived, *parts):
    half = x_keep.shape[2]
    for k, part in enumerate(parts):
        part[:, :half] = x_keep[k] + x_arrived[k]
        part[:, half:] = b_keep[k] + b_arrived[k]


def gather_sum_kernel(own, first, second, third, out):
    total = own[...].astype(F32) + first[...].astype(F32) + second[...].astype(F32) + third[...].astype(F32)
    out[...] = total.astype(BF16)


def final_kernel(wide, pieces, order, own, arrived, *refs):
    outs, total = refs[:-1], refs[-1]
    half = wide // 2
    total[:, span(order[SLOTS], half)] = own[:, :half].astype(F32)
    total[:, span(1 - order[SLOTS], half)] = arrived[:, :half].astype(F32)
    total[:, wide:] = own[:, half:].astype(F32) + arrived[:, half:].astype(F32)
    for (start, size), out in zip(pieces, outs):
        out[...] = total[:, start : start + size]


class Scatter:
    def __init__(self, keep, give, order, wide, pieces):
        self.order, self.wide, self.pieces = order, wide, pieces
        self.rows, self.columns = keep.shape[2:]
        self.keep, self.give = keep, give
        if direct():
            self.arrived = swap(give)

    def split(self):
        rows, half, rest = self.rows, self.wide // 2, self.columns - self.wide
        four = pl.BlockSpec((2, 1, rows, self.columns), lambda z: (0, z, 0, 0))
        a_block = pl.BlockSpec((2, 1, rows, half), lambda z: (0, z, 0, 0))
        b_block = pl.BlockSpec((1, rows, rest), lambda z: (z, 0, 0))
        a_shape, b_shape = shape_of(2, 4, rows, half), shape_of(4, rows, rest)
        self.a_keep, a_send, self.b_keep, b_send = pl.pallas_call(
            functools.partial(split_kernel, self.wide),
            grid=(4,),
            out_shape=(a_shape, a_shape, b_shape, b_shape),
            in_specs=[smem_spec(), four, four],
            out_specs=(a_block, a_block, b_block, b_block),
            compiler_params=params(14),
            cost_estimate=cost(5),
            name="split",
        )(self.order, self.keep, self.arrived)
        self.a_arrived = other(a_send)
        self.b_arrived = flip(b_send)
        return a_send

    def fold(self):
        rows, half = self.rows, self.wide // 2
        a_block = pl.BlockSpec((2, 1, rows, half), lambda z: (0, z, 0, 0))
        x_block = pl.BlockSpec((1, rows, half), lambda z: (z, 0, 0))
        x_shape = shape_of(4, rows, half)
        self.x_keep, x_send = pl.pallas_call(
            fold_kernel,
            grid=(4,),
            out_shape=(x_shape, x_shape),
            in_specs=[a_block, a_block],
            out_specs=(x_block, x_block),
            compiler_params=params(10),
            cost_estimate=cost(4),
            name="fold",
        )(self.a_keep, self.a_arrived)
        self.x_arrived = flip(x_send)
        return x_send

    def join(self):
        shape = shape_of(self.rows, self.columns - self.wide // 2)
        parts = pl.pallas_call(
            join_kernel,
            out_shape=(shape,) * 4,
            in_specs=[vmem_spec()] * 4,
            out_specs=(vmem_spec(),) * 4,
            compiler_params=params(14),
            cost_estimate=cost(3),
            name="join",
        )(self.x_keep, self.x_arrived, self.b_keep, self.b_arrived)
        self.turned = [parts[0]] + [turn(parts[step], -step) for step in (1, 2, 3)]
        return parts[1]

    def gather(self):
        self.own = pl.pallas_call(
            gather_sum_kernel,
            out_shape=shape_of(self.rows, self.columns - self.wide // 2),
            in_specs=[vmem_spec()] * 4,
            out_specs=vmem_spec(),
            compiler_params=params(10),
            cost_estimate=cost(2),
            name="gather_sum",
        )(*self.turned)
        self.last = other(self.own)
        return self.own

    def final(self):
        return pl.pallas_call(
            functools.partial(final_kernel, self.wide, self.pieces),
            out_shape=tuple(shape_of(self.rows, size, dtype=F32) for _, size in self.pieces),
            in_specs=[smem_spec(), vmem_spec(), vmem_spec()],
            out_specs=(vmem_spec(),) * len(self.pieces),
            scratch_shapes=[pltpu.VMEM((self.rows, self.columns), F32)],
            compiler_params=params(12),
            cost_estimate=cost(2),
            name="final",
        )(self.order, self.own, self.last)


def bulk_final_kernel(own, arrived, inner, outer, square, small):
    part, hidden = inner.shape
    width = own.shape[1]
    total = own[...].astype(F32) + arrived[...].astype(F32)
    folds = hidden // width
    for m in range(folds):
        inner[:, m * width : (m + 1) * width] = total[m * part : (m + 1) * part]
    outer[...] = total[folds * part : 2 * folds * part]
    square[...] = total[2 * folds * part : (2 * folds + 1) * part]
    small[...] = total[(2 * folds + 1) * part :]


def plain_total(whole):
    return rep_total(lax.psum_scatter(whole, "shard", scatter_dimension=0, tiled=True))


def plain_scatter(blocks, parts):
    keep, give = blocks
    full = jnp.stack([keep, give]).transpose(2, 1, 0, 3, 4).reshape(SLOTS, keep.shape[2], keep.shape[3])
    width = SLOTS * keep.shape[2]
    return [plain_total(full[:, :, start:stop].reshape(width, -1)) for start, stop in parts]


def rep_total(piece):
    count = lax.axis_size("rep")
    total = piece.astype(F32)
    for step in range(1, count):
        route = [(i, (i + step) % count) for i in range(count)]
        total = total + lax.ppermute(piece, "rep", route).astype(F32)
    return total


def shift(block, distance):
    count = lax.axis_size("shard")
    return lax.ppermute(
        block, "shard", [(i, i + distance) for i in range(count) if 0 <= i + distance < count]
    )


def swap(block):
    return lax.ppermute(block, "shard", [(i, i ^ 1) for i in range(lax.axis_size("shard"))])


def hop(block, outer):
    count = lax.axis_size("shard")
    route = [(i, i + (2 if (i % 2 == 0) == outer else -2)) for i in range(count)]
    return lax.ppermute(block, "shard", [(i, j) for i, j in route if 0 <= j < count])


def shards(
    tokens,
    query_proj,
    key_proj,
    value_proj,
    pooled_query,
    output_proj,
    conv_taps,
    output_bias,
    first_gain,
    first_shift,
    inner_proj,
    inner_bias,
    outer_proj,
    outer_bias,
    second_gain,
    second_shift,
    block_ids,
    cotangent,
):
    seqs, tok_span, width = tokens.shape
    rows = seqs * tok_span
    hidden = inner_proj.shape[1]
    device_count = lax.axis_size("shard")
    device_index = lax.axis_index("shard")
    seq_length = tok_span * device_count
    pools = tok_span // STRIDE
    pool_reach = POOL_SPAN // (2 * STRIDE)
    n_pair = width // PAIR
    core = lax.rem(device_index, 2)

    tok = tokens.reshape(rows, width)
    cot = cotangent.reshape(rows, width)
    vectors = [output_bias, first_gain, first_shift, outer_bias, second_gain, second_shift]
    part = width // device_count
    block = width // SLOTS
    order = block_order()
    if direct():
        packed = pl.pallas_call(
            pack_kernel,
            out_shape=(
                shape_of(part, 3 * width // 2 + 128),
                shape_of(bulk_rows(width, hidden), width),
                shape_of(seqs, HALF, width),
                shape_of(seqs, HALF, width),
            ),
            in_specs=[smem_spec()] + [vmem_spec()] * 16,
            out_specs=(vmem_spec(),) * 4,
            scratch_shapes=[pltpu.VMEM((part, 3 * width), BF16), pltpu.VMEM((128, 128), F32)],
            compiler_params=params(),
            cost_estimate=cost(3),
            name="pack",
        )(
            order,
            query_proj,
            key_proj,
            value_proj,
            pooled_query,
            output_proj,
            inner_proj,
            outer_proj,
            tokens,
            conv_taps,
            *[vector.reshape(1, part) for vector in vectors],
            inner_bias.reshape(4, part),
        )
        lead = Gather(packed[0])
        bulk = lax.all_gather(packed[1], "shard", axis=0, tiled=True)
        lead.turn()
        lead.cross()
        tick = after(jnp.zeros((8, 128), F32), lead.across)
        lead.rep()
        tok_low = shift(after(packed[2], tick), 1).reshape(seqs * HALF, width)
        tok_high = shift(after(packed[3], tick), -1).reshape(seqs * HALF, width)
        lead, lead_table = lead.cores(tok_low, tok_high)
    else:
        tok_low = shift(tokens[:, tok_span - HALF :], 1).reshape(seqs * HALF, width)
        tok_high = shift(tokens[:, :HALF], -1).reshape(seqs * HALF, width)
        small = jnp.concatenate(vectors + [conv_taps.reshape(-1), inner_bias]).reshape(SMALL, part).T
        small = jnp.pad(small, ((0, 0), (0, 128 - SMALL)))
        lead, lead_table = plain_gather(jnp.concatenate([query_proj, key_proj, value_proj], axis=1), small)
        square = [
            lax.all_gather(block_rows, "shard", axis=0, tiled=True).reshape(SLOTS, block, width)
            for block_rows in (pooled_query, output_proj)
        ]
        full = lax.all_gather(inner_proj, "shard", axis=0, tiled=True)
        full = full.reshape(SLOTS, block, hidden // width, width).transpose(0, 2, 1, 3)
        full = full.reshape(SLOTS, hidden // SLOTS, width)
        down = lax.all_gather(outer_proj, "shard", axis=0, tiled=True)
        down = down.reshape(SLOTS, hidden // SLOTS, width)
        bulk = jnp.concatenate(square + [full, down], axis=1).reshape(-1, width)

    query = jnp.arange(tok_span, dtype=jnp.int32)[None, :]
    slot = jnp.arange(WINDOW, dtype=jnp.int32)[:, None]
    query_ids = lax.dynamic_slice_in_dim(block_ids, device_index * tok_span, tok_span, 1)[:, None, :]

    def bias_for(ids, start, length, step, reach):
        ids = lax.dynamic_slice_in_dim(jnp.pad(ids, ((0, 0), (reach, reach + WINDOW))), start, WIDE, 1)
        near = slot >= query // step
        place = start - reach + jnp.where(near, slot, slot + WINDOW)
        key_ids = jnp.where(near[None], ids[:, :WINDOW, None], ids[:, WINDOW:, None])
        allowed = ((place >= 0) & (place < length))[None] & (key_ids <= query_ids)
        return jnp.where(allowed, 0.0, neg_fill)

    bias_one = bias_for(block_ids, device_index * tok_span, seq_length, 1, HALF)
    bias_two = bias_for(
        block_ids[:, ::STRIDE], device_index * pools, seq_length // STRIDE, STRIDE, pool_reach
    )

    n_lead = len(lead)
    queries, pairs, pooled, vecs = pl.pallas_call(
        functools.partial(project_kernel, lead_table),
        out_shape=(
            shape_of(rows, width),
            shape_of(seqs * WIDE, 2 * width),
            shape_of(seqs * pools, 2 * width),
            shape_of(24, width, dtype=F32),
        ),
        in_specs=[smem_spec()] + [vmem_spec()] * 3 + [hbm_spec()] * n_lead,
        out_specs=(vmem_spec(),) * 4,
        scratch_shapes=[
            pltpu.VMEM((seqs * WIDE, width), BF16),
            pltpu.VMEM((width, 3 * width), BF16),
            pltpu.VMEM((width, 128), BF16),
            pltpu.SemaphoreType.DMA,
        ],
        compiler_params=params(54),
        cost_estimate=cost(15),
        name="project",
    )(order, tok, tok_low, tok_high, *lead)
    bias_in = vecs[BIAS_ROW:SMALL].reshape(4, device_count, part).transpose(1, 0, 2).reshape(1, hidden)

    pool_away = swap(pooled)
    pool_far = hop(pooled, True)
    pool_near = hop(pooled, False)
    places = jnp.where(
        core == 0, jnp.array([2, 3, 1, 4, 0], jnp.int32), jnp.array([2, 1, 3, 0, 4], jnp.int32)
    )

    seq_block = lambda r, c: pl.BlockSpec((r, c), lambda s: (s, 0))
    whole_block = lambda r, c: pl.BlockSpec((r, c), lambda s: (0, 0))
    bias_block = pl.BlockSpec((1, WINDOW, tok_span), lambda s: (s, 0, 0))
    prob_block = pl.BlockSpec((1, n_pair, WINDOW, 2 * tok_span), lambda s: (s, 0, 0, 0))
    prob_shape = shape_of(seqs, n_pair, WINDOW, 2 * tok_span)

    attended, probs_one = pl.pallas_call(
        window_kernel,
        grid=(seqs,),
        out_shape=(shape_of(rows, width), prob_shape),
        in_specs=[seq_block(tok_span, width), seq_block(WIDE, 2 * width), bias_block],
        out_specs=(seq_block(tok_span, width), prob_block),
        compiler_params=params(12),
        cost_estimate=cost(10),
        name="window",
    )(queries, pairs, bias_one)

    pool_near = after(pool_near, attended)
    pool_blocks = (pooled, pool_away, swap(pool_near), pool_near, pool_far)
    pool_specs = [seq_block(pools, 2 * width)] * 5
    second, mixed, probs_two, pooled_weights = pl.pallas_call(
        pooled_kernel,
        grid=(seqs,),
        out_shape=(shape_of(rows, width), shape_of(rows, width), prob_shape, shape_of(width, width)),
        in_specs=[smem_spec(), whole_block(rows, width), bias_block, hbm_spec()] + pool_specs,
        out_specs=(
            whole_block(rows, width),
            seq_block(tok_span, width),
            prob_block,
            whole_block(width, width),
        ),
        scratch_shapes=[pltpu.VMEM((WIDE, 2 * width), BF16), pltpu.SemaphoreType.DMA],
        compiler_params=params(54),
        cost_estimate=cost(14),
        name="pooled",
    )(places, attended, bias_two, bulk, *pool_blocks)

    each = (2 * hidden + width) // SLOTS + SMALL_ROWS
    result, grad_resid, grad_mixed, grad_bulk, _ = pl.pallas_call(
        feed_kernel,
        out_shape=(
            shape_of(rows, width),
            shape_of(rows, width, dtype=F32),
            shape_of(rows, width),
            shape_of(SLOTS * each, width),
            shape_of(8, width, dtype=F32),
        ),
        in_specs=[vmem_spec()] * 5 + [hbm_spec()],
        out_specs=(vmem_spec(),) * 3 + (any_spec(), vmem_spec()),
        scratch_shapes=[
            pltpu.VMEM((width, width), BF16),
            pltpu.VMEM((width, hidden), BF16),
            pltpu.VMEM((hidden, width), BF16),
            pltpu.VMEM((rows, width), F32),
            pltpu.VMEM((rows, 128), F32),
            pltpu.VMEM((rows, width), BF16),
            pltpu.VMEM((width, rows), BF16),
            pltpu.VMEM((rows, hidden), BF16),
            pltpu.VMEM((rows, hidden), BF16),
            pltpu.VMEM((rows, width), F32),
            pltpu.VMEM((rows, width), BF16),
            pltpu.VMEM((width, hidden), BF16),
            pltpu.VMEM((hidden, width), BF16),
            pltpu.VMEM((width, width), BF16),
            pltpu.VMEM((1, hidden), F32),
            pltpu.VMEM((SLOTS, SMALL_ROWS, width), BF16),
            pltpu.SemaphoreType.DMA((4,)),
        ],
        compiler_params=params(58),
        cost_estimate=cost(45),
        name="feed",
    )(tok, mixed, cot, vecs, bias_in, bulk)
    if direct():
        own_bulk = lax.psum_scatter(grad_bulk, "shard", scatter_dimension=0, tiled=True)

    back_shape = shape_of(seqs * pools, 2 * width)
    grad_second, pg_own, pg_away, pg_near, pg_far = pl.pallas_call(
        pooled_back_kernel,
        grid=(seqs,),
        out_shape=(
            shape_of(rows, width),
            back_shape,
            shape_of(2, seqs * pools, 2 * width),
            back_shape,
            back_shape,
        ),
        in_specs=[
            smem_spec(),
            seq_block(tok_span, width),
            seq_block(tok_span, width),
            prob_block,
        ]
        + pool_specs,
        out_specs=(
            seq_block(tok_span, width),
            seq_block(pools, 2 * width),
            pl.BlockSpec((2, pools, 2 * width), lambda s: (0, s, 0)),
            seq_block(pools, 2 * width),
            seq_block(pools, 2 * width),
        ),
        scratch_shapes=[pltpu.VMEM((WIDE, 2 * width), BF16), pltpu.VMEM((WIDE, 2 * width), F32)],
        compiler_params=params(56),
        cost_estimate=cost(15),
        name="pooled_back",
    )(places, grad_mixed, second, probs_two, *pool_blocks)

    pg_cross = swap(pg_away)
    pg_near = (pg_near.astype(F32) + pg_cross[1].astype(F32)).astype(BF16)
    back_near = lax.ppermute(pg_near, "shard", back_route(device_count, False))
    back_far = lax.ppermute(pg_far, "shard", back_route(device_count, True))
    grad_second = after(grad_second, pg_near)

    grad_queries, grad_pairs, grad_pooled = pl.pallas_call(
        window_back_kernel,
        grid=(seqs,),
        out_shape=(shape_of(rows, width), shape_of(seqs * WIDE, 2 * width), shape_of(width, width)),
        in_specs=[
            whole_block(rows, width),
            whole_block(rows, width),
            whole_block(rows, width),
            seq_block(tok_span, width),
            seq_block(WIDE, 2 * width),
            prob_block,
            whole_block(width, width),
        ],
        out_specs=(seq_block(tok_span, width), seq_block(WIDE, 2 * width), whole_block(width, width)),
        scratch_shapes=[pltpu.VMEM((rows, width), BF16)],
        compiler_params=params(20),
        cost_estimate=cost(22),
        name="window_back",
    )(grad_mixed, grad_second, attended, queries, pairs, probs_one, pooled_weights)

    lead_shape = shape_of(2, 4, block, 4 * width + 128)
    lead_keep, lead_give = pl.pallas_call(
        query_grad_kernel,
        out_shape=(lead_shape, lead_shape),
        in_specs=[smem_spec()] + [vmem_spec()] * 3,
        out_specs=(any_spec(),) * 2,
        scratch_shapes=[
            pltpu.VMEM((width, rows), BF16),
            pltpu.VMEM((width, width), BF16),
            pltpu.SemaphoreType.DMA,
        ],
        compiler_params=params(12),
        cost_estimate=cost(5),
        name="query_grad",
    )(order, tok, grad_queries, grad_pooled)
    vecs = after(vecs, lead_keep)

    pair_total, tap_grads, edges = pl.pallas_call(
        functools.partial(conv_back_kernel, lead_table),
        out_shape=(
            shape_of(seqs * WIDE, 2 * width),
            shape_of(16, width, dtype=F32),
            shape_of(2 * seqs * HALF, width),
        ),
        in_specs=[smem_spec()] + [vmem_spec()] * 7 + [hbm_spec()] * n_lead,
        out_specs=(vmem_spec(),) * 3,
        scratch_shapes=[
            pltpu.VMEM((width, 3 * width), BF16),
            pltpu.VMEM((2 * seqs * HALF, 2 * width), BF16),
            pltpu.SemaphoreType.DMA,
        ],
        compiler_params=params(28),
        cost_estimate=cost(12),
        name="conv_back",
    )(order, pg_own, pg_cross[0], back_near, back_far, vecs, pairs, grad_pairs, *lead)

    lead_keep, lead_give = pl.pallas_call(
        weight_grad_kernel,
        out_shape=(lead_shape, lead_shape),
        in_specs=[smem_spec()] + [vmem_spec()] * 5 + [any_spec()] * 2,
        out_specs=(any_spec(),) * 2,
        input_output_aliases={6: 0, 7: 1},
        scratch_shapes=[
            pltpu.VMEM((width, seqs * WIDE), BF16),
            pltpu.VMEM((width, 2 * width), BF16),
            pltpu.VMEM((width, 128), BF16),
            pltpu.SemaphoreType.DMA,
        ],
        compiler_params=params(18),
        cost_estimate=cost(10),
        name="weight_grad",
    )(order, tok, tok_low, tok_high, pair_total, tap_grads, lead_keep, lead_give)
    pieces = tuple((k * width, width) for k in range(4)) + ((4 * width, 128),)
    lead_sum = Scatter(lead_keep, lead_give, order, 24 * 128, pieces)
    if direct():
        lead_sum.split()
        edges = after(edges, lead_sum.b_keep)
    edge_high = shift(edges[: seqs * HALF], -1)
    edge_low = shift(edges[seqs * HALF :], 1)

    tokens_grad = pl.pallas_call(
        functools.partial(token_grad_kernel, lead_table),
        out_shape=shape_of(rows, width, dtype=F32),
        in_specs=[smem_spec()] + [vmem_spec()] * 5 + [hbm_spec()] * n_lead,
        out_specs=vmem_spec(),
        scratch_shapes=[
            pltpu.VMEM((width, 3 * width), BF16),
            pltpu.VMEM((rows, 3 * width), BF16),
            pltpu.SemaphoreType.DMA,
        ],
        compiler_params=params(22),
        cost_estimate=cost(11),
        name="token_grad",
    )(order, grad_resid, grad_queries, pair_total, edge_low, edge_high, *lead)

    folds = hidden // width
    if direct():
        lead_sum.a_keep = after(lead_sum.a_keep, tokens_grad, lead_sum.b_arrived)
        lead_sum.fold()
        lead_sum.join()
        own_bulk = after(own_bulk, lead_sum.turned[1])
        lead_sum.gather()
        own_in, own_down, own_out, small_own = pl.pallas_call(
            bulk_final_kernel,
            out_shape=(
                shape_of(part, hidden, dtype=F32),
                shape_of(folds * part, width, dtype=F32),
                shape_of(part, width, dtype=F32),
                shape_of(SMALL_ROWS, width, dtype=F32),
            ),
            in_specs=[vmem_spec()] * 2,
            out_specs=(vmem_spec(),) * 4,
            compiler_params=params(10),
            cost_estimate=cost(2),
            name="bulk_final",
        )(own_bulk, other(own_bulk))
        vec_own = [small_own[k, :part] for k in range(6)]
        bias_own = small_own[8, : folds * part]
        own_query, own_keys, own_values, own_pooled, taps_own = lead_sum.final()
    else:
        whole = grad_bulk.reshape(SLOTS, each, width)
        inner_part = whole[:, : folds * block].reshape(SLOTS, folds, block, width).transpose(0, 2, 1, 3)
        own_in = plain_total(inner_part.reshape(width, hidden))
        own_down = plain_total(whole[:, folds * block : 2 * folds * block].reshape(hidden, width))
        small = whole[:, (2 * folds + 1) * block :]
        vec_own = [plain_total(small[:, k, :block].reshape(width)) for k in range(6)]
        bias_own = plain_total(small[:, 8, : folds * block].reshape(hidden))
        own_out = plain_total(whole[:, 2 * folds * block : (2 * folds + 1) * block].reshape(width, width))
        parts = [(k * width, (k + 1) * width) for k in range(4)] + [(4 * width, None)]
        own_query, own_keys, own_values, own_pooled, taps_own = plain_scatter(
            (lead_keep, lead_give), parts
        )
    taps_own = taps_own.T[: 2 * KERNEL].reshape(KERNEL, 2, part)
    return (
        result.reshape(tokens.shape),
        tokens_grad.reshape(tokens.shape),
        own_query,
        own_keys,
        own_values,
        own_pooled,
        own_out,
        taps_own,
        vec_own[0],
        vec_own[1],
        vec_own[2],
        own_in,
        bias_own,
        own_down,
        vec_own[3],
        vec_own[4],
        vec_own[5],
    )


def back_route(count, outer):
    route = [(i, i + (2 if (i % 2 == 0) == outer else -2)) for i in range(count)]
    return [(j, i) for i, j in route if 0 <= j < count]


def solution(mesh):
    in_specs = (
        P("rep", "shard", None),
        P("shard", None),
        P("shard", None),
        P("shard", None),
        P("shard", None),
        P("shard", None),
        P(None, None, "shard"),
        P("shard"),
        P("shard"),
        P("shard"),
        P("shard", None),
        P("shard"),
        P("shard", None),
        P("shard"),
        P("shard"),
        P("shard"),
        P("rep", None),
        P("rep", "shard", None),
    )
    out_specs = (
        P("rep", "shard", None),
        P("rep", "shard", None),
        P("shard", None),
        P("shard", None),
        P("shard", None),
        P("shard", None),
        P("shard", None),
        P(None, None, "shard"),
        P("shard"),
        P("shard"),
        P("shard"),
        P("shard", None),
        P("shard"),
        P("shard", None),
        P("shard"),
        P("shard"),
        P("shard"),
    )
    return jax.shard_map(shards, mesh=mesh, in_specs=in_specs, out_specs=out_specs, check_vma=False)
```
